512 devices in a mesh: row: 64 (over z, y_hi, core), col: 8 (over x, y_lo).
Axes of the slice: x: 4, y: 8 (y_hi: 4, y_lo: 2; y = y_hi * 2 + y_lo), z: 8, core: 2. Of those that a mesh axis runs over, the one named last changes fastest.
Arguments:
- bands: bfloat16 [64, 36, 1296], P('row'), may hold values from -6 to 6
- projections: bfloat16 [64, 256], P('row'), may hold values from -6 to 6
- qfunc: float32 [2, 2, 64, 1024], replicated, may hold values from -6 to 6
- species: int32 [32], replicated, may hold values from 0 to 1
- positions: float32 [3, 32], replicated, may hold values from 0 to 1
- glist: int32 [1024], replicated, may hold values from 1296 to 14255, as said below
Outputs:
- exchange: float32 [64, 36, 1296], P('row', None, 'col')
- proj_exchange: float32 [64, 256], P('row', 'col')
The draws below stay inside these ranges and needn't reach their ends.
Inputs may be any that keep to these rules, and one draw needn't show every extreme that they name: `glist`: distinct; each index (kx 36 + ky) * 36 + kz has 1 <= kx <= 17 and kx^2 + my^2 + mz^2 <= 110, with my, mz the signed frequencies of ky, kz.
All inputs are finite; a program needn't handle non-finite values.
Results may differ from the reference program's by a relative error of at most 0.0005.
Values may be sent and summed in bfloat16 or wider, within the bound.
A program may use at most 64 MiB of HBM per device.

```python
import math
import jax
import jax.numpy as jnp
from jax import lax

GRID = 36
NH = 8
NSPEC = 2
ATOMS = 32
NG = 1024
AUG_R2 = 110
NB = 64
NPROJ = 256


def draw_glist(key, part):
    key = jax.random.fold_in(key, 11)
    half_size = GRID // 2 + 1
    total_count = half_size * GRID * GRID
    position = jnp.arange(total_count, dtype=jnp.int32)
    freq_x = position // (GRID * GRID)
    freq_y = position // GRID % GRID
    freq_z = position % GRID
    signed_y = jnp.where(freq_y > GRID // 2, freq_y - GRID, freq_y)
    signed_z = jnp.where(freq_z > GRID // 2, freq_z - GRID, freq_z)
    norm_sq = freq_x * freq_x + signed_y * signed_y + signed_z * signed_z
    inside = (freq_x >= 1) & (freq_x <= GRID // 2 - 1) & (norm_sq <= AUG_R2)
    lowest = jnp.min(jnp.where(inside, position, total_count))
    highest = jnp.max(jnp.where(inside, position, -1))
    random_part = jax.random.randint(key, (total_count,), 0, 4096, dtype=jnp.int32)
    random_part = jnp.where((position == lowest) | (position == highest), 4096, random_part)
    scores = jnp.where(inside, random_part * total_count + position, -1 - position)
    unused, chosen = lax.top_k(scores, NG)
    return chosen.astype(jnp.int32)


def touch_ends(result, own_key, smallest, top_value):
    extent = result.shape
    index_at = [jax.random.randint(jax.random.fold_in(own_key, axis), (), 0, extent[axis]) for axis in range(len(extent))]
    result = result.at[tuple(index_at)].set(smallest)
    longest = extent.index(max(extent))
    index_at[longest] = (index_at[longest] + 1) % extent[longest]
    return result.at[tuple(index_at)].set(top_value)


def level_of(own_key, extent, shards, low, largest):
    factor_of, own = 1.0, jax.random.fold_in(own_key, 6)
    for dim, shards_of in shards:
        heights = jnp.exp(jax.random.uniform(jax.random.fold_in(own, dim), (shards_of,), jnp.float32, low / len(shards), largest / len(shards)))
        factor_of = factor_of * jnp.repeat(heights, extent[dim] // shards_of).reshape([-1 if axis == dim else 1 for axis in range(len(extent))])
    return factor_of


def gaussian(rng, extent, deviation, bound, cuts=(), held_as=jnp.bfloat16):
    loudness = level_of(rng, extent, cuts, -0.22, 0.18) if cuts else 1.0
    values = jax.random.normal(rng, extent, jnp.float32) * deviation * loudness
    return jnp.minimum(jnp.maximum(values, -bound), bound).astype(held_as)


def setup_inputs(seed: int = 0) -> dict:
    splits = jax.random.split(jax.random.key(seed), 7)
    return {
        "bands": gaussian(splits[0], (NB, GRID, GRID * GRID), 1.0, 6.0, ((0, 64),)),
        "projections": gaussian(splits[1], (NB, NPROJ), 1.0, 6.0, ((0, 64),)),
        "qfunc": gaussian(splits[2], (2, NSPEC, NH * NH, NG), 1.0, 6.0, (), jnp.float32),
        "species": touch_ends(jax.random.randint(splits[3], (ATOMS,), 0, NSPEC), jax.random.fold_in(splits[3], 1), 0, NSPEC - 1).astype(jnp.int32),
        "positions": jnp.clip(jax.random.uniform(splits[4], (3, ATOMS), jnp.float32, 0.0, 1.0), 0.0, 1.0),
        "glist": draw_glist(jax.random.fold_in(splits[6], 71), 0),
    }


def signed_freq(values, grid_size):
    return jnp.where(values > grid_size // 2, values - grid_size, values)

def reference(bands, projections, qfunc, species, positions, glist):
    grid_size = GRID
    half_size = grid_size // 2 + 1
    strength = grid_size ** 1.5 / 4.0
    aug_scale = grid_size ** 1.5 / (NH * math.sqrt(ATOMS))
    fields = bands.astype(jnp.float32).reshape(NB, grid_size, grid_size, grid_size)
    coeffs = projections.astype(jnp.float32).reshape(NB, ATOMS, NH)
    freq_x = (glist // (grid_size * grid_size)).astype(jnp.float32)
    freq_y = signed_freq(glist // grid_size % grid_size, grid_size).astype(jnp.float32)
    freq_z = signed_freq(glist % grid_size, grid_size).astype(jnp.float32)
    turns = positions[0][:, None] * freq_x[None, :] + positions[1][:, None] * freq_y[None, :] + positions[2][:, None] * freq_z[None, :]
    turns = turns - jnp.floor(turns)
    phase_re = jnp.cos(2.0 * math.pi * turns)
    phase_im = -jnp.sin(2.0 * math.pi * turns)
    chooser = (species[:, None] == jnp.arange(NSPEC, dtype=jnp.int32)[None, :]).astype(jnp.float32)
    q_re = qfunc[0].reshape(NSPEC * NH * NH, NG)
    q_im = qfunc[1].reshape(NSPEC * NH * NH, NG)
    axis_x = jnp.arange(half_size, dtype=jnp.int32)
    axis_y = signed_freq(jnp.arange(grid_size, dtype=jnp.int32), grid_size)
    norm_sq = axis_x[:, None, None] ** 2 + axis_y[None, :, None] ** 2 + axis_y[None, None, :] ** 2
    kernel = jnp.where(norm_sq > 0, strength / jnp.maximum(norm_sq, 1).astype(jnp.float32), 0.0).reshape(-1)
    highest = lax.Precision.HIGHEST

    def pair_terms(first_field, first_coef, second_field, second_coef):
        density = first_field * second_field
        spectrum = jnp.fft.rfftn(density, axes=(1, 2, 0)).reshape(-1)
        outer = 0.5 * (first_coef[:, :, None] * second_coef[:, None, :] + second_coef[:, :, None] * first_coef[:, None, :])
        mixed = (chooser[:, :, None] * outer.reshape(ATOMS, 1, NH * NH)).reshape(ATOMS, NSPEC * NH * NH)
        z_re = jnp.dot(mixed, q_re, precision=highest)
        z_im = jnp.dot(mixed, q_im, precision=highest)
        aug_re = aug_scale * lax.optimization_barrier(jnp.sum(phase_re * z_re - phase_im * z_im, axis=0))
        aug_im = aug_scale * lax.optimization_barrier(jnp.sum(phase_re * z_im + phase_im * z_re, axis=0))
        spectrum = spectrum.at[glist].add(lax.complex(aug_re, aug_im))
        weighted = spectrum * kernel
        potential = jnp.fft.irfftn(weighted.reshape(half_size, grid_size, grid_size), s=(grid_size, grid_size, grid_size), axes=(1, 2, 0))
        picked = weighted[glist]
        w_re = jnp.real(picked)
        w_im = jnp.imag(picked)
        cross_re = w_re * phase_re + w_im * phase_im
        cross_im = w_re * phase_im - w_im * phase_re
        slopes = 2.0 * aug_scale / grid_size ** 3 * (jnp.dot(cross_re, q_re.T, precision=highest) - jnp.dot(cross_im, q_im.T, precision=highest))
        local = lax.optimization_barrier(jnp.sum(slopes.reshape(ATOMS, NSPEC, NH * NH) * chooser[:, :, None], axis=1)).reshape(ATOMS, NH, NH)
        symmetric = 0.5 * (local + jnp.swapaxes(local, 1, 2))
        own_proj = lax.optimization_barrier(jnp.sum(symmetric * second_coef[:, None, :], axis=2)).reshape(-1)
        return (potential.astype(jnp.float32) * second_field, own_proj)

    def band_terms(index):
        first_field = fields[index]
        first_coef = coeffs[index]

        def add_pair(carry, other):
            grid_part, proj_part = pair_terms(first_field, first_coef, fields[other], coeffs[other])
            return ((carry[0] + grid_part, carry[1] + proj_part), None)
        start = (jnp.zeros((grid_size, grid_size, grid_size), jnp.float32), jnp.zeros((ATOMS * NH,), jnp.float32))
        totals, unused = lax.scan(add_pair, start, jnp.arange(NB, dtype=jnp.int32))
        return (-0.5 * totals[0], -0.5 * totals[1])
    grid_out, proj_out = lax.map(band_terms, jnp.arange(NB, dtype=jnp.int32))
    return (grid_out.reshape(NB, grid_size, grid_size * grid_size), proj_out)
```

```python
import functools
import math

import jax
import jax.numpy as jnp
import ml_dtypes
import numpy as np
from jax import lax
from jax.experimental import pallas as pl
from jax.experimental.pallas import tpu as pltpu
from jax.sharding import PartitionSpec as P

N = 36
NG6 = 6
LG = 256
LANES = NG6 * LG
XB = 48
XO = 40
KR = 24
KA = 16
ATOMS, NH, NSPEC, NLIST = 32, 8, 2, 1024
LM = NSPEC * NH * NH
AUG = N**1.5 / (NH * math.sqrt(ATOMS))
SLOTS = 5
F32, BF16 = jnp.float32, jnp.bfloat16


def split_np(a):
    hi = a.astype(np.float32).astype(ml_dtypes.bfloat16)
    lo = (a - hi.astype(np.float64)).astype(np.float32).astype(ml_dtypes.bfloat16)
    return hi, lo


def make_tables():
    k = np.arange(19)[:, None]
    x = np.arange(N)[None, :]
    ang = 2 * np.pi * (k * x % N) / N
    fwd = np.zeros((2 * KR, XB))
    fwd[:19, :N] = np.cos(ang)
    fwd[KR : KR + 19, :N] = -np.sin(ang)
    weight = np.where((k == 0) | (k == N // 2), 1.0, 2.0) / N**3
    inv = np.zeros((XO, 2 * KR))
    inv[:N, :19] = (weight * np.cos(ang)).T
    inv[:N, KR : KR + 19] = (-weight * np.sin(ang)).T
    fh, fl = split_np(fwd)
    ih, il = split_np(inv)
    fwd3 = np.concatenate([fh, fh, fl], axis=1)
    inv3 = np.concatenate([ih, ih, il], axis=1)
    r = np.arange(6)
    z = np.arange(N)
    r_of = np.repeat(r, N)
    z_of = np.tile(z, 6)
    ang = 2 * np.pi * ((6 * r_of[:, None] * r_of[None, :] + z_of[:, None] * z_of[None, :]) % N) / N
    c = np.zeros((LG, LG))
    s = np.zeros((LG, LG))
    c[:216, :216] = np.cos(ang)
    s[:216, :216] = np.sin(ang)
    wf = np.block([[c, -s], [s, c]])
    wi = np.block([[c, s], [-s, c]])
    wfh, wfl = split_np(wf)
    wih, wil = split_np(wi)
    tw = np.zeros((16, LG), np.float32)
    for q in range(6):
        a = 2 * np.pi * (r_of * q % N) / N
        tw[q, :216] = np.cos(a)
        tw[8 + q, :216] = -np.sin(a)
    kern = np.zeros((NG6 * KR, LG), np.float32)
    sg = lambda v: np.where(v > N // 2, v - N, v)
    for q in range(6):
        ky = q + 6 * r_of
        for kx in range(19):
            n2 = kx**2 + sg(ky) ** 2 + sg(z_of) ** 2
            kern[q * KR + kx, :216] = np.where(n2 > 0, N**1.5 / 4 / np.maximum(n2, 1), 0)
    kk = np.arange(256)[:, None]
    col = np.arange(LM)[None, :]
    rl = (kk % NH == (col % 64) // NH).astype(np.float32)
    rm = (kk % NH == col % NH).astype(np.float32)
    rep = np.concatenate([rl, rm], axis=1).astype(ml_dtypes.bfloat16)
    rsum = rl.T.astype(ml_dtypes.bfloat16)
    return dict(fwd3=fwd3, inv3=inv3, wfh=wfh, wfl=wfl, wih=wih, wil=wil, tw=tw, kern=kern, rep=rep, rsum=rsum)


TABLES = make_tables()
TABLE_NAMES = ("fwd3", "inv3", "wfh", "wfl", "wih", "wil", "tw", "kern", "rep", "rsum")


def split(a):
    hi = a.astype(BF16)
    return hi, (a - hi.astype(F32)).astype(BF16)


def mm(a, b):
    return jnp.dot(a, b, preferred_element_type=F32)


def mm_nt(a, b):
    return lax.dot_general(a, b, (((1,), (1,)), ((), ())), preferred_element_type=F32)


def dft3(a, b, c, sign):
    h = math.sqrt(3.0) / 2
    sr, si = b[0] + c[0], b[1] + c[1]
    dr, di = (b[0] - c[0]) * h, (b[1] - c[1]) * h
    tr, ti = a[0] - 0.5 * sr, a[1] - 0.5 * si
    zero = (a[0] + sr, a[1] + si)
    minus = (tr + di, ti - dr)
    plus = (tr - di, ti + dr)
    return (zero, minus, plus) if sign < 0 else (zero, plus, minus)


def dft6(v, sign):
    add = lambda p, q: (p[0] + q[0], p[1] + q[1])
    sub = lambda p, q: (p[0] - q[0], p[1] - q[1])
    e = dft3(add(v[0], v[3]), add(v[1], v[4]), add(v[2], v[5]), sign)
    o = dft3(sub(v[0], v[3]), sub(v[4], v[1]), sub(v[2], v[5]), sign)
    return [e[0], o[2], e[1], o[0], e[2], o[1]]


def pair_indices(special, x):
    one = jnp.where(special, 0, 1)
    first = (jnp.where(special, x, 0), one, jnp.where(special, 1 - x, 0), one, 1)
    second = (2, jnp.where(special, 0, 2), 3, jnp.where(special, 1, 3), 1)
    return first, second


def setup_lists(glist_ref, positions_ref, species_ref, yzt_ref, phase_ref, choose_ref):
    g = glist_ref[...]
    kx = g // (N * N)
    ky = g // N % N
    kz = g % N
    where = (ky % 6) * LG + (ky // 6) * N + kz
    step = 256
    for base in range(0, LANES, step):
        rows = lax.broadcasted_iota(jnp.int32, (step, NLIST), 0) + base
        yzt_ref[base : base + step, :] = jnp.where(rows == where, 1.0, 0.0).astype(BF16)
    sg = lambda v: jnp.where(v > N // 2, v - N, v).astype(F32)
    eye = lax.broadcasted_iota(jnp.int32, (ATOMS, ATOMS), 0) == lax.broadcasted_iota(jnp.int32, (ATOMS, ATOMS), 1)
    column = lambda row: jnp.sum(jnp.where(eye, row, 0.0), axis=1, keepdims=True)
    turns = (
        column(positions_ref[0:1, :]) * kx.astype(F32)
        + column(positions_ref[1:2, :]) * sg(ky)
        + column(positions_ref[2:3, :]) * sg(kz)
    )
    theta = (turns - jnp.floor(turns)) * (2.0 * math.pi)
    phase_ref[0] = jnp.cos(theta)
    phase_ref[1] = -jnp.sin(theta)
    spec = column(species_ref[...].astype(F32))
    of_lane = lax.broadcasted_iota(jnp.int32, (ATOMS, LM), 1) // (NH * NH)
    choose_ref[...] = jnp.where(spec == of_lane.astype(F32), 1.0, 0.0)


def expand_coef(coef_ref, b, rep_ref, exp_ref):
    row = coef_ref[b].astype(F32)
    own = lax.broadcasted_iota(jnp.int32, (ATOMS, 256), 1) // NH == lax.broadcasted_iota(jnp.int32, (ATOMS, 256), 0)
    exp_ref[b] = mm(jnp.where(own, row, 0.0).astype(BF16), rep_ref[...])


def kx_of_rows(glist_ref):
    kx = glist_ref[...] // (N * N)
    rows = lax.broadcasted_iota(jnp.int32, (SLOTS * 2 * KA, NLIST), 0) % KA
    return rows == kx


def augment(first, second, glist_ref, qs_ref, exp_ref, choose_ref, phase_ref, yzt_ref, faug_ref):
    mixed = jnp.concatenate(
        [exp_ref[i][:, :LM] * exp_ref[j][:, LM:] * choose_ref[...] for i, j in zip(first, second)], axis=0
    )
    hi, lo = split(mixed)
    rows = []
    zs = []
    for c in range(2):
        qh, ql = split(qs_ref[c])
        zs.append(mm(hi, qh) + mm(lo, qh) + mm(hi, ql))
    z_re, z_im = zs
    for t in range(SLOTS):
        zr, zi = z_re[t * ATOMS : (t + 1) * ATOMS], z_im[t * ATOMS : (t + 1) * ATOMS]
        rows.append(jnp.sum(phase_ref[0] * zr - phase_ref[1] * zi, axis=0, keepdims=True) * AUG)
        rows.append(jnp.sum(phase_ref[0] * zi + phase_ref[1] * zr, axis=0, keepdims=True) * AUG)
    spread = jnp.concatenate([jnp.broadcast_to(row, (KA, NLIST)) for row in rows], axis=0)
    spread = jnp.where(kx_of_rows(glist_ref), spread, 0.0)
    hi, lo = split(spread)
    for base in range(0, LANES, LG):
        part = yzt_ref[base : base + LG, :]
        faug_ref[:, base : base + LG] = mm_nt(hi, part) + mm_nt(lo, part)


def pairs(slots, first, second, band_ref, faug_ref, wst_ref, acc_ref, lhs_ref, tabs):
    n = len(slots)
    for m, t in enumerate(slots):
        rho = band_ref[first[t]].astype(F32) * band_ref[second[t]].astype(F32)
        hi, lo = split(rho)
        spec = mm(tabs["fwd3"][...], jnp.concatenate([hi, lo, hi], axis=0))
        v = [
            (spec[:KR, g * LG : (g + 1) * LG], spec[KR:, g * LG : (g + 1) * LG]) for g in range(NG6)
        ]
        for q, (re, im) in enumerate(dft6(v, -1)):
            if q:
                cr, ci = tabs["tw"][q : q + 1, :], tabs["tw"][8 + q : 9 + q, :]
                re, im = re * cr - im * ci, re * ci + im * cr
            at = (q * n + m) * KR
            lhs_ref[at : at + KR, :LG] = re
            lhs_ref[at : at + KR, LG:] = im
    rows = NG6 * n * KR
    hi, lo = split(lhs_ref[:rows, :])
    f = mm(hi, tabs["wfh"][...]) + mm(lo, tabs["wfh"][...]) + mm(hi, tabs["wfl"][...])
    for q in range(NG6):
        kern = tabs["kern"][q * KR : (q + 1) * KR, :]
        for m, t in enumerate(slots):
            at = (q * n + m) * KR
            for c in range(2):
                w = f[at : at + KR, c * LG : (c + 1) * LG]
                a = (t * 2 + c) * KA
                low = (w[:KA] + faug_ref[a : a + KA, q * LG : (q + 1) * LG]) * kern[:KA]
                wst_ref[a : a + KA, q * LG : (q + 1) * LG] = low
                lhs_ref[at : at + KA, c * LG : (c + 1) * LG] = low
                lhs_ref[at + KA : at + KR, c * LG : (c + 1) * LG] = w[KA:] * kern[KA:]
    hi, lo = split(lhs_ref[:rows, :])
    f = mm(hi, tabs["wih"][...]) + mm(lo, tabs["wih"][...]) + mm(hi, tabs["wil"][...])
    for m, t in enumerate(slots):
        v = []
        for q in range(NG6):
            at = (q * n + m) * KR
            re, im = f[at : at + KR, :LG], f[at : at + KR, LG:]
            if q:
                cr, ci = tabs["tw"][q : q + 1, :], tabs["tw"][8 + q : 9 + q, :]
                re, im = re * cr + im * ci, im * cr - re * ci
            v.append((re, im))
        v = dft6(v, 1)
        w = jnp.concatenate([jnp.concatenate([p[0], p[1]], axis=0) for p in v], axis=1)
        hi, lo = split(w)
        pot = mm(tabs["inv3"][...], jnp.concatenate([hi, lo, hi], axis=0))
        i, j = first[t], second[t]
        acc_ref[i] += pot * band_ref[j].astype(F32)[:XO]
        twice = jnp.where(jnp.int32(i) == jnp.int32(j), 0.0, 1.0)
        acc_ref[j] += pot * band_ref[i].astype(F32)[:XO] * twice


def slopes(slots, first, second, glist_ref, qs_ref, exp_ref, choose_ref, phase_ref, yzt_ref, wst_ref, pacc_ref):
    hi, lo = split(wst_ref[...])
    picked = mm(hi, yzt_ref[...]) + mm(lo, yzt_ref[...])
    picked = jnp.where(kx_of_rows(glist_ref), picked, 0.0)
    re_rows, im_rows = [], []
    for t in range(SLOTS):
        a = t * 2 * KA
        wr = jnp.sum(picked[a : a + KA], axis=0, keepdims=True)
        wi = jnp.sum(picked[a + KA : a + 2 * KA], axis=0, keepdims=True)
        re_rows.append(wr * phase_ref[0] + wi * phase_ref[1])
        im_rows.append(wi * phase_ref[0] - wr * phase_ref[1])
    total = None
    for c, cross in enumerate((re_rows, im_rows)):
        ch, cl = split(jnp.concatenate(cross, axis=0))
        qh, ql = split(qs_ref[c])
        part = mm_nt(ch, qh) + mm_nt(cl, qh) + mm_nt(ch, ql)
        total = part if total is None else total + part
    total = total * (2.0 * AUG / N**3)
    for t in range(SLOTS):
        slope = total[t * ATOMS : (t + 1) * ATOMS] * choose_ref[...]
        i, j = first[t], second[t]

        def give(slope=slope, i=i, j=j):
            pacc_ref[i] += slope * exp_ref[j][:, LM:]
            twice = jnp.where(jnp.int32(i) == jnp.int32(j), 0.0, 1.0)
            pacc_ref[j] += slope * exp_ref[i][:, LM:] * twice

        if t in slots:
            give()
        else:
            pl.when(slots[t])(give)


def coef_rows(pacc_ref, rsum_ref):
    own = lax.broadcasted_iota(jnp.int32, (ATOMS, 256), 1) // NH == lax.broadcasted_iota(jnp.int32, (ATOMS, 256), 0)
    out = []
    for b in range(4):
        hi, lo = split(pacc_ref[b])
        full = mm(hi, rsum_ref[...]) + mm(lo, rsum_ref[...])
        out.append(jnp.sum(jnp.where(own, full, 0.0), axis=0, keepdims=True))
    return out


def local_kernel(*refs):
    nt = len(TABLE_NAMES)
    (meta_ref, band_ref, coef_ref, qs_ref, species_ref, positions_ref, glist_ref) = refs[:7]
    tabs = dict(zip(TABLE_NAMES, refs[7 : 7 + nt]))
    acc_ref = refs[7 + nt]
    (yzt_ref, phase_ref, choose_ref, exp_ref, faug_ref, wst_ref, lhs_ref, pacc_ref) = refs[8 + nt :]
    special = meta_ref[0] == 1
    x = meta_ref[1]
    setup_lists(glist_ref, positions_ref, species_ref, yzt_ref, phase_ref, choose_ref)
    for b in range(4):
        expand_coef(coef_ref, b, tabs["rep"], exp_ref)
    first, second = pair_indices(special, x)
    acc_ref[...] = jnp.zeros_like(acc_ref)
    pacc_ref[...] = jnp.zeros_like(pacc_ref)
    wst_ref[...] = jnp.zeros_like(wst_ref)
    augment(first, second, glist_ref, qs_ref, exp_ref, choose_ref, phase_ref, yzt_ref, faug_ref)
    run = functools.partial(pairs, first=first, second=second, band_ref=band_ref, faug_ref=faug_ref,
                            wst_ref=wst_ref, acc_ref=acc_ref, lhs_ref=lhs_ref, tabs=tabs)
    run((0, 1))
    run((2, 3))
    pl.when(special)(lambda: run((4,)))
    slopes(SlotSet(special), first, second, glist_ref, qs_ref,
           exp_ref, choose_ref, phase_ref, yzt_ref, wst_ref, pacc_ref)
    for b, row in enumerate(coef_rows(pacc_ref, tabs["rsum"])):
        acc_ref[b, N : N + 1, :LG] = row


class SlotSet:
    def __init__(self, special):
        self.special = special

    def __contains__(self, t):
        return t < 4

    def __getitem__(self, t):
        return self.special


def local_call(meta, bands4, coefs4, qs, species, positions, glist):
    vm = pl.BlockSpec(memory_space=pltpu.VMEM)
    return pl.pallas_call(
        local_kernel,
        out_shape=jax.ShapeDtypeStruct((4, XO, LANES), F32),
        in_specs=[pl.BlockSpec(memory_space=pltpu.SMEM)] + [vm] * (6 + len(TABLE_NAMES)),
        out_specs=vm,
        scratch_shapes=[
            pltpu.VMEM((LANES, NLIST), BF16),
            pltpu.VMEM((2, ATOMS, NLIST), F32),
            pltpu.VMEM((ATOMS, LM), F32),
            pltpu.VMEM((4, ATOMS, 2 * LM), F32),
            pltpu.VMEM((SLOTS * 2 * KA, LANES), F32),
            pltpu.VMEM((SLOTS * 2 * KA, LANES), F32),
            pltpu.VMEM((2 * NG6 * KR, 2 * LG), F32),
            pltpu.VMEM((4, ATOMS, LM), F32),
        ],
        compiler_params=pltpu.CompilerParams(vmem_limit_bytes=48 * 2**20),
    )(meta, bands4, coefs4, qs, species.reshape(1, ATOMS), positions, glist.reshape(1, NLIST),
      *[jnp.asarray(TABLES[name]) for name in TABLE_NAMES])


def offset_of(slot):
    return slot + 1 if slot % 2 == 0 or slot == 15 else 32 - (slot + 1)


def on_device(bands, projections, qfunc, species, positions, glist):
    row, col = lax.axis_index("row"), lax.axis_index("col")
    group, core = row // 2, row % 2
    slot = col * 2 + core
    special = slot == 15
    x = jnp.where(group >= 16, 1, 0)
    meta = jnp.stack([special.astype(jnp.int32), x.astype(jnp.int32)])
    dev = lambda g, c, k: ((g % 32) * 2 + k) * 8 + c
    ids = [(g, c, k) for g in range(32) for c in range(8) for k in range(2)]
    sib = [(dev(g, c, k), dev(g, c, 1 - k)) for g, c, k in ids]
    near = [(dev(g, c, k), dev(g - offset_of(2 * c + k), c, k)) for g, c, k in ids]
    far = [(dev(g, c, k), dev(g - offset_of(2 * c + 1 - k), c, 1 - k)) for g, c, k in ids]
    back = [(b, a) for a, b in near]
    axes = ("row", "col")
    field = jnp.pad(bands[0].reshape(N, NG6, 216), ((0, XB - N), (0, 0), (0, LG - 216))).reshape(XB, LANES)
    coef = projections
    parts = [(field, coef)] + [(lax.ppermute(field, axes, p), lax.ppermute(coef, axes, p)) for p in (sib, near, far)]
    bands4 = jnp.stack([p[0] for p in parts])
    coefs4 = jnp.stack([p[1] for p in parts])
    q5 = qfunc.reshape(2, NSPEC, NH, NH, NLIST)
    qs = (0.5 * (q5 + jnp.swapaxes(q5, 2, 3))).reshape(2, LM, NLIST)
    acc = local_call(meta, bands4, coefs4, qs, species, positions, glist)
    got = lax.ppermute(acc[2:], axes, back)
    mine = acc[:2] + got
    total = mine[0] + lax.ppermute(mine[1], axes, sib)
    grid = total[:N].reshape(N, NG6, LG)[:, :, :216].reshape(N, 8, 162).transpose(1, 0, 2)
    proj = total[N, :LG].reshape(8, 32)
    grid = lax.all_to_all(grid, "col", 0, 0, tiled=True)
    proj = lax.all_to_all(proj, "col", 0, 0, tiled=True)
    return (-0.5 * jnp.sum(grid.reshape(8, N, 162), axis=0)[None], -0.5 * jnp.sum(proj.reshape(8, 32), axis=0)[None])


def solution(mesh):
    return jax.shard_map(
        on_device,
        mesh=mesh,
        in_specs=(P("row", None, None), P("row", None), P(), P(), P(), P()),
        out_specs=(P("row", None, "col"), P("row", "col")),
        check_vma=False,
    )
```

```python
import functools
import math

import jax
import jax.numpy as jnp
import ml_dtypes
import numpy as np
from jax import lax
from jax.experimental import pallas as pl
from jax.experimental.pallas import tpu as pltpu
from jax.sharding import PartitionSpec as P

N = 36
NG6 = 6
LG = 256
LANES = NG6 * LG
XB = 48
XO = 40
KR = 24
KA = 16
ATOMS, NH, NSPEC, NLIST = 32, 8, 2, 1024
LM = NSPEC * NH * NH
AUG = N**1.5 / (NH * math.sqrt(ATOMS))
SLOTS = 5
TAIL = 384
CHUNK = 162
F32, BF16 = jnp.float32, jnp.bfloat16


def split_np(a):
    hi = a.astype(np.float32).astype(ml_dtypes.bfloat16)
    lo = (a - hi.astype(np.float64)).astype(np.float32).astype(ml_dtypes.bfloat16)
    return hi, lo


def make_tables():
    k = np.arange(19)[:, None]
    x = np.arange(N)[None, :]
    ang = 2 * np.pi * (k * x % N) / N
    fwd = np.zeros((2 * KR, XB))
    fwd[:19, :N] = np.cos(ang)
    fwd[KR : KR + 19, :N] = -np.sin(ang)
    weight = np.where((k == 0) | (k == N // 2), 1.0, 2.0) / N**3
    inv = np.zeros((XO, 2 * KR))
    inv[:N, :19] = (weight * np.cos(ang)).T
    inv[:N, KR : KR + 19] = (-weight * np.sin(ang)).T
    fh, fl = split_np(fwd)
    ih, il = split_np(inv)
    fwd3 = np.concatenate([fh, fh, fl], axis=1)
    inv3 = np.concatenate([ih, ih, il], axis=1)
    r = np.arange(6)
    z = np.arange(N)
    r_of = np.repeat(r, N)
    z_of = np.tile(z, 6)
    ang = 2 * np.pi * ((6 * r_of[:, None] * r_of[None, :] + z_of[:, None] * z_of[None, :]) % N) / N
    c = np.zeros((LG, LG))
    s = np.zeros((LG, LG))
    c[:216, :216] = np.cos(ang)
    s[:216, :216] = np.sin(ang)
    wf = np.block([[c, -s], [s, c]])
    wi = np.block([[c, s], [-s, c]])
    wfh, wfl = split_np(wf)
    wih, wil = split_np(wi)
    tw = np.zeros((16, LG), np.float32)
    for q in range(6):
        a = 2 * np.pi * (r_of * q % N) / N
        tw[q, :216] = np.cos(a)
        tw[8 + q, :216] = -np.sin(a)
    kern = np.zeros((NG6 * KR, LG), np.float32)
    sg = lambda v: np.where(v > N // 2, v - N, v)
    for q in range(6):
        ky = q + 6 * r_of
        for kx in range(19):
            n2 = kx**2 + sg(ky) ** 2 + sg(z_of) ** 2
            kern[q * KR + kx, :216] = np.where(n2 > 0, N**1.5 / 4 / np.maximum(n2, 1), 0)
    kk = np.arange(256)[:, None]
    col = np.arange(LM)[None, :]
    rl = (kk % NH == (col % 64) // NH).astype(np.float32)
    rm = (kk % NH == col % NH).astype(np.float32)
    rep = np.concatenate([rl, rm], axis=1).astype(ml_dtypes.bfloat16)
    rsum = np.ascontiguousarray(rep.T)
    dft = np.stack([wfh, wfl, wih, wil])
    return dict(fwd3=fwd3, inv3=inv3, dft=dft, tw=tw, kern=kern, rep=rep, rsum=rsum)


TABLES = make_tables()
TABLE_NAMES = ("fwd3", "inv3", "dft", "tw", "kern", "rep", "rsum")


def split(a):
    hi = a.astype(BF16)
    return hi, (a - hi.astype(F32)).astype(BF16)


def mm(a, b):
    return jnp.dot(a, b, preferred_element_type=F32)


def mm_nt(a, b):
    return lax.dot_general(a, b, (((1,), (1,)), ((), ())), preferred_element_type=F32)


def dft3(a, b, c, sign):
    h = math.sqrt(3.0) / 2
    sr, si = b[0] + c[0], b[1] + c[1]
    dr, di = (b[0] - c[0]) * h, (b[1] - c[1]) * h
    tr, ti = a[0] - 0.5 * sr, a[1] - 0.5 * si
    zero = (a[0] + sr, a[1] + si)
    minus = (tr + di, ti - dr)
    plus = (tr - di, ti + dr)
    return (zero, minus, plus) if sign < 0 else (zero, plus, minus)


def dft6(v, sign):
    add = lambda p, q: (p[0] + q[0], p[1] + q[1])
    sub = lambda p, q: (p[0] - q[0], p[1] - q[1])
    e = dft3(add(v[0], v[3]), add(v[1], v[4]), add(v[2], v[5]), sign)
    o = dft3(sub(v[0], v[3]), sub(v[4], v[1]), sub(v[2], v[5]), sign)
    return [e[0], o[2], e[1], o[0], e[2], o[1]]


def pair_indices(special, x):
    first = (jnp.where(special, x, 0), 1, jnp.where(special, 1 - x, 0), jnp.where(special, 0, 1), 0)
    second = (2, jnp.where(special, 1, 2), 3, jnp.where(special, 1, 3), 0)
    return first, second


def setup_lists(glist_ref, positions_ref, species_ref, yzt_ref, phase_ref, choose_ref):
    g = glist_ref[...]
    kx = g // (N * N)
    ky = g // N % N
    kz = g % N
    where = (ky % 6) * LG + (ky // 6) * N + kz
    step = 256
    for base in range(0, LANES, step):
        rows = lax.broadcasted_iota(jnp.int32, (step, NLIST), 0) + base
        yzt_ref[base : base + step, :] = jnp.where(rows == where, 1.0, 0.0).astype(BF16)
    sg = lambda v: jnp.where(v > N // 2, v - N, v).astype(F32)
    eye = lax.broadcasted_iota(jnp.int32, (ATOMS, ATOMS), 0) == lax.broadcasted_iota(jnp.int32, (ATOMS, ATOMS), 1)
    column = lambda row: jnp.sum(jnp.where(eye, row, 0.0), axis=1, keepdims=True)
    turns = (
        column(positions_ref[0:1, :]) * kx.astype(F32)
        + column(positions_ref[1:2, :]) * sg(ky)
        + column(positions_ref[2:3, :]) * sg(kz)
    )
    theta = (turns - jnp.floor(turns)) * (2.0 * math.pi)
    phase_ref[0] = jnp.cos(theta)
    phase_ref[1] = -jnp.sin(theta)
    spec = column(species_ref[...].astype(F32))
    of_lane = lax.broadcasted_iota(jnp.int32, (ATOMS, LM), 1) // (NH * NH)
    choose_ref[...] = jnp.where(spec == of_lane.astype(F32), 1.0, 0.0)


def atom_of_lane():
    lane = lax.broadcasted_iota(jnp.int32, (ATOMS, 256), 1)
    return lane // NH == lax.broadcasted_iota(jnp.int32, (ATOMS, 256), 0)


def expand_coef(row, rep):
    return mm(jnp.where(atom_of_lane(), row, 0.0).astype(BF16), rep)


def kx_of_rows(glist_ref):
    kx = glist_ref[...] // (N * N)
    rows = lax.broadcasted_iota(jnp.int32, (SLOTS * 2 * KA, NLIST), 0) % KA
    return rows == kx


def augment(first, second, glist_ref, qs_ref, exp_ref, choose_ref, phase_ref, yzt_ref, faug_ref):
    mixed = jnp.concatenate(
        [
            (exp_ref[i][:, :LM] * exp_ref[j][:, LM:] + exp_ref[j][:, :LM] * exp_ref[i][:, LM:])
            * (0.5 * choose_ref[...])
            for i, j in zip(first, second)
        ],
        axis=0,
    )
    hi, lo = split(mixed)
    rows = []
    zs = []
    for c in range(2):
        qh, ql = qs_ref[2 * c], qs_ref[2 * c + 1]
        zs.append(mm(hi, qh) + mm(lo, qh) + mm(hi, ql))
    z_re, z_im = zs
    for t in range(SLOTS):
        zr, zi = z_re[t * ATOMS : (t + 1) * ATOMS], z_im[t * ATOMS : (t + 1) * ATOMS]
        rows.append(jnp.sum(phase_ref[0] * zr - phase_ref[1] * zi, axis=0, keepdims=True) * AUG)
        rows.append(jnp.sum(phase_ref[0] * zi + phase_ref[1] * zr, axis=0, keepdims=True) * AUG)
    spread = jnp.concatenate([jnp.broadcast_to(row, (KA, NLIST)) for row in rows], axis=0)
    spread = jnp.where(kx_of_rows(glist_ref), spread, 0.0)
    hi, lo = split(spread)
    for base in range(0, LANES, LG):
        part = yzt_ref[base : base + LG, :]
        faug_ref[:, base : base + LG] = mm_nt(hi, part) + mm_nt(lo, part)


def pairs(slots, first, second, band_ref, faug_ref, wst_ref, acc_ref, lhs_ref, tabs):
    n = len(slots)
    for m, t in enumerate(slots):
        rho = band_ref[first[t]].astype(F32) * band_ref[second[t]].astype(F32)
        hi, lo = split(rho)
        spec = mm(tabs["fwd3"][...], jnp.concatenate([hi, lo, hi], axis=0))
        v = [
            (spec[:KR, g * LG : (g + 1) * LG], spec[KR:, g * LG : (g + 1) * LG]) for g in range(NG6)
        ]
        for q, (re, im) in enumerate(dft6(v, -1)):
            if q:
                cr, ci = tabs["tw"][q : q + 1, :], tabs["tw"][8 + q : 9 + q, :]
                re, im = re * cr - im * ci, re * ci + im * cr
            at = (q * n + m) * KR
            lhs_ref[at : at + KR, :LG] = re
            lhs_ref[at : at + KR, LG:] = im
    rows = NG6 * n * KR
    hi, lo = split(lhs_ref[:rows, :])
    f = mm(hi, tabs["dft"][0]) + mm(lo, tabs["dft"][0]) + mm(hi, tabs["dft"][1])
    for q in range(NG6):
        kern = tabs["kern"][q * KR : (q + 1) * KR, :]
        for m, t in enumerate(slots):
            at = (q * n + m) * KR
            for c in range(2):
                w = f[at : at + KR, c * LG : (c + 1) * LG]
                a = (t * 2 + c) * KA
                low = (w[:KA] + faug_ref[a : a + KA, q * LG : (q + 1) * LG]) * kern[:KA]
                wst_ref[a : a + KA, q * LG : (q + 1) * LG] = low
                lhs_ref[at : at + KA, c * LG : (c + 1) * LG] = low
                lhs_ref[at + KA : at + KR, c * LG : (c + 1) * LG] = w[KA:] * kern[KA:]
    hi, lo = split(lhs_ref[:rows, :])
    f = mm(hi, tabs["dft"][2]) + mm(lo, tabs["dft"][2]) + mm(hi, tabs["dft"][3])
    for m, t in enumerate(slots):
        v = []
        for q in range(NG6):
            at = (q * n + m) * KR
            re, im = f[at : at + KR, :LG], f[at : at + KR, LG:]
            if q:
                cr, ci = tabs["tw"][q : q + 1, :], tabs["tw"][8 + q : 9 + q, :]
                re, im = re * cr + im * ci, im * cr - re * ci
            v.append((re, im))
        v = dft6(v, 1)
        w = jnp.concatenate([jnp.concatenate([p[0], p[1]], axis=0) for p in v], axis=1)
        hi, lo = split(w)
        pot = mm(tabs["inv3"][...], jnp.concatenate([hi, lo, hi], axis=0))
        i, j = first[t], second[t]
        acc_ref[i] += pot * band_ref[j].astype(F32)[:XO]
        twice = jnp.where(jnp.int32(i) == jnp.int32(j), 0.0, 1.0)
        acc_ref[j] += pot * band_ref[i].astype(F32)[:XO] * twice


def slopes(special, first, second, glist_ref, qs_ref, exp_ref, choose_ref, phase_ref, yzt_ref, wst_ref, pacc_ref):
    hi, lo = split(wst_ref[...])
    picked = mm(hi, yzt_ref[...]) + mm(lo, yzt_ref[...])
    picked = jnp.where(kx_of_rows(glist_ref), picked, 0.0)
    re_rows, im_rows = [], []
    for t in range(SLOTS):
        a = t * 2 * KA
        wr = jnp.sum(picked[a : a + KA], axis=0, keepdims=True)
        wi = jnp.sum(picked[a + KA : a + 2 * KA], axis=0, keepdims=True)
        re_rows.append(wr * phase_ref[0] + wi * phase_ref[1])
        im_rows.append(wi * phase_ref[0] - wr * phase_ref[1])
    total = None
    for c, cross in enumerate((re_rows, im_rows)):
        ch, cl = split(jnp.concatenate(cross, axis=0))
        qh, ql = qs_ref[2 * c], qs_ref[2 * c + 1]
        part = mm_nt(ch, qh) + mm_nt(cl, qh) + mm_nt(ch, ql)
        total = part if total is None else total + part
    total = total * (AUG / N**3)
    for t in range(SLOTS):
        slope = total[t * ATOMS : (t + 1) * ATOMS] * choose_ref[...]
        slope = jnp.concatenate([slope, slope], axis=1)
        if t == 4:
            slope = slope * jnp.where(special, 1.0, 0.0)
        i, j = first[t], second[t]
        swap = lambda b: jnp.concatenate([exp_ref[b][:, LM:], exp_ref[b][:, :LM]], axis=1)
        twice = jnp.where(jnp.int32(i) == jnp.int32(j), 0.0, 1.0)
        pacc_ref[i] += slope * swap(j)
        pacc_ref[j] += slope * swap(i) * twice


def coef_row(pacc, rsum):
    hi, lo = split(pacc)
    full = mm(hi, rsum) + mm(lo, rsum)
    return jnp.sum(jnp.where(atom_of_lane(), full, 0.0), axis=0, keepdims=True)


def pack_tail(rows):
    return jnp.concatenate([rows[:, TAIL * j : TAIL * (j + 1)] for j in range(4)], axis=0)


def unpack_tail(tail):
    rows = jnp.concatenate([tail[4 * j : 4 * (j + 1)] for j in range(4)], axis=1)
    return jnp.concatenate([rows, jnp.zeros((12, LANES), F32)], axis=0)


def columns(total, c):
    start = CHUNK * c
    parts = []
    while start < CHUNK * (c + 1):
        g, at = divmod(start, 216)
        end = min(216 * (g + 1), CHUNK * (c + 1))
        parts.append(total[:, g * LG + at : g * LG + at + end - start])
        start = end
    return parts[0] if len(parts) == 1 else jnp.concatenate(parts, axis=1)


def pack_chunk(total, proj, c):
    part = columns(total, c)
    coefs = jnp.concatenate([proj[:, 32 * c : 32 * (c + 1)], jnp.zeros((1, 96), F32)], axis=1)
    main = jnp.concatenate([part[:N, :128], coefs, jnp.zeros((3, 128), F32)], axis=0)
    rest = part[:, 128:]
    last = jnp.concatenate([rest[32:40], jnp.zeros((8, 34), F32)], axis=0)
    rest = jnp.concatenate([rest[:16], rest[16:32], last, jnp.zeros((16, 26), F32)], axis=1)
    return jnp.concatenate([main, rest], axis=0)


def kernel(*refs):
    nt = len(TABLE_NAMES)
    bands_ref, coef_ref, q_hbm, species_ref, positions_ref, glist_ref = refs[:6]
    tables_hbm = refs[6 : 6 + nt]
    out_ref, proj_ref = refs[6 + nt : 8 + nt]
    scratch = refs[8 + nt :]
    tabs = dict(zip(TABLE_NAMES, scratch[:nt]))
    (band_ref, tail_ref, q_ref, qs_ref, yzt_ref, phase_ref, choose_ref, exp_ref, faug_ref, wst_ref, lhs_ref, pacc_ref,
     acc_ref, got_ref, pgive_ref, pgot_ref, chunk_ref, chunks_ref,
     table_sem, tail_send, tail_recv, band_send, band_recv, sum_send, sum_recv, coef_send, coef_recv,
     chunk_send, chunk_recv) = scratch[nt:]
    row, col = lax.axis_index("row"), lax.axis_index("col")
    group, core = row // 2, row % 2
    offset = (2 * col + core + 1) * (1 - 2 * core)
    other_offset = (2 * col + 2 - core) * (2 * core - 1)
    at = lambda g, k: (((g + 64) % 32) * 2 + k, col)
    sibling = at(group, 1 - core)
    ahead, ahead_other = at(group + offset, core), at(group + offset, 1 - core)
    behind, behind_other = at(group - offset, core), at(group - other_offset, 1 - core)
    peers = [(row, (col + step) % 8) for step in range(1, 8)]
    mesh_id = pl.DeviceIdType.MESH

    barrier = pltpu.get_barrier_semaphore()
    partners = [sibling, ahead, ahead_other, behind, behind_other] + peers
    for partner in partners:
        pl.semaphore_signal(barrier, inc=1, device_id=partner, device_id_type=mesh_id)

    loads = [
        pltpu.make_async_copy(src, dst, table_sem.at[n])
        for n, (src, dst) in enumerate(zip((*tables_hbm, q_hbm), (*scratch[:nt], q_ref)))
    ]
    for load in loads:
        load.start()

    def send(src, dst, to, sems, recvs, n):
        copy = pltpu.make_async_remote_copy(
            src_ref=src, dst_ref=dst, send_sem=sems.at[n], recv_sem=recvs.at[n], device_id=to, device_id_type=mesh_id
        )
        copy.start()
        return copy

    field = bands_ref[0].astype(F32)
    zero = jnp.zeros((N, LG - 216), F32)
    field = jnp.concatenate(
        [piece for g in range(NG6) for piece in (field[:, 216 * g : 216 * (g + 1)], zero)], axis=1
    )
    band_ref[0, 0:32, :] = field[:32].astype(BF16)
    tail = pack_tail(field[32:36])
    coef_rows = jnp.concatenate([coef_ref[...].astype(F32), jnp.zeros((1, TAIL - 256), F32)], axis=1)
    tail = jnp.concatenate([tail, coef_rows, jnp.zeros((15, TAIL), F32)], axis=0)
    tail_ref[0] = tail.astype(BF16)

    pl.semaphore_wait(barrier, len(partners))
    sends = []
    targets = (behind, behind_other, sibling)
    slots = (2, 3, 1)
    tails = [send(tail_ref.at[0], tail_ref.at[b], to, tail_send, tail_recv, b - 1) for b, to in zip(slots, targets)]
    fields = [
        send(band_ref.at[0, pl.ds(0, 32)], band_ref.at[b, pl.ds(0, 32)], to, band_send, band_recv, b - 1)
        for b, to in zip(slots, targets)
    ]
    sends += tails + fields

    special = jnp.logical_and(core == 1, col == 7)
    x = group // 16
    setup_lists(glist_ref, positions_ref, species_ref, yzt_ref, phase_ref, choose_ref)
    acc_ref[...] = jnp.zeros_like(acc_ref)
    pacc_ref[...] = jnp.zeros_like(pacc_ref)
    wst_ref[...] = jnp.zeros_like(wst_ref)
    for load in loads:
        load.wait()
    for c in range(2):
        for s in range(NSPEC):
            hi, lo = split(q_ref[c, s])
            qs_ref[2 * c, s * 64 : (s + 1) * 64] = hi
            qs_ref[2 * c + 1, s * 64 : (s + 1) * 64] = lo
    for b in range(4):
        if b:
            tails[slots.index(b)].wait_recv()
        tail = tail_ref[b].astype(F32)
        band_ref[b, 32:48, :] = unpack_tail(tail[:16]).astype(BF16)
        exp_ref[b] = expand_coef(tail[16:17, :256], tabs["rep"][...])
    first, second = pair_indices(special, x)
    augment(first, second, glist_ref, qs_ref, exp_ref, choose_ref, phase_ref, yzt_ref, faug_ref)
    run = functools.partial(
        pairs, first=first, second=second, band_ref=band_ref, faug_ref=faug_ref, wst_ref=wst_ref, acc_ref=acc_ref,
        lhs_ref=lhs_ref, tabs=tabs,
    )
    fields[2].wait_recv()
    fields[0].wait_recv()
    run((0, 1))
    sums = [send(acc_ref.at[2], got_ref.at[0], ahead, sum_send, sum_recv, 0)]
    fields[1].wait_recv()
    run((2, 3))
    sums.append(send(acc_ref.at[3], got_ref.at[1], ahead_other, sum_send, sum_recv, 1))
    sums.append(send(acc_ref.at[1], got_ref.at[2], sibling, sum_send, sum_recv, 2))
    pl.when(special)(lambda: run((4,)))
    slopes(special, first, second, glist_ref, qs_ref, exp_ref, choose_ref, phase_ref, yzt_ref, wst_ref, pacc_ref)
    for n, b in enumerate((2, 3, 1)):
        pgive_ref[n] = jnp.broadcast_to(coef_row(pacc_ref[b], tabs["rsum"][...]), (8, 256))
    coefs = [
        send(pgive_ref.at[n], pgot_ref.at[n], to, coef_send, coef_recv, n)
        for n, to in enumerate((ahead, ahead_other, sibling))
    ]
    sends += sums + coefs
    proj = coef_row(pacc_ref[0], tabs["rsum"][...])
    total = acc_ref[0]
    for n in (2, 0, 1):
        sums[n].wait_recv()
        total = total + got_ref[n]
    for n in (2, 0, 1):
        coefs[n].wait_recv()
        proj = proj + pgot_ref[n, 0:1, :]
    for c in range(8):
        chunk_ref[c] = pack_chunk(total, proj, c)
    chunks = []
    for step in range(1, 8):
        to = (col + step) % 8
        chunks.append(send(chunk_ref.at[to], chunks_ref.at[step - 1], (row, to), chunk_send, chunk_recv, step - 1))
    whole = chunk_ref[col]
    for n, copy in enumerate(chunks):
        copy.wait_recv()
        whole = whole + chunks_ref[n]
    whole = whole * -0.5
    out_ref[0, :, 0:128] = whole[:N]
    out_ref[0, 0:16, 128:CHUNK] = whole[40:56, 0:34]
    out_ref[0, 16:32, 128:CHUNK] = whole[40:56, 34:68]
    out_ref[0, 32:36, 128:CHUNK] = whole[40:44, 68:102]
    proj_ref[...] = whole[N : N + 1, 0:32]
    for copy in sends + chunks:
        copy.wait_send()


def on_device(bands, projections, qfunc, species, positions, glist):
    vm = pl.BlockSpec(memory_space=pltpu.VMEM)
    hbm = pl.BlockSpec(memory_space=pl.ANY)
    tables = [jnp.asarray(TABLES[name]) for name in TABLE_NAMES]
    dma = pltpu.SemaphoreType.DMA
    return pl.pallas_call(
        kernel,
        out_shape=(jax.ShapeDtypeStruct((1, N, CHUNK), F32), jax.ShapeDtypeStruct((1, 32), F32)),
        in_specs=[vm, vm, hbm, vm, vm, vm] + [hbm] * len(tables),
        out_specs=(vm, vm),
        scratch_shapes=[
            *[pltpu.VMEM(t.shape, t.dtype) for t in tables],
            pltpu.VMEM((4, XB, LANES), BF16),
            pltpu.VMEM((4, 32, TAIL), BF16),
            pltpu.VMEM((2, NSPEC, NH * NH, NLIST), F32),
            pltpu.VMEM((4, LM, NLIST), BF16),
            pltpu.VMEM((LANES, NLIST), BF16),
            pltpu.VMEM((2, ATOMS, NLIST), F32),
            pltpu.VMEM((ATOMS, LM), F32),
            pltpu.VMEM((4, ATOMS, 2 * LM), F32),
            pltpu.VMEM((SLOTS * 2 * KA, LANES), F32),
            pltpu.VMEM((SLOTS * 2 * KA, LANES), F32),
            pltpu.VMEM((2 * NG6 * KR, 2 * LG), F32),
            pltpu.VMEM((4, ATOMS, 2 * LM), F32),
            pltpu.VMEM((4, XO, LANES), F32),
            pltpu.VMEM((3, XO, LANES), F32),
            pltpu.VMEM((3, 8, 256), F32),
            pltpu.VMEM((3, 8, 256), F32),
            pltpu.VMEM((8, 56, 128), F32),
            pltpu.VMEM((7, 56, 128), F32),
            dma((len(tables) + 1,)),
            *[dma((3,)) for unused in range(8)],
            *[dma((7,)) for unused in range(2)],
        ],
        compiler_params=pltpu.CompilerParams(
            collective_id=0, has_side_effects=True, vmem_limit_bytes=48 * 2**20
        ),
    )(bands, projections, qfunc, species.reshape(1, ATOMS), positions, glist.reshape(1, NLIST), *tables)


def solution(mesh):
    return jax.shard_map(
        on_device,
        mesh=mesh,
        in_specs=(P("row", None, None), P("row", None), P(), P(), P(), P()),
        out_specs=(P("row", None, "col"), P("row", "col")),
        check_vma=False,
    )
```

```python
import functools
import math

import jax
import jax.numpy as jnp
import ml_dtypes
import numpy as np
from jax import lax
from jax.experimental import pallas as pl
from jax.experimental.pallas import tpu as pltpu
from jax.sharding import PartitionSpec as P

N = 36
NG6 = 6
LG = 256
LOWL = 128
LANES = NG6 * LG
XB = 48
XO = 40
KL = 24
KR = 40
ATOMS, NH, NSPEC, NLIST = 32, 8, 2, 1024
PK = 80
AUG = N**1.5 / (NH * math.sqrt(ATOMS))
STEPS = 4
TAIL = 384
CHUNK = 162
F32, BF16 = jnp.float32, jnp.bfloat16

OFFSETS = [
    *[[(1, j), (-1, (j + 1) % 4), (3, (j + 2) % 4), (-3, (j + 3) % 4)] for j in range(4)],
    *[[(2, j), (-2, 1 ^ j), (2, 2 ^ j), (-2, 3 ^ j)] for j in range(2)],
    *[[(0, j), (4, 1 ^ j), (0, 2 ^ j), (4, 3 ^ j)] for j in range(2)],
]


def split_np(a):
    hi = a.astype(np.float32).astype(ml_dtypes.bfloat16)
    lo = (a - hi.astype(np.float64)).astype(np.float32).astype(ml_dtypes.bfloat16)
    return hi, lo


def row_of(pair, kx):
    return 11 * pair + kx if kx <= 10 else KL + 8 * pair + kx - 11


def make_tables():
    k = np.arange(19)[:, None]
    x = np.arange(N)[None, :]
    ang = 2 * np.pi * (k * x % N) / N
    weight = np.where((k == 0) | (k == N // 2), 1.0, 2.0) / N**3
    parts = (np.cos(ang), -np.sin(ang))
    bf = ml_dtypes.bfloat16
    fwd = np.zeros((4 * KR, 4 * XB), bf)
    inv = np.zeros((2 * XO, 6 * KR), bf)
    for pair in range(2):
        for c, part in enumerate(parts):
            fh, fl = split_np(part)
            ih, il = split_np(weight * part)
            for kx in range(19):
                r = c * KR + row_of(pair, kx)
                fwd[r, 96 * pair : 96 * pair + N] = fh[kx]
                fwd[r, 96 * pair + XB : 96 * pair + XB + N] = fh[kx]
                fwd[2 * KR + r, 96 * pair : 96 * pair + N] = fl[kx]
                for b, values in enumerate((ih, ih, il)):
                    inv[XO * pair : XO * pair + N, 2 * KR * b + r] = values[kx]
    r_of = np.repeat(np.arange(6), N)
    z_of = np.tile(np.arange(N), 6)
    near = [(s, kz) for s in (0, 1, 4, 5) for kz in (*range(11), *range(26, 36))]
    order = near + [(s, kz) for s in range(6) for kz in range(N) if (s, kz) not in near]
    s_of = np.array([p[0] for p in order])
    k_of = np.array([p[1] for p in order])
    ang = 2 * np.pi * ((6 * r_of[:, None] * s_of[None, :] + z_of[:, None] * k_of[None, :]) % N) / N
    c = np.zeros((LG, LG))
    s = np.zeros((LG, LG))
    c[:216, :216] = np.cos(ang)
    s[:216, :216] = np.sin(ang)

    def stacked(w):
        hi, lo = split_np(w)
        return np.concatenate([hi, hi, lo], axis=0)

    dft = np.stack([stacked(w) for w in (c, c - s, c + s, c.T, (c + s).T, (c - s).T)])
    tw = np.zeros((16, LG), np.float32)
    for q in range(6):
        a = 2 * np.pi * (r_of * q % N) / N
        tw[q, :216] = np.cos(a)
        tw[8 + q, :216] = -np.sin(a)
    signed = lambda v: np.where(v > N // 2, v - N, v)
    kern = np.zeros((NG6 * KR, LG), np.float32)
    for q in range(6):
        for pair in range(2):
            for kx in range(19):
                n2 = kx**2 + signed(q + 6 * s_of) ** 2 + signed(k_of) ** 2
                kern[q * KR + row_of(pair, kx), :216] = np.where(n2 > 0, N**1.5 / 4 / np.maximum(n2, 1), 0)
    packed = [(s, l, m) for s in range(NSPEC) for l in range(NH) for m in range(l, NH)]
    sel = np.zeros((PK, NSPEC * NH * NH), np.float32)
    rep = np.zeros((256, 768), np.float32)
    rsum = np.zeros((256, 256), np.float32)
    weight = np.zeros((NSPEC, LG), np.float32)
    kk = np.arange(256) % NH
    for p, (s, l, m) in enumerate(packed):
        sel[p, s * 64 + l * 8 + m] += 0.5
        sel[p, s * 64 + m * 8 + l] += 0.5
        for b in range(3):
            rep[kk == l, PK * b + p] = 1
            rep[kk == m, LG + PK * b + p] = 1
            weight[s, PK * b + p] = 0.5 if l == m else 1.0
        rep[kk == m, 2 * LG + p] = 1
        rsum[p, kk == l] = 1
        if l != m:
            rep[kk == l, 2 * LG + PK + p] = 1
            rsum[PK + p, kk == m] = 1
    return dict(
        fwd=fwd, inv=inv, dft=dft, tw=tw, kern=kern, sel=sel.astype(bf), rep=rep.astype(bf), rsum=rsum.astype(bf),
        weight=np.concatenate([weight, np.zeros((6, LG), np.float32)]),
    )


TABLES = make_tables()
TABLE_NAMES = ("fwd", "inv", "dft", "tw", "kern", "sel", "rep", "rsum", "weight")


def split(a):
    hi = a.astype(BF16)
    return hi, (a - hi.astype(F32)).astype(BF16)


def mm(a, b):
    return jnp.dot(a, b, preferred_element_type=F32)


def mm_nt(a, b):
    return lax.dot_general(a, b, (((1,), (1,)), ((), ())), preferred_element_type=F32)


def dft3(a, b, c, sign):
    h = math.sqrt(3.0) / 2
    sr, si = b[0] + c[0], b[1] + c[1]
    dr, di = (b[0] - c[0]) * h, (b[1] - c[1]) * h
    tr, ti = a[0] - 0.5 * sr, a[1] - 0.5 * si
    zero = (a[0] + sr, a[1] + si)
    minus = (tr + di, ti - dr)
    plus = (tr - di, ti + dr)
    return (zero, minus, plus) if sign < 0 else (zero, plus, minus)


def dft6(v, sign):
    add = lambda p, q: (p[0] + q[0], p[1] + q[1])
    sub = lambda p, q: (p[0] - q[0], p[1] - q[1])
    e = dft3(add(v[0], v[3]), add(v[1], v[4]), add(v[2], v[5]), sign)
    o = dft3(sub(v[0], v[3]), sub(v[4], v[1]), sub(v[2], v[5]), sign)
    return [e[0], o[2], e[1], o[0], e[2], o[1]]


def mm3(x, w):
    hi, lo = split(x)
    return mm(jnp.concatenate([hi, lo, hi], axis=1), w)


def atom_of_lane():
    lane = lax.broadcasted_iota(jnp.int32, (ATOMS, 256), 1)
    return lane // NH == lax.broadcasted_iota(jnp.int32, (ATOMS, 256), 0)


def setup_lists(glist_ref, positions_ref, species_ref, weight_ref, yzt_ref, phase_ref, choose_ref):
    g = glist_ref[...]
    kx = g // (N * N)
    ky = g // N % N
    kz = g % N
    s = ky // 6
    where = (ky % 6) * LOWL + jnp.where(s < 2, s, s - 2) * 21 + jnp.where(kz <= 10, kz, kz - 15)
    step = 256
    for base in range(0, NG6 * LOWL, step):
        rows = lax.broadcasted_iota(jnp.int32, (step, NLIST), 0) + base
        yzt_ref[base : base + step, :] = jnp.where(rows == where, 1.0, 0.0).astype(BF16)
    sg = lambda v: jnp.where(v > N // 2, v - N, v).astype(F32)
    eye = lax.broadcasted_iota(jnp.int32, (ATOMS, ATOMS), 0) == lax.broadcasted_iota(jnp.int32, (ATOMS, ATOMS), 1)
    column = lambda row: jnp.sum(jnp.where(eye, row, 0.0), axis=1, keepdims=True)
    turns = (
        column(positions_ref[0:1, :]) * kx.astype(F32)
        + column(positions_ref[1:2, :]) * sg(ky)
        + column(positions_ref[2:3, :]) * sg(kz)
    )
    theta = (turns - jnp.floor(turns)) * (2.0 * math.pi)
    phase_ref[0] = jnp.cos(theta)
    phase_ref[1] = -jnp.sin(theta)
    spec = column(species_ref[...].astype(F32))
    choose = jnp.zeros((ATOMS, LG), F32)
    for s in range(NSPEC):
        choose = choose + jnp.where(spec == float(s), 1.0, 0.0) * weight_ref[s : s + 1, :]
    choose_ref[...] = choose


def kx_rows(glist_ref):
    kx = glist_ref[...] // (N * N)
    rows = lax.broadcasted_iota(jnp.int32, (KL, NLIST), 0)
    return rows == kx, rows == kx + 11


def augment(glist_ref, qz_ref, exp_ref, choose_ref, phase_ref, yzt_ref, faug_ref):
    lane = lax.broadcasted_iota(jnp.int32, (ATOMS, LG), 1)
    middle = jnp.logical_and(lane >= PK, lane < 2 * PK)
    mixed = []
    for t in range(STEPS):
        for i in range(2):
            a, b = exp_ref[i], exp_ref[2 + t]
            full = (a[:, :LG] * b[:, LG : 2 * LG] + b[:, :LG] * a[:, LG : 2 * LG]) * choose_ref[...]
            hi = full.astype(BF16).astype(F32)
            mixed.append(jnp.where(middle, full - hi, hi).astype(BF16)[:, : 3 * PK])
    mixed = jnp.concatenate(mixed, axis=0)
    z_re = mm(mixed, qz_ref[:, :NLIST])
    z_im = mm(mixed, qz_ref[:, NLIST:])
    first, second = kx_rows(glist_ref)
    spread = []
    for t in range(STEPS):
        re, im = [], []
        for i in range(2):
            at = (2 * t + i) * ATOMS
            zr, zi = z_re[at : at + ATOMS], z_im[at : at + ATOMS]
            re.append(jnp.sum(phase_ref[0] * zr - phase_ref[1] * zi, axis=0, keepdims=True) * AUG)
            im.append(jnp.sum(phase_ref[0] * zi + phase_ref[1] * zr, axis=0, keepdims=True) * AUG)
        for rows in (re, im):
            spread.append(jnp.where(first, rows[0], jnp.where(second, rows[1], 0.0)))
    hi, lo = split(jnp.concatenate(spread, axis=0))
    both = jnp.concatenate([hi, lo], axis=0)
    for base in range(0, NG6 * LOWL, LG):
        part = mm_nt(both, yzt_ref[base : base + LG, :])
        part = part[:192] + part[192:]
        for t in range(STEPS):
            faug_ref[t, :, base : base + LG] = part[48 * t : 48 * (t + 1)]


def batch(t, band_ref, faug_ref, wst_ref, acc_ref, tabs):
    other = band_ref[2 + t].astype(F32)
    halves = []
    for i in range(2):
        halves += split(band_ref[i].astype(F32) * other)
    out = mm(tabs["fwd"][...], jnp.concatenate(halves, axis=0))
    spec = out[: 2 * KR] + out[2 * KR :]
    v = [(spec[:KR, g * LG : (g + 1) * LG], spec[KR:, g * LG : (g + 1) * LG]) for g in range(NG6)]
    re_rows, im_rows = [], []
    for q, (re, im) in enumerate(dft6(v, -1)):
        if q:
            cr, ci = tabs["tw"][q : q + 1, :], tabs["tw"][8 + q : 9 + q, :]
            re, im = re * cr - im * ci, re * ci + im * cr
        re_rows.append(re)
        im_rows.append(im)
    re, im = jnp.concatenate(re_rows, axis=0), jnp.concatenate(im_rows, axis=0)
    both = mm3(re + im, tabs["dft"][0])
    f = (both - mm3(im, tabs["dft"][1]), both - mm3(re, tabs["dft"][2]))
    w = []
    for c in range(2):
        rows = []
        for q in range(NG6):
            block = f[c][q * KR : (q + 1) * KR]
            kern = tabs["kern"][q * KR : (q + 1) * KR, :]
            low = (block[:KL, :LOWL] + faug_ref[t, c * KL : (c + 1) * KL, q * LOWL : (q + 1) * LOWL]) * kern[:KL, :LOWL]
            wst_ref[t, c * KL : (c + 1) * KL, q * LOWL : (q + 1) * LOWL] = low
            rows.append(jnp.concatenate([low, block[:KL, LOWL:] * kern[:KL, LOWL:]], axis=1))
            rows.append(block[KL:] * kern[KL:])
        w.append(jnp.concatenate(rows, axis=0))
    both = mm3(w[0] + w[1], tabs["dft"][3])
    re, im = both - mm3(w[1], tabs["dft"][4]), both - mm3(w[0], tabs["dft"][5])
    v = []
    for q in range(NG6):
        a, b = re[q * KR : (q + 1) * KR], im[q * KR : (q + 1) * KR]
        if q:
            cr, ci = tabs["tw"][q : q + 1, :], tabs["tw"][8 + q : 9 + q, :]
            a, b = a * cr + b * ci, b * cr - a * ci
        v.append((a, b))
    v = dft6(v, 1)
    w = jnp.concatenate([jnp.concatenate([p[0], p[1]], axis=0) for p in v], axis=1)
    hi, lo = split(w)
    pot = mm(tabs["inv"][...], jnp.concatenate([hi, lo, hi], axis=0))
    acc_ref[0] += pot[:XO] * other[:XO]
    acc_ref[1] += pot[XO:] * other[:XO]


def slopes(glist_ref, qz_ref, exp_ref, choose_ref, phase_ref, yzt_ref, wst_ref):
    hi, lo = split(wst_ref[...].reshape(STEPS * 2 * KL, NG6 * LOWL))
    picked = mm(jnp.concatenate([hi, lo], axis=0), yzt_ref[...])
    picked = picked[:192] + picked[192:]
    first, second = kx_rows(glist_ref)
    cross = []
    for t in range(STEPS):
        for mask in (first, second):
            at = t * 2 * KL
            wr = jnp.sum(jnp.where(mask, picked[at : at + KL], 0.0), axis=0, keepdims=True)
            wi = jnp.sum(jnp.where(mask, picked[at + KL : at + 2 * KL], 0.0), axis=0, keepdims=True)
            re = wr * phase_ref[0] + wi * phase_ref[1]
            im = wi * phase_ref[0] - wr * phase_ref[1]
            cross.append(jnp.concatenate([re, im], axis=1))
    hi, lo = split(jnp.concatenate(cross, axis=0))
    full = mm_nt(jnp.concatenate([hi, lo], axis=0), qz_ref[...])
    high, low = full[:256], full[256:]
    rest = high[:, 2 * PK :]
    slope = (high[:, : 2 * PK] + low[:, : 2 * PK] + jnp.concatenate([rest, rest], axis=1)) * (2.0 * AUG / N**3)
    slope = jnp.concatenate([slope, jnp.zeros((256, LG - 2 * PK), F32)], axis=1)
    chosen = jnp.where(choose_ref[...] > 0.0, 1.0, 0.0)
    sums = []
    for i in range(2):
        total = jnp.zeros((ATOMS, LG), F32)
        for t in range(STEPS):
            at = (2 * t + i) * ATOMS
            total = total + slope[at : at + ATOMS] * exp_ref[2 + t][:, 2 * LG :]
        sums.append(total * chosen)
    return sums


def coef_row(packed, rsum):
    hi, lo = split(packed)
    full = mm(hi, rsum) + mm(lo, rsum)
    return jnp.sum(jnp.where(atom_of_lane(), full, 0.0), axis=0, keepdims=True)


def pack_tail(rows):
    return jnp.concatenate([rows[:, TAIL * j : TAIL * (j + 1)] for j in range(4)], axis=0)


def unpack_tail(tail):
    rows = jnp.concatenate([tail[4 * j : 4 * (j + 1)] for j in range(4)], axis=1)
    return jnp.concatenate([rows, jnp.zeros((12, LANES), F32)], axis=0)


def columns(total, c):
    start = CHUNK * c
    parts = []
    while start < CHUNK * (c + 1):
        g, at = divmod(start, 216)
        end = min(216 * (g + 1), CHUNK * (c + 1))
        parts.append(total[:, g * LG + at : g * LG + at + end - start])
        start = end
    return parts[0] if len(parts) == 1 else jnp.concatenate(parts, axis=1)


def pack_chunk(total, c):
    part = columns(total, c)
    main = part[:, :128]
    rest = part[:, 128:]
    last = jnp.concatenate([rest[32:40], jnp.zeros((8, 34), F32)], axis=0)
    rest = jnp.concatenate([rest[:16], rest[16:32], last, jnp.zeros((16, 26), F32)], axis=1)
    return jnp.concatenate([main, rest], axis=0)


def kernel(*refs):
    nt = len(TABLE_NAMES)
    sources = refs[: 6 + nt]
    out_ref, proj_ref = refs[6 + nt : 8 + nt]
    scratch = refs[8 + nt :]
    bands_ref, coef_ref, q_ref, species_ref, positions_ref, glist_ref = scratch[:6]
    tabs = dict(zip(TABLE_NAMES, scratch[6 : 6 + nt]))
    (band_ref, tail_ref, qz_ref, yzt_ref, phase_ref, choose_ref, exp_ref, faug_ref, wst_ref,
     acc_ref, got_ref, pgive_ref, pgot_ref, chunk_ref, chunks_ref,
     load_sem, tail_send, tail_recv, band_send, band_recv, sum_send, sum_recv, coef_send, coef_recv,
     chunk_send, chunk_recv) = scratch[6 + nt :]
    row, col = lax.axis_index("row"), lax.axis_index("col")
    zed, wide, core = row // 8, row // 2 % 4, row % 2

    def pick(values):
        return sum(jnp.where(col == c, v, 0) for c, v in enumerate(values))

    def at(dz, dy, k):
        return (((zed + dz + 16) % 8 * 4 + (wide + dy + 8) % 4) * 2 + k, col)

    sibling = at(0, 0, 1 - core)
    targets, origins = [], []
    for m in range(4):
        targets.append(at(-pick([o[m][0] for o in OFFSETS]), -pick([o[m][1] for o in OFFSETS]), m % 2))
    for n in range(2):
        dz, dy = (
            pick([o[2 * n][e] for o in OFFSETS]) * (1 - core) + pick([o[2 * n + 1][e] for o in OFFSETS]) * core
            for e in range(2)
        )
        origins += [at(dz, dy, k) for k in range(2)]
    home = jnp.logical_and(col == 6, core == 0)
    away = jnp.logical_not(home)
    peers = [(row, (col + step) % 8) for step in range(1, 8)]
    cousins = [(sibling[0], (col + step) % 8) for step in range(1, 8)]
    mesh_id = pl.DeviceIdType.MESH

    barrier = pltpu.get_barrier_semaphore()

    def greet(partner):
        pl.semaphore_signal(barrier, inc=1, device_id=partner, device_id_type=mesh_id)

    pl.when(away)(lambda: greet(origins[0]))
    others = origins[1:] + [sibling] + peers + cousins
    for partner in others:
        greet(partner)

    loads = [
        pltpu.make_async_copy(src, dst, load_sem.at[n]) for n, (src, dst) in enumerate(zip(sources, scratch[: 6 + nt]))
    ]
    for load in loads:
        load.start()

    def remote(src, dst, to, sems, recvs, n, m=None):
        return pltpu.make_async_remote_copy(
            src_ref=src, dst_ref=dst, send_sem=sems.at[n], recv_sem=recvs.at[n if m is None else m],
            device_id=to, device_id_type=mesh_id,
        )

    loads[0].wait()
    loads[1].wait()
    field = bands_ref[0].astype(F32)
    zero = jnp.zeros((N, LG - 216), F32)
    field = jnp.concatenate(
        [piece for g in range(NG6) for piece in (field[:, 216 * g : 216 * (g + 1)], zero)], axis=1
    )
    band_ref[0, 0:32, :] = field[:32].astype(BF16)
    tail = pack_tail(field[32:36])
    coef_rows = jnp.concatenate([coef_ref[...].astype(F32), jnp.zeros((1, TAIL - 256), F32)], axis=1)
    tail = jnp.concatenate([tail, coef_rows, jnp.zeros((15, TAIL), F32)], axis=0)
    tail_ref[0] = tail.astype(BF16)

    pl.semaphore_wait(barrier, len(others) + 1 - home.astype(jnp.int32))
    tails = [remote(tail_ref.at[0], tail_ref.at[1], sibling, tail_send, tail_recv, 4)]
    fields = [remote(band_ref.at[0, pl.ds(0, 32)], band_ref.at[1, pl.ds(0, 32)], sibling, band_send, band_recv, 4)]
    for m in range(4):
        t = 2 * (m // 2) + core
        tails.append(remote(tail_ref.at[0], tail_ref.at[2 + t], targets[m], tail_send, tail_recv, m, t))
        fields.append(
            remote(
                band_ref.at[0, pl.ds(0, 32)], band_ref.at[2 + t, pl.ds(0, 32)], targets[m], band_send, band_recv, m, t
            )
        )
    for group in (tails, fields):
        for n, copy in enumerate(group):
            if n == 1:
                pl.when(away)(copy.start)
            else:
                copy.start()

    for load in loads[2:]:
        load.wait()
    setup_lists(glist_ref, positions_ref, species_ref, tabs["weight"], yzt_ref, phase_ref, choose_ref)
    acc_ref[...] = jnp.zeros_like(acc_ref)
    for c in range(2):
        hi, lo = split(q_ref[c].reshape(NSPEC * NH * NH, NLIST))
        packed = mm(tabs["sel"][...], hi) + mm(tabs["sel"][...], lo)
        hi, lo = split(packed)
        qz_ref[:, c * NLIST : (c + 1) * NLIST] = jnp.concatenate([hi, hi, lo], axis=0)

    def arrived(which, ref, recvs, n):
        pltpu.make_async_remote_copy(
            src_ref=which, dst_ref=ref, send_sem=recvs.at[n], recv_sem=recvs.at[n], device_id=sibling,
            device_id_type=mesh_id,
        ).wait_recv()

    def home_tail():
        tail_ref[2] = tail_ref[0]

    pl.when(home)(home_tail)
    for b in range(2 + STEPS):
        if b:
            wait = functools.partial(arrived, tail_ref.at[0], tail_ref.at[b], tail_recv, (b + 3) % 5)
            if b == 2:
                pl.when(away)(wait)
            else:
                wait()
        tail = tail_ref[b].astype(F32)
        band_ref[b, 32:48, :] = unpack_tail(tail[:16]).astype(BF16)
        spread = jnp.where(atom_of_lane(), tail[16:17, :256], 0.0).astype(BF16)
        exp_ref[b] = mm(spread, tabs["rep"][...])
    augment(glist_ref, qz_ref, exp_ref, choose_ref, phase_ref, yzt_ref, faug_ref)

    def home_band():
        band_ref[2, 0:32, :] = band_ref[0, 0:32, :]

    pl.when(home)(home_band)
    arrived(band_ref.at[0, pl.ds(0, 32)], band_ref.at[1, pl.ds(0, 32)], band_recv, 4)

    def step(t, carry):
        wait = lambda: arrived(band_ref.at[0, pl.ds(0, 32)], band_ref.at[2 + t, pl.ds(0, 32)], band_recv, t)
        pl.when(jnp.logical_or(away, t > 0))(wait)
        batch(t, band_ref, faug_ref, wst_ref, acc_ref, tabs)
        return carry

    lax.fori_loop(0, STEPS, step, 0)
    give = remote(acc_ref.at[1], got_ref, sibling, sum_send, sum_recv, 0)
    give.start()
    give.wait_recv()
    total = acc_ref[0] + got_ref[...]
    for c in range(8):
        chunk_ref[c] = pack_chunk(total, c)
    chunks = []
    for n, to in enumerate(peers):
        chunks.append(remote(chunk_ref.at[to[1]], chunks_ref.at[n], to, chunk_send, chunk_recv, n))
        chunks[-1].start()
    sums = slopes(glist_ref, qz_ref, exp_ref, choose_ref, phase_ref, yzt_ref, wst_ref)
    rows = [coef_row(packed, tabs["rsum"][...]) for packed in sums]
    for i in range(2):
        pgive_ref[i] = jnp.broadcast_to(rows[i], (8, 256))
    coefs = []
    for n, to in enumerate(peers + [sibling] + cousins):
        coefs.append(remote(pgive_ref.at[0 if n < 7 else 1], pgot_ref.at[n], to, coef_send, coef_recv, n))
        coefs[-1].start()
    whole = chunk_ref[col]
    for n, copy in enumerate(chunks):
        copy.wait_recv()
        whole = whole + chunks_ref[n]
    whole = whole * -0.5
    out_ref[0, :, 0:128] = whole[:N]
    out_ref[0, 0:16, 128:CHUNK] = whole[40:56, 0:34]
    out_ref[0, 16:32, 128:CHUNK] = whole[40:56, 34:68]
    out_ref[0, 32:36, 128:CHUNK] = whole[40:44, 68:102]
    proj = rows[0]
    for n, copy in enumerate(coefs):
        copy.wait_recv()
        proj = proj + pgot_ref[n, 0:1, :]
    proj_ref[...] = -0.5 * sum(jnp.where(col == c, proj[:, 32 * c : 32 * (c + 1)], 0.0) for c in range(8))
    for group in (tails, fields):
        for n, copy in enumerate(group):
            if n == 1:
                pl.when(away)(copy.wait_send)
            else:
                copy.wait_send()
    for copy in [give] + chunks + coefs:
        copy.wait_send()


def on_device(bands, projections, qfunc, species, positions, glist):
    hbm = pl.BlockSpec(memory_space=pltpu.HBM)
    vm = pl.BlockSpec(memory_space=pltpu.VMEM)
    sources = [bands, projections, qfunc, species.reshape(1, ATOMS), positions, glist.reshape(1, NLIST)]
    sources += [jnp.asarray(TABLES[name]) for name in TABLE_NAMES]
    dma = pltpu.SemaphoreType.DMA
    return pl.pallas_call(
        kernel,
        out_shape=(jax.ShapeDtypeStruct((1, N, CHUNK), F32), jax.ShapeDtypeStruct((1, 32), F32)),
        in_specs=[hbm] * len(sources),
        out_specs=(vm, vm),
        scratch_shapes=[
            *[pltpu.VMEM(t.shape, t.dtype) for t in sources],
            pltpu.VMEM((2 + STEPS, XB, LANES), BF16),
            pltpu.VMEM((2 + STEPS, 32, TAIL), BF16),
            pltpu.VMEM((3 * PK, 2 * NLIST), BF16),
            pltpu.VMEM((NG6 * LOWL, NLIST), BF16),
            pltpu.VMEM((2, ATOMS, NLIST), F32),
            pltpu.VMEM((ATOMS, LG), F32),
            pltpu.VMEM((2 + STEPS, ATOMS, 3 * LG), F32),
            pltpu.VMEM((STEPS, 2 * KL, NG6 * LOWL), F32),
            pltpu.VMEM((STEPS, 2 * KL, NG6 * LOWL), F32),
            pltpu.VMEM((2, XO, LANES), F32),
            pltpu.VMEM((XO, LANES), F32),
            pltpu.VMEM((2, 8, 256), F32),
            pltpu.VMEM((15, 8, 256), F32),
            pltpu.VMEM((8, 56, 128), F32),
            pltpu.VMEM((7, 56, 128), F32),
            dma((len(sources),)),
            *[dma((5,)) for unused in range(4)],
            *[dma((1,)) for unused in range(2)],
            *[dma((15,)) for unused in range(2)],
            *[dma((7,)) for unused in range(2)],
        ],
        compiler_params=pltpu.CompilerParams(
            collective_id=0, has_side_effects=True, vmem_limit_bytes=60 * 2**20
        ),
    )(*sources)


def solution(mesh):
    return jax.shard_map(
        on_device,
        mesh=mesh,
        in_specs=(P("row", None, None), P("row", None), P(), P(), P(), P()),
        out_specs=(P("row", None, "col"), P("row", "col")),
        check_vma=False,
    )
```

```python
import functools
import math

import jax
import jax.numpy as jnp
import ml_dtypes
import numpy as np
from jax import lax
from jax.experimental import pallas as pl
from jax.experimental.pallas import tpu as pltpu
from jax.sharding import PartitionSpec as P

N = 36
NG6 = 6
LG = 256
LOWL = 128
LANES = NG6 * LG
XB = 48
XO = 40
KL = 24
KR = 40
ATOMS, NH, NSPEC, NLIST = 32, 8, 2, 1024
PK = 80
AUG = N**1.5 / (NH * math.sqrt(ATOMS))
STEPS = 4
TAIL = 384
CHUNK = 162
F32, BF16 = jnp.float32, jnp.bfloat16

OFFSETS = [
    [(1, -1), (3, 0), (-1, 2), (-3, -1)],
    [(-1, 1), (-3, 0), (1, 2), (3, 1)],
    [(-2, 0), (2, -1), (2, 2), (-2, -1)],
    [(2, 0), (-2, 1), (-2, 2), (2, 1)],
    [(1, 0), (-1, -1), (-3, 2), (3, -1)],
    [(-1, 0), (1, 1), (3, 2), (-3, 1)],
    [(0, 0), (0, -1), (4, 2), (4, -1)],
    [(0, 2), (0, 1), (4, 0), (4, 1)],
]


def make_targets():
    targets = []
    for col in range(8):
        mine = []
        for to in (col, col ^ 1):
            for e, (dz, dy) in enumerate(OFFSETS[to]):
                if (dy == 0) == (to == col):
                    mine.append((e // 2, abs(dz) + (0, 1, 3, 1)[dy % 4], to, e % 2, dz, dy))
        targets.append([(to, n, k, dz, dy) for n, unused, to, k, dz, dy in sorted(mine)])
    return targets


TARGETS = make_targets()


def split_np(a):
    hi = a.astype(np.float32).astype(ml_dtypes.bfloat16)
    lo = (a - hi.astype(np.float64)).astype(np.float32).astype(ml_dtypes.bfloat16)
    return hi, lo


def row_of(pair, kx):
    return 11 * pair + kx if kx <= 10 else KL + 8 * pair + kx - 11


def make_tables():
    k = np.arange(19)[:, None]
    x = np.arange(N)[None, :]
    ang = 2 * np.pi * (k * x % N) / N
    weight = np.where((k == 0) | (k == N // 2), 1.0, 2.0) / N**3
    parts = (np.cos(ang), -np.sin(ang))
    bf = ml_dtypes.bfloat16
    fwd = np.zeros((4 * KR, 4 * XB), bf)
    inv = np.zeros((2 * XO, 6 * KR), bf)
    for pair in range(2):
        for c, part in enumerate(parts):
            fh, fl = split_np(part)
            ih, il = split_np(weight * part)
            for kx in range(19):
                r = c * KR + row_of(pair, kx)
                fwd[r, 96 * pair : 96 * pair + N] = fh[kx]
                fwd[r, 96 * pair + XB : 96 * pair + XB + N] = fh[kx]
                fwd[2 * KR + r, 96 * pair : 96 * pair + N] = fl[kx]
                for b, values in enumerate((ih, ih, il)):
                    inv[XO * pair : XO * pair + N, 2 * KR * b + r] = values[kx]
    r_of = np.repeat(np.arange(6), N)
    z_of = np.tile(np.arange(N), 6)
    near = [(s, kz) for s in (0, 1, 4, 5) for kz in (*range(11), *range(26, 36))]
    order = near + [(s, kz) for s in range(6) for kz in range(N) if (s, kz) not in near]
    s_of = np.array([p[0] for p in order])
    k_of = np.array([p[1] for p in order])
    ang = 2 * np.pi * ((6 * r_of[:, None] * s_of[None, :] + z_of[:, None] * k_of[None, :]) % N) / N
    c = np.zeros((LG, LG))
    s = np.zeros((LG, LG))
    c[:216, :216] = np.cos(ang)
    s[:216, :216] = np.sin(ang)

    def stacked(w):
        hi, lo = split_np(w)
        return np.concatenate([hi, hi, lo], axis=0)

    dft = np.stack([stacked(w) for w in (c, c - s, c + s, c.T, (c + s).T, (c - s).T)])
    tw = np.zeros((16, LG), np.float32)
    for q in range(6):
        a = 2 * np.pi * (r_of * q % N) / N
        tw[q, :216] = np.cos(a)
        tw[8 + q, :216] = -np.sin(a)
    signed = lambda v: np.where(v > N // 2, v - N, v)
    kern = np.zeros((NG6 * KR, LG), np.float32)
    for q in range(6):
        for pair in range(2):
            for kx in range(19):
                n2 = kx**2 + signed(q + 6 * s_of) ** 2 + signed(k_of) ** 2
                kern[q * KR + row_of(pair, kx), :216] = np.where(n2 > 0, N**1.5 / 4 / np.maximum(n2, 1), 0)
    packed = [(s, l, m) for s in range(NSPEC) for l in range(NH) for m in range(l, NH)]
    sel = np.zeros((PK, NSPEC * NH * NH), np.float32)
    rep = np.zeros((NH, 768), np.float32)
    rsum = np.zeros((256, 256), np.float32)
    weight = np.zeros((NSPEC, LG), np.float32)
    kk = np.arange(256) % NH
    k8 = np.arange(NH)
    fold = kk[:, None] == k8[None, :]
    for p, (s, l, m) in enumerate(packed):
        sel[p, s * 64 + l * 8 + m] += 0.5
        sel[p, s * 64 + m * 8 + l] += 0.5
        for b in range(3):
            rep[k8 == l, PK * b + p] = 1
            rep[k8 == m, LG + PK * b + p] = 1
            weight[s, PK * b + p] = 0.5 if l == m else 1.0
        rep[k8 == m, 2 * LG + p] = 1
        rsum[p, kk == l] = 1
        if l != m:
            rep[k8 == l, 2 * LG + PK + p] = 1
            rsum[PK + p, kk == m] = 1
    return dict(
        fwd=fwd, inv=inv, dft=dft, tw=tw, kern=kern, sel=sel.astype(bf), rep=rep.astype(bf), rsum=rsum.astype(bf), fold=fold.astype(bf),
        weight=np.concatenate([weight, np.zeros((6, LG), np.float32)]),
    )


TABLES = make_tables()
TABLE_NAMES = ("fwd", "inv", "dft", "tw", "kern", "sel", "rep", "rsum", "fold", "weight")


def split(a):
    hi = a.astype(BF16)
    return hi, (a - hi.astype(F32)).astype(BF16)


def mm(a, b):
    return jnp.dot(a, b, preferred_element_type=F32)


def mm_nt(a, b):
    return lax.dot_general(a, b, (((1,), (1,)), ((), ())), preferred_element_type=F32)


def dft3(a, b, c, sign):
    h = math.sqrt(3.0) / 2
    sr, si = b[0] + c[0], b[1] + c[1]
    dr, di = (b[0] - c[0]) * h, (b[1] - c[1]) * h
    tr, ti = a[0] - 0.5 * sr, a[1] - 0.5 * si
    zero = (a[0] + sr, a[1] + si)
    minus = (tr + di, ti - dr)
    plus = (tr - di, ti + dr)
    return (zero, minus, plus) if sign < 0 else (zero, plus, minus)


def dft6(v, sign):
    add = lambda p, q: (p[0] + q[0], p[1] + q[1])
    sub = lambda p, q: (p[0] - q[0], p[1] - q[1])
    e = dft3(add(v[0], v[3]), add(v[1], v[4]), add(v[2], v[5]), sign)
    o = dft3(sub(v[0], v[3]), sub(v[4], v[1]), sub(v[2], v[5]), sign)
    return [e[0], o[2], e[1], o[0], e[2], o[1]]


def mm3(x, w):
    hi, lo = split(x)
    return mm(jnp.concatenate([hi, lo, hi], axis=1), w)


def atom_of_lane():
    lane = lax.broadcasted_iota(jnp.int32, (ATOMS, 256), 1)
    return lane // NH == lax.broadcasted_iota(jnp.int32, (ATOMS, 256), 0)


def setup_lists(glist_ref, positions_ref, species_ref, weight_ref, yzt_ref, phase_ref, choose_ref):
    g = glist_ref[...]
    kx = g // (N * N)
    ky = g // N % N
    kz = g % N
    s = ky // 6
    where = (ky % 6) * LOWL + jnp.where(s < 2, s, s - 2) * 21 + jnp.where(kz <= 10, kz, kz - 15)
    step = 256
    for base in range(0, NG6 * LOWL, step):
        rows = lax.broadcasted_iota(jnp.int32, (step, NLIST), 0) + base
        yzt_ref[base : base + step, :] = jnp.where(rows == where, 1.0, 0.0).astype(BF16)
    sg = lambda v: jnp.where(v > N // 2, v - N, v).astype(F32)
    eye = lax.broadcasted_iota(jnp.int32, (ATOMS, ATOMS), 0) == lax.broadcasted_iota(jnp.int32, (ATOMS, ATOMS), 1)
    column = lambda row: jnp.sum(jnp.where(eye, row, 0.0), axis=1, keepdims=True)
    turns = (
        column(positions_ref[0:1, :]) * kx.astype(F32)
        + column(positions_ref[1:2, :]) * sg(ky)
        + column(positions_ref[2:3, :]) * sg(kz)
    )
    theta = (turns - jnp.floor(turns)) * (2.0 * math.pi)
    phase_ref[0] = jnp.cos(theta)
    phase_ref[1] = -jnp.sin(theta)
    spec = column(species_ref[...].astype(F32))
    choose = jnp.zeros((ATOMS, LG), F32)
    for s in range(NSPEC):
        choose = choose + jnp.where(spec == float(s), 1.0, 0.0) * weight_ref[s : s + 1, :]
    choose_ref[...] = choose


def kx_rows(glist_ref):
    kx = glist_ref[...] // (N * N)
    rows = lax.broadcasted_iota(jnp.int32, (KL, NLIST), 0)
    return rows == kx, rows == kx + 11


def augment(n, glist_ref, qz_ref, exp_ref, choose_ref, phase_ref, yzt_ref, faug_ref):
    lane = lax.broadcasted_iota(jnp.int32, (ATOMS, LG), 1)
    middle = jnp.logical_and(lane >= PK, lane < 2 * PK)
    mixed = []
    for t in range(2):
        for i in range(2):
            a, b = exp_ref[i], exp_ref[2 + 2 * n + t]
            full = (a[:, :LG] * b[:, LG : 2 * LG] + b[:, :LG] * a[:, LG : 2 * LG]) * choose_ref[...]
            hi = full.astype(BF16).astype(F32)
            mixed.append(jnp.where(middle, full - hi, hi).astype(BF16)[:, : 3 * PK])
    mixed = jnp.concatenate(mixed, axis=0)
    z_re = mm(mixed, qz_ref[:, :NLIST])
    z_im = mm(mixed, qz_ref[:, NLIST:])
    first, second = kx_rows(glist_ref)
    spread = []
    for t in range(2):
        re, im = [], []
        for i in range(2):
            at = (2 * t + i) * ATOMS
            zr, zi = z_re[at : at + ATOMS], z_im[at : at + ATOMS]
            re.append(jnp.sum(phase_ref[0] * zr - phase_ref[1] * zi, axis=0, keepdims=True) * AUG)
            im.append(jnp.sum(phase_ref[0] * zi + phase_ref[1] * zr, axis=0, keepdims=True) * AUG)
        for rows in (re, im):
            spread.append(jnp.where(first, rows[0], jnp.where(second, rows[1], 0.0)))
    hi, lo = split(jnp.concatenate(spread, axis=0))
    both = jnp.concatenate([hi, lo], axis=0)
    for base in range(0, NG6 * LOWL, LG):
        part = mm_nt(both, yzt_ref[base : base + LG, :])
        part = part[:96] + part[96:]
        for t in range(2):
            faug_ref[2 * n + t, :, base : base + LG] = part[48 * t : 48 * (t + 1)]


def batch(t, band_ref, faug_ref, wst_ref, acc_ref, tabs):
    other = band_ref[2 + t].astype(F32)
    halves = []
    for i in range(2):
        halves += split(band_ref[i].astype(F32) * other)
    out = mm(tabs["fwd"][...], jnp.concatenate(halves, axis=0))
    spec = out[: 2 * KR] + out[2 * KR :]
    v = [(spec[:KR, g * LG : (g + 1) * LG], spec[KR:, g * LG : (g + 1) * LG]) for g in range(NG6)]
    re_rows, im_rows = [], []
    for q, (re, im) in enumerate(dft6(v, -1)):
        if q:
            cr, ci = tabs["tw"][q : q + 1, :], tabs["tw"][8 + q : 9 + q, :]
            re, im = re * cr - im * ci, re * ci + im * cr
        re_rows.append(re)
        im_rows.append(im)
    re, im = jnp.concatenate(re_rows, axis=0), jnp.concatenate(im_rows, axis=0)
    both = mm3(re + im, tabs["dft"][0])
    f = (both - mm3(im, tabs["dft"][1]), both - mm3(re, tabs["dft"][2]))
    w = []
    for c in range(2):
        rows = []
        for q in range(NG6):
            block = f[c][q * KR : (q + 1) * KR]
            kern = tabs["kern"][q * KR : (q + 1) * KR, :]
            low = (block[:KL, :LOWL] + faug_ref[t, c * KL : (c + 1) * KL, q * LOWL : (q + 1) * LOWL]) * kern[:KL, :LOWL]
            wst_ref[t, c * KL : (c + 1) * KL, q * LOWL : (q + 1) * LOWL] = low
            rows.append(jnp.concatenate([low, block[:KL, LOWL:] * kern[:KL, LOWL:]], axis=1))
            rows.append(block[KL:] * kern[KL:])
        w.append(jnp.concatenate(rows, axis=0))
    both = mm3(w[0] + w[1], tabs["dft"][3])
    re, im = both - mm3(w[1], tabs["dft"][4]), both - mm3(w[0], tabs["dft"][5])
    v = []
    for q in range(NG6):
        a, b = re[q * KR : (q + 1) * KR], im[q * KR : (q + 1) * KR]
        if q:
            cr, ci = tabs["tw"][q : q + 1, :], tabs["tw"][8 + q : 9 + q, :]
            a, b = a * cr + b * ci, b * cr - a * ci
        v.append((a, b))
    v = dft6(v, 1)
    w = jnp.concatenate([jnp.concatenate([p[0], p[1]], axis=0) for p in v], axis=1)
    hi, lo = split(w)
    pot = mm(tabs["inv"][...], jnp.concatenate([hi, lo, hi], axis=0))
    acc_ref[0] += pot[:XO] * other[:XO]
    acc_ref[1] += pot[XO:] * other[:XO]


def slopes(n, glist_ref, qz_ref, exp_ref, choose_ref, phase_ref, yzt_ref, wst_ref):
    hi, lo = split(wst_ref[2 * n : 2 * n + 2].reshape(4 * KL, NG6 * LOWL))
    picked = mm(jnp.concatenate([hi, lo], axis=0), yzt_ref[...])
    picked = picked[:96] + picked[96:]
    first, second = kx_rows(glist_ref)
    cross = []
    for t in range(2):
        for mask in (first, second):
            at = t * 2 * KL
            wr = jnp.sum(jnp.where(mask, picked[at : at + KL], 0.0), axis=0, keepdims=True)
            wi = jnp.sum(jnp.where(mask, picked[at + KL : at + 2 * KL], 0.0), axis=0, keepdims=True)
            re = wr * phase_ref[0] + wi * phase_ref[1]
            im = wi * phase_ref[0] - wr * phase_ref[1]
            cross.append(jnp.concatenate([re, im], axis=1))
    hi, lo = split(jnp.concatenate(cross, axis=0))
    full = mm_nt(jnp.concatenate([hi, lo], axis=0), qz_ref[...])
    high, low = full[:128], full[128:]
    rest = high[:, 2 * PK :]
    slope = (high[:, : 2 * PK] + low[:, : 2 * PK] + jnp.concatenate([rest, rest], axis=1)) * (2.0 * AUG / N**3)
    slope = jnp.concatenate([slope, jnp.zeros((128, LG - 2 * PK), F32)], axis=1)
    chosen = jnp.where(choose_ref[...] > 0.0, 1.0, 0.0)
    sums = []
    for i in range(2):
        total = jnp.zeros((ATOMS, LG), F32)
        for t in range(2):
            at = (2 * t + i) * ATOMS
            total = total + slope[at : at + ATOMS] * exp_ref[2 + 2 * n + t][:, 2 * LG :]
        sums.append(total * chosen)
    return sums


def coef_row(packed, rsum):
    hi, lo = split(packed)
    full = mm(hi, rsum) + mm(lo, rsum)
    return jnp.sum(jnp.where(atom_of_lane(), full, 0.0), axis=0, keepdims=True)


def pack_tail(rows, coefs):
    rows = jnp.concatenate([rows[:, 324 * j : 324 * (j + 1)] for j in range(4)], axis=0)
    return jnp.concatenate([rows, coefs[:16], coefs[16:], jnp.zeros((16, TAIL - 340), F32)], axis=1)


def tail_coefs(tail):
    return jnp.concatenate([tail[:, 324:332], tail[:, 332:340]], axis=0)


def spread_band(main, tail):
    rows = jnp.concatenate([tail[4 * j : 4 * (j + 1), :324] for j in range(4)], axis=1)
    full = jnp.concatenate([main, rows, jnp.zeros((12, 1296), F32)], axis=0)
    zero = jnp.zeros((XB, LG - 216), F32)
    return jnp.concatenate([p for g in range(NG6) for p in (full[:, 216 * g : 216 * (g + 1)], zero)], axis=1)


def columns(total, c):
    start = CHUNK * c
    parts = []
    while start < CHUNK * (c + 1):
        g, at = divmod(start, 216)
        end = min(216 * (g + 1), CHUNK * (c + 1))
        parts.append(total[:, g * LG + at : g * LG + at + end - start])
        start = end
    return parts[0] if len(parts) == 1 else jnp.concatenate(parts, axis=1)


def pack_chunk(total, c):
    part = columns(total, c)
    main = part[:, :128]
    rest = part[:, 128:]
    last = jnp.concatenate([rest[32:40], jnp.zeros((8, 34), F32)], axis=0)
    rest = jnp.concatenate([rest[:16], rest[16:32], last, jnp.zeros((16, 26), F32)], axis=1)
    return jnp.concatenate([main, rest], axis=0)


def kernel(*refs):
    nt = len(TABLE_NAMES)
    sources = refs[: 6 + nt]
    out_ref, proj_ref = refs[6 + nt : 8 + nt]
    scratch = refs[8 + nt :]
    bands_ref, coef_ref, q_ref, species_ref, positions_ref, glist_ref = scratch[:6]
    tabs = dict(zip(TABLE_NAMES, scratch[6 : 6 + nt]))
    (band_ref, raw_ref, tail_ref, qz_ref, yzt_ref, phase_ref, choose_ref, exp_ref, faug_ref, wst_ref,
     acc_ref, got_ref, pgive_ref, pgot_ref, chunk_ref, chunks_ref,
     load_sem, tail_send, tail_recv, band_send, band_recv, sum_send, sum_recv, coef_send, coef_recv,
     chunk_send, chunk_recv) = scratch[6 + nt :]
    row, col = lax.axis_index("row"), lax.axis_index("col")
    zed, wide, core = row // 8, row // 2 % 4, row % 2

    def pick(values):
        return sum(jnp.where(col == c, v, 0) for c, v in enumerate(values))

    def at(dz, dy, k, c):
        return (((zed + dz + 16) % 8 * 4 + (wide + dy + 8) % 4) * 2 + k, c)

    sibling = at(0, 0, 1 - core, col)
    targets, origins = [], []
    for m in range(4):
        to, n, k, dz, dy = (pick([entries[m][e] for entries in TARGETS]) for e in range(5))
        targets.append((at(-dz, -dy, k, to), 2 * n + core))
    for n in range(2):
        dz, dy, other = (
            pick([e[2 * n][0] for e in OFFSETS]) * (1 - core) + pick([e[2 * n + 1][0] for e in OFFSETS]) * core,
            pick([e[2 * n][1] for e in OFFSETS]) * (1 - core) + pick([e[2 * n + 1][1] for e in OFFSETS]) * core,
            pick([int(e[2 * n][1] != 0) for e in OFFSETS]) * (1 - core)
            + pick([int(e[2 * n + 1][1] != 0) for e in OFFSETS]) * core,
        )
        origins += [at(dz, dy, k, col + other * (1 - 2 * (col % 2))) for k in range(2)]
    home = jnp.logical_and(col == 6, core == 0)
    away = jnp.logical_not(home)
    peers = [(row, (col + step) % 8) for step in range(1, 8)]
    cousins = [(sibling[0], (col + step) % 8) for step in range(1, 8)]
    mesh_id = pl.DeviceIdType.MESH

    barrier = pltpu.get_barrier_semaphore()

    def greet(partner):
        pl.semaphore_signal(barrier, inc=1, device_id=partner, device_id_type=mesh_id)

    pl.when(away)(lambda: greet(origins[0]))
    others = origins[1:] + [sibling] + peers + cousins
    for partner in others:
        greet(partner)

    names = ("bands", "projections", "qfunc", "species", "positions", "glist", *TABLE_NAMES)
    loads = [
        pltpu.make_async_copy(src, dst, load_sem.at[n]) for n, (src, dst) in enumerate(zip(sources, scratch[: 6 + nt]))
    ]
    for load in loads:
        load.start()

    def remote(src, dst, to, sems, recvs, n, m=None):
        return pltpu.make_async_remote_copy(
            src_ref=src, dst_ref=dst, send_sem=sems.at[n], recv_sem=recvs.at[n if m is None else m],
            device_id=to, device_id_type=mesh_id,
        )

    loads[0].wait()
    loads[1].wait()
    loads[names.index("fold")].wait()
    own = jnp.where(atom_of_lane(), coef_ref[...].astype(F32), 0.0).astype(BF16)
    tail_ref[0] = pack_tail(bands_ref[0].astype(F32)[32:36], mm(own, tabs["fold"][...])).astype(BF16)
    main = bands_ref.at[0, pl.ds(0, 32)]

    pl.semaphore_wait(barrier, len(others) + 1 - home.astype(jnp.int32))
    tails = [remote(tail_ref.at[0], tail_ref.at[1], sibling, tail_send, tail_recv, 4)]
    fields = [remote(main, raw_ref.at[1], sibling, band_send, band_recv, 4)]
    for m, (to, t) in enumerate(targets):
        tails.append(remote(tail_ref.at[0], tail_ref.at[2 + t], to, tail_send, tail_recv, m, t))
        fields.append(remote(main, raw_ref.at[2 + t], to, band_send, band_recv, m, t))

    def each(group, numbers, act):
        for n in numbers:
            if n == 1:
                pl.when(away)(lambda: act(group[n]))
            else:
                act(group[n])

    for numbers in ((0, 1, 2), (3, 4)):
        for group in (tails, fields):
            each(group, numbers, lambda copy: copy.start())

    for n, load in enumerate(loads):
        if n > 1 and names[n] != "fold":
            load.wait()
    setup_lists(glist_ref, positions_ref, species_ref, tabs["weight"], yzt_ref, phase_ref, choose_ref)
    acc_ref[...] = jnp.zeros_like(acc_ref)
    for c in range(2):
        hi, lo = split(q_ref[c].reshape(NSPEC * NH * NH, NLIST))
        packed = mm(tabs["sel"][...], hi) + mm(tabs["sel"][...], lo)
        hi, lo = split(packed)
        qz_ref[:, c * NLIST : (c + 1) * NLIST] = jnp.concatenate([hi, hi, lo], axis=0)

    def arrived(which, ref, recvs, n):
        pltpu.make_async_remote_copy(
            src_ref=which, dst_ref=ref, send_sem=recvs.at[n], recv_sem=recvs.at[n], device_id=sibling,
            device_id_type=mesh_id,
        ).wait_recv()

    def unpack(b):
        band_ref[b] = spread_band(raw_ref[b].astype(F32), tail_ref[b].astype(F32)).astype(BF16)

    def expand(b):
        exp_ref[b] = mm(tail_coefs(tail_ref[b].astype(F32)).astype(BF16), tabs["rep"][...])

    def copy_home():
        tail_ref[2] = tail_ref[0]
        raw_ref[2] = bands_ref[0, 0:32, :]

    pl.when(home)(copy_home)
    raw_ref[0] = bands_ref[0, 0:32, :]
    unpack(0)
    expand(0)
    arrived(tail_ref.at[0], tail_ref.at[1], tail_recv, 4)
    expand(1)
    arrived(main, raw_ref.at[1], band_recv, 4)
    unpack(1)

    def step(t, carry):
        pl.when(jnp.logical_or(away, t > 0))(lambda: arrived(main, raw_ref.at[2 + t], band_recv, t))
        unpack(2 + t)
        batch(t, band_ref, faug_ref, wst_ref, acc_ref, tabs)
        return carry

    sums = []
    for n in range(2):
        for t in (2 * n, 2 * n + 1):
            wait = functools.partial(arrived, tail_ref.at[0], tail_ref.at[2 + t], tail_recv, t)
            if t == 0:
                pl.when(away)(wait)
            else:
                wait()
            expand(2 + t)
        augment(n, glist_ref, qz_ref, exp_ref, choose_ref, phase_ref, yzt_ref, faug_ref)
        lax.fori_loop(2 * n, 2 * n + 2, step, 0)
        if n == 0:
            sums.append(slopes(n, glist_ref, qz_ref, exp_ref, choose_ref, phase_ref, yzt_ref, wst_ref))
    give = remote(acc_ref.at[1], got_ref, sibling, sum_send, sum_recv, 0)
    give.start()
    give.wait_recv()
    total = acc_ref[0] + got_ref[...]
    for c in range(8):
        chunk_ref[c] = pack_chunk(total, c)
    chunks = []
    for n, to in enumerate(peers):
        chunks.append(remote(chunk_ref.at[to[1]], chunks_ref.at[n], to, chunk_send, chunk_recv, n))
        chunks[-1].start()
    sums.append(slopes(1, glist_ref, qz_ref, exp_ref, choose_ref, phase_ref, yzt_ref, wst_ref))
    rows = [coef_row(sums[0][i] + sums[1][i], tabs["rsum"][...]) for i in range(2)]
    for i in range(2):
        pgive_ref[i] = jnp.broadcast_to(rows[i], (8, 256))
    coefs = []
    for n, to in enumerate(peers + [sibling] + cousins):
        coefs.append(remote(pgive_ref.at[0 if n < 7 else 1], pgot_ref.at[n], to, coef_send, coef_recv, n))
        coefs[-1].start()
    whole = chunk_ref[col]
    for n, copy in enumerate(chunks):
        copy.wait_recv()
        whole = whole + chunks_ref[n]
    whole = whole * -0.5
    out_ref[:, 0, 0:128] = whole[:N]
    out_ref[0:16, 0, 128:CHUNK] = whole[40:56, 0:34]
    out_ref[16:32, 0, 128:CHUNK] = whole[40:56, 34:68]
    out_ref[32:36, 0, 128:CHUNK] = whole[40:44, 68:102]
    proj = rows[0]
    for n, copy in enumerate(coefs):
        copy.wait_recv()
        proj = proj + pgot_ref[n, 0:1, :]
    proj_ref[...] = -0.5 * sum(jnp.where(col == c, proj[:, 32 * c : 32 * (c + 1)], 0.0) for c in range(8))
    for group in (tails, fields):
        each(group, range(5), lambda copy: copy.wait_send())
    for copy in [give] + chunks + coefs:
        copy.wait_send()


def on_device(bands, projections, qfunc, species, positions, glist):
    hbm = pl.BlockSpec(memory_space=pltpu.HBM)
    vm = pl.BlockSpec(memory_space=pltpu.VMEM)
    sources = [bands, projections, qfunc, species.reshape(1, ATOMS), positions, glist.reshape(1, NLIST)]
    sources += [jnp.asarray(TABLES[name]) for name in TABLE_NAMES]
    dma = pltpu.SemaphoreType.DMA
    grid, proj = pl.pallas_call(
        kernel,
        out_shape=(jax.ShapeDtypeStruct((N, 1, CHUNK), F32), jax.ShapeDtypeStruct((1, 32), F32)),
        in_specs=[hbm] * len(sources),
        out_specs=(vm, vm),
        scratch_shapes=[
            *[pltpu.VMEM(t.shape, t.dtype) for t in sources],
            pltpu.VMEM((2 + STEPS, XB, LANES), BF16),
            pltpu.VMEM((2 + STEPS, 32, 1296), BF16),
            pltpu.VMEM((2 + STEPS, 16, TAIL), BF16),
            pltpu.VMEM((3 * PK, 2 * NLIST), BF16),
            pltpu.VMEM((NG6 * LOWL, NLIST), BF16),
            pltpu.VMEM((2, ATOMS, NLIST), F32),
            pltpu.VMEM((ATOMS, LG), F32),
            pltpu.VMEM((2 + STEPS, ATOMS, 3 * LG), F32),
            pltpu.VMEM((STEPS, 2 * KL, NG6 * LOWL), F32),
            pltpu.VMEM((STEPS, 2 * KL, NG6 * LOWL), F32),
            pltpu.VMEM((2, XO, LANES), F32),
            pltpu.VMEM((XO, LANES), F32),
            pltpu.VMEM((2, 8, 256), F32),
            pltpu.VMEM((15, 8, 256), F32),
            pltpu.VMEM((8, 56, 128), F32),
            pltpu.VMEM((7, 56, 128), F32),
            dma((len(sources),)),
            *[dma((5,)) for unused in range(4)],
            *[dma((1,)) for unused in range(2)],
            *[dma((15,)) for unused in range(2)],
            *[dma((7,)) for unused in range(2)],
        ],
        compiler_params=pltpu.CompilerParams(
            collective_id=0, has_side_effects=True, vmem_limit_bytes=60 * 2**20
        ),
    )(*sources)
    return (jnp.swapaxes(grid, 0, 1), proj)


def solution(mesh):
    return jax.shard_map(
        on_device,
        mesh=mesh,
        in_specs=(P("row", None, None), P("row", None), P(), P(), P(), P()),
        out_specs=(P("row", None, "col"), P("row", "col")),
        check_vma=False,
    )
```

```python
import functools
import math

import jax
import jax.numpy as jnp
import ml_dtypes
import numpy as np
from jax import lax
from jax.experimental import pallas as pl
from jax.experimental.pallas import tpu as pltpu
from jax.sharding import PartitionSpec as P

N = 36
NG6 = 6
LG = 256
LOWL = 128
LANES = NG6 * LG
XB = 48
XO = 40
KL = 24
KR = 40
ATOMS, NH, NSPEC, NLIST = 32, 8, 2, 1024
PK = 80
AUG = N**1.5 / (NH * math.sqrt(ATOMS))
STEPS = 4
TAIL = 384
CHUNK = 162
F32, BF16 = jnp.float32, jnp.bfloat16

OFFSETS = [
    [(1, -1), (3, 0), (-1, 2), (-3, -1)],
    [(-1, 1), (-3, 0), (1, 2), (3, 1)],
    [(-2, 0), (2, -1), (2, 2), (-2, -1)],
    [(2, 0), (-2, 1), (-2, 2), (2, 1)],
    [(1, 0), (-1, -1), (-3, 2), (3, -1)],
    [(-1, 0), (1, 1), (3, 2), (-3, 1)],
    [(0, 0), (0, -1), (4, 2), (4, -1)],
    [(0, 2), (0, 1), (4, 0), (4, 1)],
]


def make_targets():
    targets = []
    for col in range(8):
        mine = []
        for to in (col, col ^ 1):
            for e, (dz, dy) in enumerate(OFFSETS[to]):
                if (dy == 0) == (to == col):
                    mine.append((e // 2, abs(dz) + (0, 1, 3, 1)[dy % 4], to, e % 2, dz, dy))
        targets.append([(to, n, k, dz, dy) for n, unused, to, k, dz, dy in sorted(mine)])
    return targets


TARGETS = make_targets()


def split_np(a):
    hi = a.astype(np.float32).astype(ml_dtypes.bfloat16)
    lo = (a - hi.astype(np.float64)).astype(np.float32).astype(ml_dtypes.bfloat16)
    return hi, lo


def row_of(pair, kx):
    return 11 * pair + kx if kx <= 10 else KL + 8 * pair + kx - 11


def make_tables():
    k = np.arange(19)[:, None]
    x = np.arange(N)[None, :]
    ang = 2 * np.pi * (k * x % N) / N
    weight = np.where((k == 0) | (k == N // 2), 1.0, 2.0) / N**3
    parts = (np.cos(ang), -np.sin(ang))
    bf = ml_dtypes.bfloat16
    fwd = np.zeros((4 * KR, 4 * XB), bf)
    inv = np.zeros((2 * XO, 6 * KR), bf)
    for pair in range(2):
        for c, part in enumerate(parts):
            fh, fl = split_np(part)
            ih, il = split_np(weight * part)
            for kx in range(19):
                r = c * KR + row_of(pair, kx)
                fwd[r, 96 * pair : 96 * pair + N] = fh[kx]
                fwd[r, 96 * pair + XB : 96 * pair + XB + N] = fh[kx]
                fwd[2 * KR + r, 96 * pair : 96 * pair + N] = fl[kx]
                for b, values in enumerate((ih, ih, il)):
                    inv[XO * pair : XO * pair + N, 2 * KR * b + r] = values[kx]
    r_of = np.repeat(np.arange(6), N)
    z_of = np.tile(np.arange(N), 6)
    near = [(s, kz) for s in (0, 1, 4, 5) for kz in (*range(11), *range(26, 36))]
    order = near + [(s, kz) for s in range(6) for kz in range(N) if (s, kz) not in near]
    s_of = np.array([p[0] for p in order])
    k_of = np.array([p[1] for p in order])
    ang = 2 * np.pi * ((6 * r_of[:, None] * s_of[None, :] + z_of[:, None] * k_of[None, :]) % N) / N
    c = np.zeros((LG, LG))
    s = np.zeros((LG, LG))
    c[:216, :216] = np.cos(ang)
    s[:216, :216] = np.sin(ang)

    def stacked(w):
        hi, lo = split_np(w)
        return np.concatenate([hi, hi, lo], axis=0)

    dft = np.stack([stacked(w) for w in (c, c - s, c + s, c.T, (c + s).T, (c - s).T)])
    tw = np.zeros((16, LG), np.float32)
    for q in range(6):
        a = 2 * np.pi * (r_of * q % N) / N
        tw[q, :216] = np.cos(a)
        tw[8 + q, :216] = -np.sin(a)
    signed = lambda v: np.where(v > N // 2, v - N, v)
    kern = np.zeros((NG6 * KR, LG), np.float32)
    for q in range(6):
        for pair in range(2):
            for kx in range(19):
                n2 = kx**2 + signed(q + 6 * s_of) ** 2 + signed(k_of) ** 2
                kern[q * KR + row_of(pair, kx), :216] = np.where(n2 > 0, N**1.5 / 4 / np.maximum(n2, 1), 0)
    packed = [(s, l, m) for s in range(NSPEC) for l in range(NH) for m in range(l, NH)]
    sel = np.zeros((PK, NSPEC * NH * NH), np.float32)
    rep = np.zeros((NH, 768), np.float32)
    rsum = np.zeros((256, 256), np.float32)
    weight = np.zeros((NSPEC, LG), np.float32)
    kk = np.arange(256) % NH
    k8 = np.arange(NH)
    fold = kk[:, None] == k8[None, :]
    for p, (s, l, m) in enumerate(packed):
        sel[p, s * 64 + l * 8 + m] += 0.5
        sel[p, s * 64 + m * 8 + l] += 0.5
        for b in range(3):
            rep[k8 == l, PK * b + p] = 1
            rep[k8 == m, LG + PK * b + p] = 1
            weight[s, PK * b + p] = 0.5 if l == m else 1.0
        rep[k8 == m, 2 * LG + p] = 1
        rsum[p, kk == l] = 1
        if l != m:
            rep[k8 == l, 2 * LG + PK + p] = 1
            rsum[PK + p, kk == m] = 1
    return dict(
        fwd=fwd, inv=inv, dft=dft, tw=tw, kern=kern, sel=sel.astype(bf), rep=rep.astype(bf), rsum=rsum.astype(bf), fold=fold.astype(bf),
        weight=np.concatenate([weight, np.zeros((6, LG), np.float32)]),
    )


TABLES = make_tables()
TABLE_NAMES = ("fwd", "inv", "dft", "tw", "kern", "sel", "rep", "rsum", "fold", "weight")


def split(a):
    hi = a.astype(BF16)
    return hi, (a - hi.astype(F32)).astype(BF16)


def mm(a, b):
    return jnp.dot(a, b, preferred_element_type=F32)


def mm_nt(a, b):
    return lax.dot_general(a, b, (((1,), (1,)), ((), ())), preferred_element_type=F32)


def dft3(a, b, c, sign):
    h = math.sqrt(3.0) / 2
    sr, si = b[0] + c[0], b[1] + c[1]
    dr, di = (b[0] - c[0]) * h, (b[1] - c[1]) * h
    tr, ti = a[0] - 0.5 * sr, a[1] - 0.5 * si
    zero = (a[0] + sr, a[1] + si)
    minus = (tr + di, ti - dr)
    plus = (tr - di, ti + dr)
    return (zero, minus, plus) if sign < 0 else (zero, plus, minus)


def dft6(v, sign):
    add = lambda p, q: (p[0] + q[0], p[1] + q[1])
    sub = lambda p, q: (p[0] - q[0], p[1] - q[1])
    e = dft3(add(v[0], v[3]), add(v[1], v[4]), add(v[2], v[5]), sign)
    o = dft3(sub(v[0], v[3]), sub(v[4], v[1]), sub(v[2], v[5]), sign)
    return [e[0], o[2], e[1], o[0], e[2], o[1]]


def mm3(x, w):
    hi, lo = split(x)
    return mm(jnp.concatenate([hi, lo, hi], axis=1), w)


def atom_of_lane():
    lane = lax.broadcasted_iota(jnp.int32, (ATOMS, 256), 1)
    return lane // NH == lax.broadcasted_iota(jnp.int32, (ATOMS, 256), 0)


def setup_lists(glist_ref, positions_ref, species_ref, weight_ref, yzt_ref, phase_ref, choose_ref):
    g = glist_ref[...]
    kx = g // (N * N)
    ky = g // N % N
    kz = g % N
    s = ky // 6
    where = (ky % 6) * LOWL + jnp.where(s < 2, s, s - 2) * 21 + jnp.where(kz <= 10, kz, kz - 15)
    step = 256
    for base in range(0, NG6 * LOWL, step):
        rows = lax.broadcasted_iota(jnp.int32, (step, NLIST), 0) + base
        yzt_ref[base : base + step, :] = jnp.where(rows == where, 1.0, 0.0).astype(BF16)
    sg = lambda v: jnp.where(v > N // 2, v - N, v).astype(F32)
    eye = lax.broadcasted_iota(jnp.int32, (ATOMS, ATOMS), 0) == lax.broadcasted_iota(jnp.int32, (ATOMS, ATOMS), 1)
    column = lambda row: jnp.sum(jnp.where(eye, row, 0.0), axis=1, keepdims=True)
    turns = (
        column(positions_ref[0:1, :]) * kx.astype(F32)
        + column(positions_ref[1:2, :]) * sg(ky)
        + column(positions_ref[2:3, :]) * sg(kz)
    )
    theta = (turns - jnp.floor(turns)) * (2.0 * math.pi)
    phase_ref[0] = jnp.cos(theta)
    phase_ref[1] = -jnp.sin(theta)
    spec = column(species_ref[...].astype(F32))
    choose = jnp.zeros((ATOMS, LG), F32)
    for s in range(NSPEC):
        choose = choose + jnp.where(spec == float(s), 1.0, 0.0) * weight_ref[s : s + 1, :]
    choose_ref[...] = choose


def kx_rows(glist_ref):
    kx = glist_ref[...] // (N * N)
    rows = lax.broadcasted_iota(jnp.int32, (KL, NLIST), 0)
    return rows == kx, rows == kx + 11


def augment(n, glist_ref, qz_ref, exp_ref, choose_ref, phase_ref, yzt_ref, faug_ref):
    lane = lax.broadcasted_iota(jnp.int32, (ATOMS, LG), 1)
    middle = jnp.logical_and(lane >= PK, lane < 2 * PK)
    mixed = []
    for t in range(2):
        for i in range(2):
            a, b = exp_ref[i], exp_ref[2 + 2 * n + t]
            full = (a[:, :LG] * b[:, LG : 2 * LG] + b[:, :LG] * a[:, LG : 2 * LG]) * choose_ref[...]
            hi = full.astype(BF16).astype(F32)
            mixed.append(jnp.where(middle, full - hi, hi).astype(BF16)[:, : 3 * PK])
    mixed = jnp.concatenate(mixed, axis=0)
    z_re = mm(mixed, qz_ref[:, :NLIST])
    z_im = mm(mixed, qz_ref[:, NLIST:])
    first, second = kx_rows(glist_ref)
    spread = []
    for t in range(2):
        re, im = [], []
        for i in range(2):
            at = (2 * t + i) * ATOMS
            zr, zi = z_re[at : at + ATOMS], z_im[at : at + ATOMS]
            re.append(jnp.sum(phase_ref[0] * zr - phase_ref[1] * zi, axis=0, keepdims=True) * AUG)
            im.append(jnp.sum(phase_ref[0] * zi + phase_ref[1] * zr, axis=0, keepdims=True) * AUG)
        for rows in (re, im):
            spread.append(jnp.where(first, rows[0], jnp.where(second, rows[1], 0.0)))
    hi, lo = split(jnp.concatenate(spread, axis=0))
    both = jnp.concatenate([hi, lo], axis=0)
    for base in range(0, NG6 * LOWL, LG):
        part = mm_nt(both, yzt_ref[base : base + LG, :])
        part = part[:96] + part[96:]
        for t in range(2):
            faug_ref[2 * n + t, :, base : base + LG] = part[48 * t : 48 * (t + 1)]


def batch(t, band_ref, faug_ref, wst_ref, acc_ref, tabs):
    other = band_ref[2 + t].astype(F32)
    halves = []
    for i in range(2):
        halves += split(band_ref[i].astype(F32) * other)
    out = mm(tabs["fwd"][...], jnp.concatenate(halves, axis=0))
    spec = out[: 2 * KR] + out[2 * KR :]
    v = [(spec[:KR, g * LG : (g + 1) * LG], spec[KR:, g * LG : (g + 1) * LG]) for g in range(NG6)]
    re_rows, im_rows = [], []
    for q, (re, im) in enumerate(dft6(v, -1)):
        if q:
            cr, ci = tabs["tw"][q : q + 1, :], tabs["tw"][8 + q : 9 + q, :]
            re, im = re * cr - im * ci, re * ci + im * cr
        re_rows.append(re)
        im_rows.append(im)
    re, im = jnp.concatenate(re_rows, axis=0), jnp.concatenate(im_rows, axis=0)
    both = mm3(re + im, tabs["dft"][0])
    f = (both - mm3(im, tabs["dft"][1]), both - mm3(re, tabs["dft"][2]))
    w = []
    for c in range(2):
        rows = []
        for q in range(NG6):
            block = f[c][q * KR : (q + 1) * KR]
            kern = tabs["kern"][q * KR : (q + 1) * KR, :]
            low = (block[:KL, :LOWL] + faug_ref[t, c * KL : (c + 1) * KL, q * LOWL : (q + 1) * LOWL]) * kern[:KL, :LOWL]
            wst_ref[t, c * KL : (c + 1) * KL, q * LOWL : (q + 1) * LOWL] = low
            rows.append(jnp.concatenate([low, block[:KL, LOWL:] * kern[:KL, LOWL:]], axis=1))
            rows.append(block[KL:] * kern[KL:])
        w.append(jnp.concatenate(rows, axis=0))
    both = mm3(w[0] + w[1], tabs["dft"][3])
    re, im = both - mm3(w[1], tabs["dft"][4]), both - mm3(w[0], tabs["dft"][5])
    v = []
    for q in range(NG6):
        a, b = re[q * KR : (q + 1) * KR], im[q * KR : (q + 1) * KR]
        if q:
            cr, ci = tabs["tw"][q : q + 1, :], tabs["tw"][8 + q : 9 + q, :]
            a, b = a * cr + b * ci, b * cr - a * ci
        v.append((a, b))
    v = dft6(v, 1)
    w = jnp.concatenate([jnp.concatenate([p[0], p[1]], axis=0) for p in v], axis=1)
    hi, lo = split(w)
    pot = mm(tabs["inv"][...], jnp.concatenate([hi, lo, hi], axis=0))
    acc_ref[0] += pot[:XO] * other[:XO]
    acc_ref[1] += pot[XO:] * other[:XO]


def slopes(n, glist_ref, qz_ref, exp_ref, choose_ref, phase_ref, yzt_ref, wst_ref):
    hi, lo = split(wst_ref[2 * n : 2 * n + 2].reshape(4 * KL, NG6 * LOWL))
    picked = mm(jnp.concatenate([hi, lo], axis=0), yzt_ref[...])
    picked = picked[:96] + picked[96:]
    first, second = kx_rows(glist_ref)
    cross = []
    for t in range(2):
        for mask in (first, second):
            at = t * 2 * KL
            wr = jnp.sum(jnp.where(mask, picked[at : at + KL], 0.0), axis=0, keepdims=True)
            wi = jnp.sum(jnp.where(mask, picked[at + KL : at + 2 * KL], 0.0), axis=0, keepdims=True)
            re = wr * phase_ref[0] + wi * phase_ref[1]
            im = wi * phase_ref[0] - wr * phase_ref[1]
            cross.append(jnp.concatenate([re, im], axis=1))
    hi, lo = split(jnp.concatenate(cross, axis=0))
    full = mm_nt(jnp.concatenate([hi, lo], axis=0), qz_ref[...])
    high, low = full[:128], full[128:]
    rest = high[:, 2 * PK :]
    slope = (high[:, : 2 * PK] + low[:, : 2 * PK] + jnp.concatenate([rest, rest], axis=1)) * (2.0 * AUG / N**3)
    slope = jnp.concatenate([slope, jnp.zeros((128, LG - 2 * PK), F32)], axis=1)
    chosen = jnp.where(choose_ref[...] > 0.0, 1.0, 0.0)
    sums = []
    for i in range(2):
        total = jnp.zeros((ATOMS, LG), F32)
        for t in range(2):
            at = (2 * t + i) * ATOMS
            total = total + slope[at : at + ATOMS] * exp_ref[2 + 2 * n + t][:, 2 * LG :]
        sums.append(total * chosen)
    return sums


def coef_row(packed, rsum):
    hi, lo = split(packed)
    full = mm(hi, rsum) + mm(lo, rsum)
    return jnp.sum(jnp.where(atom_of_lane(), full, 0.0), axis=0, keepdims=True)


def pack_tail(rows, coefs):
    rows = jnp.concatenate([rows[:, 324 * j : 324 * (j + 1)] for j in range(4)], axis=0)
    return jnp.concatenate([rows, coefs[:16], coefs[16:], jnp.zeros((16, TAIL - 340), F32)], axis=1)


def tail_coefs(tail):
    return jnp.concatenate([tail[:, 324:332], tail[:, 332:340]], axis=0)


def spread_band(main, tail):
    rows = jnp.concatenate([tail[4 * j : 4 * (j + 1), :324] for j in range(4)], axis=1)
    full = jnp.concatenate([main, rows, jnp.zeros((12, 1296), F32)], axis=0)
    zero = jnp.zeros((XB, LG - 216), F32)
    return jnp.concatenate([p for g in range(NG6) for p in (full[:, 216 * g : 216 * (g + 1)], zero)], axis=1)


def columns(total, c):
    start = CHUNK * c
    parts = []
    while start < CHUNK * (c + 1):
        g, at = divmod(start, 216)
        end = min(216 * (g + 1), CHUNK * (c + 1))
        parts.append(total[:, g * LG + at : g * LG + at + end - start])
        start = end
    return parts[0] if len(parts) == 1 else jnp.concatenate(parts, axis=1)


def pack_chunk(total, c):
    part = columns(total, c)
    main = part[:, :128]
    rest = part[:, 128:]
    last = jnp.concatenate([rest[32:40], jnp.zeros((8, 34), F32)], axis=0)
    rest = jnp.concatenate([rest[:16], rest[16:32], last, jnp.zeros((16, 26), F32)], axis=1)
    return jnp.concatenate([main, rest], axis=0)


def kernel(*refs):
    nt = len(TABLE_NAMES)
    sources = refs[: 6 + nt]
    out_ref, proj_ref = refs[6 + nt : 8 + nt]
    scratch = refs[8 + nt :]
    bands_ref, coef_ref, q_ref, species_ref, positions_ref, glist_ref = scratch[:6]
    tabs = dict(zip(TABLE_NAMES, scratch[6 : 6 + nt]))
    (band_ref, raw_ref, tail_ref, qz_ref, yzt_ref, phase_ref, choose_ref, exp_ref, faug_ref, wst_ref,
     acc_ref, got_ref, pgive_ref, pgot_ref, chunk_ref, chunks_ref,
     load_sem, tail_send, tail_recv, band_send, band_recv, sum_send, sum_recv, coef_send, coef_recv,
     chunk_send, chunk_recv) = scratch[6 + nt :]
    row, col = lax.axis_index("row"), lax.axis_index("col")
    zed, wide, core = row // 8, row // 2 % 4, row % 2

    def pick(values):
        return sum(jnp.where(col == c, v, 0) for c, v in enumerate(values))

    def at(dz, dy, k, c):
        return (((zed + dz + 16) % 8 * 4 + (wide + dy + 8) % 4) * 2 + k, c)

    sibling = at(0, 0, 1 - core, col)
    targets, origins = [], []
    for m in range(4):
        to, n, k, dz, dy = (pick([entries[m][e] for entries in TARGETS]) for e in range(5))
        targets.append((at(-dz, -dy, k, to), 2 * n + core))
    for n in range(2):
        dz, dy, other = (
            pick([e[2 * n][0] for e in OFFSETS]) * (1 - core) + pick([e[2 * n + 1][0] for e in OFFSETS]) * core,
            pick([e[2 * n][1] for e in OFFSETS]) * (1 - core) + pick([e[2 * n + 1][1] for e in OFFSETS]) * core,
            pick([int(e[2 * n][1] != 0) for e in OFFSETS]) * (1 - core)
            + pick([int(e[2 * n + 1][1] != 0) for e in OFFSETS]) * core,
        )
        origins += [at(dz, dy, k, col + other * (1 - 2 * (col % 2))) for k in range(2)]
    home = jnp.logical_and(col == 6, core == 0)
    away = jnp.logical_not(home)
    peers = [(row, (col + step) % 8) for step in range(1, 8)]
    mesh_id = pl.DeviceIdType.MESH

    barrier = pltpu.get_barrier_semaphore()

    def greet(partner):
        pl.semaphore_signal(barrier, inc=1, device_id=partner, device_id_type=mesh_id)

    pl.when(away)(lambda: greet(origins[0]))
    others = origins[1:] + [sibling] + peers
    for partner in others:
        greet(partner)

    names = ("bands", "projections", "qfunc", "species", "positions", "glist", *TABLE_NAMES)
    loads = [
        pltpu.make_async_copy(src, dst, load_sem.at[n]) for n, (src, dst) in enumerate(zip(sources, scratch[: 6 + nt]))
    ]
    for load in loads:
        load.start()

    def remote(src, dst, to, sems, recvs, n, m=None):
        return pltpu.make_async_remote_copy(
            src_ref=src, dst_ref=dst, send_sem=sems.at[n], recv_sem=recvs.at[n if m is None else m],
            device_id=to, device_id_type=mesh_id,
        )

    loads[0].wait()
    loads[1].wait()
    loads[names.index("fold")].wait()
    own = jnp.where(atom_of_lane(), coef_ref[...].astype(F32), 0.0).astype(BF16)
    tail_ref[0] = pack_tail(bands_ref[0].astype(F32)[32:36], mm(own, tabs["fold"][...])).astype(BF16)
    main = bands_ref.at[0, pl.ds(0, 32)]

    pl.semaphore_wait(barrier, len(others) + 1 - home.astype(jnp.int32))
    tails = [remote(tail_ref.at[0], tail_ref.at[1], sibling, tail_send, tail_recv, 4)]
    fields = [remote(main, raw_ref.at[1], sibling, band_send, band_recv, 4)]
    for m, (to, t) in enumerate(targets):
        tails.append(remote(tail_ref.at[0], tail_ref.at[2 + t], to, tail_send, tail_recv, m, t))
        fields.append(remote(main, raw_ref.at[2 + t], to, band_send, band_recv, m, t))

    def each(group, numbers, act):
        for n in numbers:
            if n == 1:
                pl.when(away)(lambda: act(group[n]))
            else:
                act(group[n])

    for numbers in ((0, 1, 2), (3, 4)):
        for group in (tails, fields):
            each(group, numbers, lambda copy: copy.start())

    for n, load in enumerate(loads):
        if n > 1 and names[n] != "fold":
            load.wait()
    setup_lists(glist_ref, positions_ref, species_ref, tabs["weight"], yzt_ref, phase_ref, choose_ref)
    acc_ref[...] = jnp.zeros_like(acc_ref)
    for c in range(2):
        hi, lo = split(q_ref[c].reshape(NSPEC * NH * NH, NLIST))
        packed = mm(tabs["sel"][...], hi) + mm(tabs["sel"][...], lo)
        hi, lo = split(packed)
        qz_ref[:, c * NLIST : (c + 1) * NLIST] = jnp.concatenate([hi, hi, lo], axis=0)

    def arrived(which, ref, recvs, n):
        pltpu.make_async_remote_copy(
            src_ref=which, dst_ref=ref, send_sem=recvs.at[n], recv_sem=recvs.at[n], device_id=sibling,
            device_id_type=mesh_id,
        ).wait_recv()

    def unpack(b):
        band_ref[b] = spread_band(raw_ref[b].astype(F32), tail_ref[b].astype(F32)).astype(BF16)

    def expand(b):
        exp_ref[b] = mm(tail_coefs(tail_ref[b].astype(F32)).astype(BF16), tabs["rep"][...])

    def copy_home():
        tail_ref[2] = tail_ref[0]
        raw_ref[2] = bands_ref[0, 0:32, :]

    pl.when(home)(copy_home)
    raw_ref[0] = bands_ref[0, 0:32, :]
    unpack(0)
    expand(0)
    arrived(tail_ref.at[0], tail_ref.at[1], tail_recv, 4)
    expand(1)
    arrived(main, raw_ref.at[1], band_recv, 4)
    unpack(1)

    def step(t, carry):
        pl.when(jnp.logical_or(away, t > 0))(lambda: arrived(main, raw_ref.at[2 + t], band_recv, t))
        unpack(2 + t)
        batch(t, band_ref, faug_ref, wst_ref, acc_ref, tabs)
        return carry

    sums = []
    for n in range(2):
        for t in (2 * n, 2 * n + 1):
            wait = functools.partial(arrived, tail_ref.at[0], tail_ref.at[2 + t], tail_recv, t)
            if t == 0:
                pl.when(away)(wait)
            else:
                wait()
            expand(2 + t)
        augment(n, glist_ref, qz_ref, exp_ref, choose_ref, phase_ref, yzt_ref, faug_ref)
        lax.fori_loop(2 * n, 2 * n + 2, step, 0)
        if n == 0:
            sums.append(slopes(n, glist_ref, qz_ref, exp_ref, choose_ref, phase_ref, yzt_ref, wst_ref))
    give = remote(acc_ref.at[1], got_ref, sibling, sum_send, sum_recv, 0)
    give.start()
    sums.append(slopes(1, glist_ref, qz_ref, exp_ref, choose_ref, phase_ref, yzt_ref, wst_ref))
    rows = [coef_row(sums[0][i] + sums[1][i], tabs["rsum"][...]) for i in range(2)]
    pgive_ref[...] = jnp.broadcast_to(rows[1], (8, 256))
    coefs = remote(pgive_ref, pgot_ref, sibling, coef_send, coef_recv, 0)
    coefs.start()
    give.wait_recv()
    total = acc_ref[0] + got_ref[...]
    for c in range(8):
        chunk_ref[c] = pack_chunk(total, c)
    coefs.wait_recv()
    proj = rows[0] + pgot_ref[0:1, :]
    for c in range(8):
        chunk_ref[c, N : N + 1, 0:32] = proj[:, 32 * c : 32 * (c + 1)]
    chunks = []
    for n, to in enumerate(peers):
        chunks.append(remote(chunk_ref.at[to[1]], chunks_ref.at[n], to, chunk_send, chunk_recv, n))
        chunks[-1].start()
    whole = chunk_ref[col]
    for n, copy in enumerate(chunks):
        copy.wait_recv()
        whole = whole + chunks_ref[n]
    whole = whole * -0.5
    out_ref[:, 0, 0:128] = whole[:N]
    out_ref[0:16, 0, 128:CHUNK] = whole[40:56, 0:34]
    out_ref[16:32, 0, 128:CHUNK] = whole[40:56, 34:68]
    out_ref[32:36, 0, 128:CHUNK] = whole[40:44, 68:102]
    proj_ref[...] = whole[N : N + 1, 0:32]
    for group in (tails, fields):
        each(group, range(5), lambda copy: copy.wait_send())
    for copy in [give, coefs] + chunks:
        copy.wait_send()


def hand_over(grid_ref, proj_ref, grid_out, proj_out, sem):
    copies = [
        pltpu.make_async_copy(src, dst, sem.at[n])
        for n, (src, dst) in enumerate(((grid_ref, grid_out), (proj_ref, proj_out)))
    ]
    for copy in copies:
        copy.start()
    for copy in copies:
        copy.wait()


def on_device(bands, projections, qfunc, species, positions, glist):
    hbm = pl.BlockSpec(memory_space=pltpu.HBM)
    vm = pl.BlockSpec(memory_space=pltpu.VMEM)
    sources = [bands, projections, qfunc, species.reshape(1, ATOMS), positions, glist.reshape(1, NLIST)]
    sources += [jnp.asarray(TABLES[name]) for name in TABLE_NAMES]
    dma = pltpu.SemaphoreType.DMA
    grid, proj = pl.pallas_call(
        kernel,
        out_shape=(jax.ShapeDtypeStruct((N, 1, CHUNK), F32), jax.ShapeDtypeStruct((1, 32), F32)),
        in_specs=[hbm] * len(sources),
        out_specs=(vm, vm),
        scratch_shapes=[
            *[pltpu.VMEM(t.shape, t.dtype) for t in sources],
            pltpu.VMEM((2 + STEPS, XB, LANES), BF16),
            pltpu.VMEM((2 + STEPS, 32, 1296), BF16),
            pltpu.VMEM((2 + STEPS, 16, TAIL), BF16),
            pltpu.VMEM((3 * PK, 2 * NLIST), BF16),
            pltpu.VMEM((NG6 * LOWL, NLIST), BF16),
            pltpu.VMEM((2, ATOMS, NLIST), F32),
            pltpu.VMEM((ATOMS, LG), F32),
            pltpu.VMEM((2 + STEPS, ATOMS, 3 * LG), F32),
            pltpu.VMEM((STEPS, 2 * KL, NG6 * LOWL), F32),
            pltpu.VMEM((STEPS, 2 * KL, NG6 * LOWL), F32),
            pltpu.VMEM((2, XO, LANES), F32),
            pltpu.VMEM((XO, LANES), F32),
            pltpu.VMEM((8, 256), F32),
            pltpu.VMEM((8, 256), F32),
            pltpu.VMEM((8, 56, 128), F32),
            pltpu.VMEM((7, 56, 128), F32),
            dma((len(sources),)),
            *[dma((5,)) for unused in range(4)],
            *[dma((1,)) for unused in range(4)],
            *[dma((7,)) for unused in range(2)],
        ],
        compiler_params=pltpu.CompilerParams(
            collective_id=0, has_side_effects=True, vmem_limit_bytes=60 * 2**20
        ),
    )(*sources)
    grid, proj = pl.pallas_call(
        hand_over,
        out_shape=(jax.ShapeDtypeStruct((N, 1, CHUNK), F32), jax.ShapeDtypeStruct((1, 32), F32)),
        in_specs=[hbm] * 2,
        out_specs=(hbm, hbm),
        scratch_shapes=[dma((2,))],
        compiler_params=pltpu.CompilerParams(vmem_limit_bytes=60 * 2**20),
    )(grid, proj)
    return (jnp.swapaxes(grid, 0, 1), proj)


def solution(mesh):
    return jax.shard_map(
        on_device,
        mesh=mesh,
        in_specs=(P("row", None, None), P("row", None), P(), P(), P(), P()),
        out_specs=(P("row", None, "col"), P("row", "col")),
        check_vma=False,
    )
```

```python
import functools
import math

import jax
import jax.numpy as jnp
import ml_dtypes
import numpy as np
from jax import lax
from jax.experimental import pallas as pl
from jax.experimental.pallas import tpu as pltpu
from jax.sharding import PartitionSpec as P

N = 36
NG6 = 6
LG = 256
LOWL = 128
LANES = NG6 * LG
XB = 48
XO = 40
KL = 24
KR = 40
ATOMS, NH, NSPEC, NLIST = 32, 8, 2, 1024
PK = 80
AUG = N**1.5 / (NH * math.sqrt(ATOMS))
STEPS = 4
TAIL = 384
CHUNK = 162
F32, BF16 = jnp.float32, jnp.bfloat16

OFFSETS = [
    [(1, -1), (3, 0), (-1, 2), (-3, -1)],
    [(-1, 1), (-3, 0), (1, 2), (3, 1)],
    [(-2, 0), (2, -1), (2, 2), (-2, -1)],
    [(2, 0), (-2, 1), (-2, 2), (2, 1)],
    [(1, 0), (-1, -1), (-3, 2), (3, -1)],
    [(-1, 0), (1, 1), (3, 2), (-3, 1)],
    [(0, 0), (0, -1), (4, 2), (4, -1)],
    [(0, 2), (0, 1), (4, 0), (4, 1)],
]


def make_targets():
    targets = []
    for col in range(8):
        mine = []
        for to in (col, col ^ 1):
            for e, (dz, dy) in enumerate(OFFSETS[to]):
                if (dy == 0) == (to == col):
                    mine.append((e // 2, abs(dz) + (0, 1, 3, 1)[dy % 4], to, e % 2, dz, dy))
        targets.append([(to, n, k, dz, dy) for n, unused, to, k, dz, dy in sorted(mine)])
    return targets


TARGETS = make_targets()


def split_np(a):
    hi = a.astype(np.float32).astype(ml_dtypes.bfloat16)
    lo = (a - hi.astype(np.float64)).astype(np.float32).astype(ml_dtypes.bfloat16)
    return hi, lo


def row_of(pair, kx):
    return 11 * pair + kx if kx <= 10 else KL + 8 * pair + kx - 11


def make_tables():
    k = np.arange(19)[:, None]
    x = np.arange(N)[None, :]
    ang = 2 * np.pi * (k * x % N) / N
    weight = np.where((k == 0) | (k == N // 2), 1.0, 2.0) / N**3
    parts = (np.cos(ang), -np.sin(ang))
    bf = ml_dtypes.bfloat16
    fwd = np.zeros((4 * KR, 4 * XB), bf)
    inv = np.zeros((2 * XO, 6 * KR), bf)
    for pair in range(2):
        for c, part in enumerate(parts):
            fh, fl = split_np(part)
            ih, il = split_np(weight * part)
            for kx in range(19):
                r = c * KR + row_of(pair, kx)
                fwd[r, 96 * pair : 96 * pair + N] = fh[kx]
                fwd[r, 96 * pair + XB : 96 * pair + XB + N] = fh[kx]
                fwd[2 * KR + r, 96 * pair : 96 * pair + N] = fl[kx]
                for b, values in enumerate((ih, ih, il)):
                    inv[XO * pair : XO * pair + N, 2 * KR * b + r] = values[kx]
    r_of = np.repeat(np.arange(6), N)
    z_of = np.tile(np.arange(N), 6)
    near = [(s, kz) for s in (0, 1, 4, 5) for kz in (*range(11), *range(26, 36))]
    order = near + [(s, kz) for s in range(6) for kz in range(N) if (s, kz) not in near]
    s_of = np.array([p[0] for p in order])
    k_of = np.array([p[1] for p in order])
    ang = 2 * np.pi * ((6 * r_of[:, None] * s_of[None, :] + z_of[:, None] * k_of[None, :]) % N) / N
    c = np.zeros((LG, LG))
    s = np.zeros((LG, LG))
    c[:216, :216] = np.cos(ang)
    s[:216, :216] = np.sin(ang)

    def stacked(w):
        hi, lo = split_np(w)
        return np.concatenate([hi, hi, lo], axis=0)

    dft = np.stack([stacked(w) for w in (c, c - s, c + s, c.T, (c + s).T, (c - s).T)])
    tw = np.zeros((16, LG), np.float32)
    for q in range(6):
        a = 2 * np.pi * (r_of * q % N) / N
        tw[q, :216] = np.cos(a)
        tw[8 + q, :216] = -np.sin(a)
    signed = lambda v: np.where(v > N // 2, v - N, v)
    kern = np.zeros((NG6 * KR, LG), np.float32)
    for q in range(6):
        for pair in range(2):
            for kx in range(19):
                n2 = kx**2 + signed(q + 6 * s_of) ** 2 + signed(k_of) ** 2
                kern[q * KR + row_of(pair, kx), :216] = np.where(n2 > 0, N**1.5 / 4 / np.maximum(n2, 1), 0)
    packed = [(s, l, m) for s in range(NSPEC) for l in range(NH) for m in range(l, NH)]
    sel = np.zeros((PK, NSPEC * NH * NH), np.float32)
    rep = np.zeros((NH, 768), np.float32)
    rsum = np.zeros((256, 256), np.float32)
    weight = np.zeros((NSPEC, LG), np.float32)
    kk = np.arange(256) % NH
    k8 = np.arange(NH)
    fold = kk[:, None] == k8[None, :]
    for p, (s, l, m) in enumerate(packed):
        sel[p, s * 64 + l * 8 + m] += 0.5
        sel[p, s * 64 + m * 8 + l] += 0.5
        for b in range(3):
            rep[k8 == l, PK * b + p] = 1
            rep[k8 == m, LG + PK * b + p] = 1
            weight[s, PK * b + p] = 0.5 if l == m else 1.0
        rep[k8 == m, 2 * LG + p] = 1
        rsum[p, kk == l] = 1
        if l != m:
            rep[k8 == l, 2 * LG + PK + p] = 1
            rsum[PK + p, kk == m] = 1
    return dict(
        fwd=fwd, inv=inv, dft=dft, tw=tw, kern=kern, sel=sel.astype(bf), rep=rep.astype(bf), rsum=rsum.astype(bf), fold=fold.astype(bf),
        weight=np.concatenate([weight, np.zeros((6, LG), np.float32)]),
    )


TABLES = make_tables()
TABLE_NAMES = ("fwd", "inv", "dft", "tw", "kern", "sel", "rep", "rsum", "fold", "weight")


def split(a):
    hi = a.astype(BF16)
    return hi, (a - hi.astype(F32)).astype(BF16)


def mm(a, b):
    return jnp.dot(a, b, preferred_element_type=F32)


def mm_nt(a, b):
    return lax.dot_general(a, b, (((1,), (1,)), ((), ())), preferred_element_type=F32)


def dft3(a, b, c, sign):
    h = math.sqrt(3.0) / 2
    sr, si = b[0] + c[0], b[1] + c[1]
    dr, di = (b[0] - c[0]) * h, (b[1] - c[1]) * h
    tr, ti = a[0] - 0.5 * sr, a[1] - 0.5 * si
    zero = (a[0] + sr, a[1] + si)
    minus = (tr + di, ti - dr)
    plus = (tr - di, ti + dr)
    return (zero, minus, plus) if sign < 0 else (zero, plus, minus)


def dft6(v, sign):
    add = lambda p, q: (p[0] + q[0], p[1] + q[1])
    sub = lambda p, q: (p[0] - q[0], p[1] - q[1])
    e = dft3(add(v[0], v[3]), add(v[1], v[4]), add(v[2], v[5]), sign)
    o = dft3(sub(v[0], v[3]), sub(v[4], v[1]), sub(v[2], v[5]), sign)
    return [e[0], o[2], e[1], o[0], e[2], o[1]]


def mm3(x, w):
    hi, lo = split(x)
    return mm(jnp.concatenate([hi, lo, hi], axis=1), w)


def atom_of_lane():
    lane = lax.broadcasted_iota(jnp.int32, (ATOMS, 256), 1)
    return lane // NH == lax.broadcasted_iota(jnp.int32, (ATOMS, 256), 0)


def setup_lists(glist_ref, positions_ref, species_ref, weight_ref, yzt_ref, phase_ref, choose_ref):
    g = glist_ref[...]
    kx = g // (N * N)
    ky = g // N % N
    kz = g % N
    s = ky // 6
    where = (ky % 6) * LOWL + jnp.where(s < 2, s, s - 2) * 21 + jnp.where(kz <= 10, kz, kz - 15)
    step = 256
    for base in range(0, NG6 * LOWL, step):
        rows = lax.broadcasted_iota(jnp.int32, (step, NLIST), 0) + base
        yzt_ref[base : base + step, :] = jnp.where(rows == where, 1.0, 0.0).astype(BF16)
    sg = lambda v: jnp.where(v > N // 2, v - N, v).astype(F32)
    eye = lax.broadcasted_iota(jnp.int32, (ATOMS, ATOMS), 0) == lax.broadcasted_iota(jnp.int32, (ATOMS, ATOMS), 1)
    column = lambda row: jnp.sum(jnp.where(eye, row, 0.0), axis=1, keepdims=True)
    turns = (
        column(positions_ref[0:1, :]) * kx.astype(F32)
        + column(positions_ref[1:2, :]) * sg(ky)
        + column(positions_ref[2:3, :]) * sg(kz)
    )
    theta = (turns - jnp.floor(turns)) * (2.0 * math.pi)
    phase_ref[0] = jnp.cos(theta)
    phase_ref[1] = -jnp.sin(theta)
    spec = column(species_ref[...].astype(F32))
    choose = jnp.zeros((ATOMS, LG), F32)
    for s in range(NSPEC):
        choose = choose + jnp.where(spec == float(s), 1.0, 0.0) * weight_ref[s : s + 1, :]
    choose_ref[...] = choose


def kx_rows(glist_ref):
    kx = glist_ref[...] // (N * N)
    rows = lax.broadcasted_iota(jnp.int32, (KL, NLIST), 0)
    return rows == kx, rows == kx + 11


def augment(n, glist_ref, qz_ref, exp_ref, choose_ref, phase_ref, yzt_ref, faug_ref):
    lane = lax.broadcasted_iota(jnp.int32, (ATOMS, LG), 1)
    middle = jnp.logical_and(lane >= PK, lane < 2 * PK)
    mixed = []
    for t in range(2):
        for i in range(2):
            a, b = exp_ref[i], exp_ref[2 + 2 * n + t]
            full = (a[:, :LG] * b[:, LG : 2 * LG] + b[:, :LG] * a[:, LG : 2 * LG]) * choose_ref[...]
            hi = full.astype(BF16).astype(F32)
            mixed.append(jnp.where(middle, full - hi, hi).astype(BF16)[:, : 3 * PK])
    mixed = jnp.concatenate(mixed, axis=0)
    z_re = mm(mixed, qz_ref[:, :NLIST])
    z_im = mm(mixed, qz_ref[:, NLIST:])
    first, second = kx_rows(glist_ref)
    spread = []
    for t in range(2):
        re, im = [], []
        for i in range(2):
            at = (2 * t + i) * ATOMS
            zr, zi = z_re[at : at + ATOMS], z_im[at : at + ATOMS]
            re.append(jnp.sum(phase_ref[0] * zr - phase_ref[1] * zi, axis=0, keepdims=True) * AUG)
            im.append(jnp.sum(phase_ref[0] * zi + phase_ref[1] * zr, axis=0, keepdims=True) * AUG)
        for rows in (re, im):
            spread.append(jnp.where(first, rows[0], jnp.where(second, rows[1], 0.0)))
    hi, lo = split(jnp.concatenate(spread, axis=0))
    both = jnp.concatenate([hi, lo], axis=0)
    for base in range(0, NG6 * LOWL, LG):
        part = mm_nt(both, yzt_ref[base : base + LG, :])
        part = part[:96] + part[96:]
        for t in range(2):
            faug_ref[2 * n + t, :, base : base + LG] = part[48 * t : 48 * (t + 1)]


def batch(t, band_ref, faug_ref, wst_ref, acc_ref, tabs):
    other = band_ref[2 + t].astype(F32)
    halves = []
    for i in range(2):
        halves += split(band_ref[i].astype(F32) * other)
    out = mm(tabs["fwd"][...], jnp.concatenate(halves, axis=0))
    spec = out[: 2 * KR] + out[2 * KR :]
    v = [(spec[:KR, g * LG : (g + 1) * LG], spec[KR:, g * LG : (g + 1) * LG]) for g in range(NG6)]
    re_rows, im_rows = [], []
    for q, (re, im) in enumerate(dft6(v, -1)):
        if q:
            cr, ci = tabs["tw"][q : q + 1, :], tabs["tw"][8 + q : 9 + q, :]
            re, im = re * cr - im * ci, re * ci + im * cr
        re_rows.append(re)
        im_rows.append(im)
    re, im = jnp.concatenate(re_rows, axis=0), jnp.concatenate(im_rows, axis=0)
    both = mm3(re + im, tabs["dft"][0])
    f = (both - mm3(im, tabs["dft"][1]), both - mm3(re, tabs["dft"][2]))
    w = []
    for c in range(2):
        rows = []
        for q in range(NG6):
            block = f[c][q * KR : (q + 1) * KR]
            kern = tabs["kern"][q * KR : (q + 1) * KR, :]
            low = (block[:KL, :LOWL] + faug_ref[t, c * KL : (c + 1) * KL, q * LOWL : (q + 1) * LOWL]) * kern[:KL, :LOWL]
            wst_ref[t, c * KL : (c + 1) * KL, q * LOWL : (q + 1) * LOWL] = low
            rows.append(jnp.concatenate([low, block[:KL, LOWL:] * kern[:KL, LOWL:]], axis=1))
            rows.append(block[KL:] * kern[KL:])
        w.append(jnp.concatenate(rows, axis=0))
    both = mm3(w[0] + w[1], tabs["dft"][3])
    re, im = both - mm3(w[1], tabs["dft"][4]), both - mm3(w[0], tabs["dft"][5])
    v = []
    for q in range(NG6):
        a, b = re[q * KR : (q + 1) * KR], im[q * KR : (q + 1) * KR]
        if q:
            cr, ci = tabs["tw"][q : q + 1, :], tabs["tw"][8 + q : 9 + q, :]
            a, b = a * cr + b * ci, b * cr - a * ci
        v.append((a, b))
    v = dft6(v, 1)
    w = jnp.concatenate([jnp.concatenate([p[0], p[1]], axis=0) for p in v], axis=1)
    hi, lo = split(w)
    pot = mm(tabs["inv"][...], jnp.concatenate([hi, lo, hi], axis=0))
    acc_ref[0] += pot[:XO] * other[:XO]
    acc_ref[1] += pot[XO:] * other[:XO]


def slopes(n, glist_ref, qz_ref, exp_ref, choose_ref, phase_ref, yzt_ref, wst_ref):
    hi, lo = split(wst_ref[2 * n : 2 * n + 2].reshape(4 * KL, NG6 * LOWL))
    picked = mm(jnp.concatenate([hi, lo], axis=0), yzt_ref[...])
    picked = picked[:96] + picked[96:]
    first, second = kx_rows(glist_ref)
    cross = []
    for t in range(2):
        for mask in (first, second):
            at = t * 2 * KL
            wr = jnp.sum(jnp.where(mask, picked[at : at + KL], 0.0), axis=0, keepdims=True)
            wi = jnp.sum(jnp.where(mask, picked[at + KL : at + 2 * KL], 0.0), axis=0, keepdims=True)
            re = wr * phase_ref[0] + wi * phase_ref[1]
            im = wi * phase_ref[0] - wr * phase_ref[1]
            cross.append(jnp.concatenate([re, im], axis=1))
    hi, lo = split(jnp.concatenate(cross, axis=0))
    full = mm_nt(jnp.concatenate([hi, lo], axis=0), qz_ref[...])
    high, low = full[:128], full[128:]
    rest = high[:, 2 * PK :]
    slope = (high[:, : 2 * PK] + low[:, : 2 * PK] + jnp.concatenate([rest, rest], axis=1)) * (2.0 * AUG / N**3)
    slope = jnp.concatenate([slope, jnp.zeros((128, LG - 2 * PK), F32)], axis=1)
    chosen = jnp.where(choose_ref[...] > 0.0, 1.0, 0.0)
    sums = []
    for i in range(2):
        total = jnp.zeros((ATOMS, LG), F32)
        for t in range(2):
            at = (2 * t + i) * ATOMS
            total = total + slope[at : at + ATOMS] * exp_ref[2 + 2 * n + t][:, 2 * LG :]
        sums.append(total * chosen)
    return sums


def coef_row(packed, rsum):
    hi, lo = split(packed)
    full = mm(hi, rsum) + mm(lo, rsum)
    return jnp.sum(jnp.where(atom_of_lane(), full, 0.0), axis=0, keepdims=True)


def pack_tail(rows, coefs):
    rows = jnp.concatenate([rows[:, 324 * j : 324 * (j + 1)] for j in range(4)], axis=0)
    return jnp.concatenate([rows, coefs[:16], coefs[16:], jnp.zeros((16, TAIL - 340), F32)], axis=1)


def tail_coefs(tail):
    return jnp.concatenate([tail[:, 324:332], tail[:, 332:340]], axis=0)


def spread_band(main, tail):
    rows = jnp.concatenate([tail[4 * j : 4 * (j + 1), :324] for j in range(4)], axis=1)
    full = jnp.concatenate([main, rows, jnp.zeros((12, 1296), F32)], axis=0)
    zero = jnp.zeros((XB, LG - 216), F32)
    return jnp.concatenate([p for g in range(NG6) for p in (full[:, 216 * g : 216 * (g + 1)], zero)], axis=1)


def columns(total, c):
    start = CHUNK * c
    parts = []
    while start < CHUNK * (c + 1):
        g, at = divmod(start, 216)
        end = min(216 * (g + 1), CHUNK * (c + 1))
        parts.append(total[:, g * LG + at : g * LG + at + end - start])
        start = end
    return parts[0] if len(parts) == 1 else jnp.concatenate(parts, axis=1)


def pack_chunk(total, c):
    part = columns(total, c)
    main = part[:, :128]
    rest = part[:, 128:]
    last = jnp.concatenate([rest[32:40], jnp.zeros((8, 34), F32)], axis=0)
    rest = jnp.concatenate([rest[:16], rest[16:32], last, jnp.zeros((16, 26), F32)], axis=1)
    return jnp.concatenate([main, rest], axis=0)


def kernel(*refs):
    nt = len(TABLE_NAMES)
    sources = refs[: 6 + nt]
    out_ref, proj_ref = refs[6 + nt : 8 + nt]
    scratch = refs[8 + nt :]
    bands_ref, coef_ref, q_ref, species_ref, positions_ref, glist_ref = scratch[:6]
    tabs = dict(zip(TABLE_NAMES, scratch[6 : 6 + nt]))
    (band_ref, raw_ref, tail_ref, qz_ref, yzt_ref, phase_ref, choose_ref, exp_ref, faug_ref, wst_ref,
     acc_ref, got_ref, pgive_ref, pgot_ref, chunk_ref, chunks_ref,
     load_sem, tail_send, tail_recv, band_send, band_recv, sum_send, sum_recv, coef_send, coef_recv,
     chunk_send, chunk_recv) = scratch[6 + nt :]
    row, col = lax.axis_index("row"), lax.axis_index("col")
    zed, wide, core = row // 8, row // 2 % 4, row % 2

    def pick(values):
        return sum(jnp.where(col == c, v, 0) for c, v in enumerate(values))

    def at(dz, dy, k, c):
        return (((zed + dz + 16) % 8 * 4 + (wide + dy + 8) % 4) * 2 + k, c)

    sibling = at(0, 0, 1 - core, col)
    targets, origins = [], []
    for m in range(4):
        to, n, k, dz, dy = (pick([entries[m][e] for entries in TARGETS]) for e in range(5))
        targets.append((at(-dz, -dy, k, to), 2 * n + core))
    for n in range(2):
        dz, dy, other = (
            pick([e[2 * n][0] for e in OFFSETS]) * (1 - core) + pick([e[2 * n + 1][0] for e in OFFSETS]) * core,
            pick([e[2 * n][1] for e in OFFSETS]) * (1 - core) + pick([e[2 * n + 1][1] for e in OFFSETS]) * core,
            pick([int(e[2 * n][1] != 0) for e in OFFSETS]) * (1 - core)
            + pick([int(e[2 * n + 1][1] != 0) for e in OFFSETS]) * core,
        )
        origins += [at(dz, dy, k, col + other * (1 - 2 * (col % 2))) for k in range(2)]
    home = jnp.logical_and(col == 6, core == 0)
    away = jnp.logical_not(home)
    peers = [(row, (col + step) % 8) for step in range(1, 8)]
    mesh_id = pl.DeviceIdType.MESH

    barrier = pltpu.get_barrier_semaphore()

    def greet(partner):
        pl.semaphore_signal(barrier, inc=1, device_id=partner, device_id_type=mesh_id)

    pl.when(away)(lambda: greet(origins[0]))
    others = origins[1:] + [sibling] + peers
    for partner in others:
        greet(partner)

    names = ("bands", "projections", "qfunc", "species", "positions", "glist", *TABLE_NAMES)
    loads = [
        pltpu.make_async_copy(src, dst, load_sem.at[n]) for n, (src, dst) in enumerate(zip(sources, scratch[: 6 + nt]))
    ]
    for load in loads:
        load.start()

    def remote(src, dst, to, sems, recvs, n, m=None):
        return pltpu.make_async_remote_copy(
            src_ref=src, dst_ref=dst, send_sem=sems.at[n], recv_sem=recvs.at[n if m is None else m],
            device_id=to, device_id_type=mesh_id,
        )

    loads[0].wait()
    loads[1].wait()
    loads[names.index("fold")].wait()
    own = jnp.where(atom_of_lane(), coef_ref[...].astype(F32), 0.0).astype(BF16)
    tail_ref[0] = pack_tail(bands_ref[0].astype(F32)[32:36], mm(own, tabs["fold"][...])).astype(BF16)
    main = bands_ref.at[0, pl.ds(0, 32)]

    pl.semaphore_wait(barrier, len(others) + 1 - home.astype(jnp.int32))
    tails = [remote(tail_ref.at[0], tail_ref.at[1], sibling, tail_send, tail_recv, 4)]
    fields = [remote(main, raw_ref.at[1], sibling, band_send, band_recv, 4)]
    for m, (to, t) in enumerate(targets):
        tails.append(remote(tail_ref.at[0], tail_ref.at[2 + t], to, tail_send, tail_recv, m, t))
        fields.append(remote(main, raw_ref.at[2 + t], to, band_send, band_recv, m, t))

    def each(group, numbers, act):
        for n in numbers:
            if n == 1:
                pl.when(away)(lambda: act(group[n]))
            else:
                act(group[n])

    each(tails, range(5), lambda copy: copy.start())
    each(fields, (0, 1, 2), lambda copy: copy.start())
    pl.when(core == 0)(lambda: each(fields, (3, 4), lambda copy: copy.start()))

    for n, load in enumerate(loads):
        if n > 1 and names[n] != "fold":
            load.wait()
    setup_lists(glist_ref, positions_ref, species_ref, tabs["weight"], yzt_ref, phase_ref, choose_ref)
    acc_ref[...] = jnp.zeros_like(acc_ref)
    for c in range(2):
        hi, lo = split(q_ref[c].reshape(NSPEC * NH * NH, NLIST))
        packed = mm(tabs["sel"][...], hi) + mm(tabs["sel"][...], lo)
        hi, lo = split(packed)
        qz_ref[:, c * NLIST : (c + 1) * NLIST] = jnp.concatenate([hi, hi, lo], axis=0)

    def arrived(which, ref, recvs, n):
        pltpu.make_async_remote_copy(
            src_ref=which, dst_ref=ref, send_sem=recvs.at[n], recv_sem=recvs.at[n], device_id=sibling,
            device_id_type=mesh_id,
        ).wait_recv()

    def unpack(b):
        band_ref[b] = spread_band(raw_ref[b].astype(F32), tail_ref[b].astype(F32)).astype(BF16)

    def expand(b):
        exp_ref[b] = mm(tail_coefs(tail_ref[b].astype(F32)).astype(BF16), tabs["rep"][...])

    def copy_home():
        tail_ref[2] = tail_ref[0]
        raw_ref[2] = bands_ref[0, 0:32, :]

    pl.when(home)(copy_home)
    raw_ref[0] = bands_ref[0, 0:32, :]
    unpack(0)
    expand(0)
    arrived(tail_ref.at[0], tail_ref.at[1], tail_recv, 4)
    expand(1)
    arrived(main, raw_ref.at[1], band_recv, 4)
    unpack(1)

    def step(t, carry):
        pl.when(jnp.logical_or(away, t > 0))(lambda: arrived(main, raw_ref.at[2 + t], band_recv, t))
        unpack(2 + t)
        batch(t, band_ref, faug_ref, wst_ref, acc_ref, tabs)
        return carry

    sums = []
    for n in range(2):
        for t in (2 * n, 2 * n + 1):
            wait = functools.partial(arrived, tail_ref.at[0], tail_ref.at[2 + t], tail_recv, t)
            if t == 0:
                pl.when(away)(wait)
            else:
                wait()
            expand(2 + t)
        augment(n, glist_ref, qz_ref, exp_ref, choose_ref, phase_ref, yzt_ref, faug_ref)
        if n == 0:
            each(fields, (0, 1, 2), lambda copy: copy.wait_send())
            step(0, 0)
            pl.when(core == 1)(lambda: each(fields, (3, 4), lambda copy: copy.start()))
            lax.fori_loop(1, 2, step, 0)
        else:
            lax.fori_loop(2, 4, step, 0)
        if n == 0:
            sums.append(slopes(n, glist_ref, qz_ref, exp_ref, choose_ref, phase_ref, yzt_ref, wst_ref))
    give = remote(acc_ref.at[1], got_ref, sibling, sum_send, sum_recv, 0)
    give.start()
    sums.append(slopes(1, glist_ref, qz_ref, exp_ref, choose_ref, phase_ref, yzt_ref, wst_ref))
    rows = [coef_row(sums[0][i] + sums[1][i], tabs["rsum"][...]) for i in range(2)]
    pgive_ref[...] = jnp.broadcast_to(rows[1], (8, 256))
    coefs = remote(pgive_ref, pgot_ref, sibling, coef_send, coef_recv, 0)
    coefs.start()
    give.wait_recv()
    total = acc_ref[0] + got_ref[...]
    for c in range(8):
        chunk_ref[c] = pack_chunk(total, c)
    coefs.wait_recv()
    proj = rows[0] + pgot_ref[0:1, :]
    for c in range(8):
        chunk_ref[c, N : N + 1, 0:32] = proj[:, 32 * c : 32 * (c + 1)]
    chunks = []
    for n, to in enumerate(peers):
        chunks.append(remote(chunk_ref.at[to[1]], chunks_ref.at[n], to, chunk_send, chunk_recv, n))
        chunks[-1].start()
    whole = chunk_ref[col]
    for n, copy in enumerate(chunks):
        copy.wait_recv()
        whole = whole + chunks_ref[n]
    whole = whole * -0.5
    out_ref[:, 0, 0:128] = whole[:N]
    out_ref[0:16, 0, 128:CHUNK] = whole[40:56, 0:34]
    out_ref[16:32, 0, 128:CHUNK] = whole[40:56, 34:68]
    out_ref[32:36, 0, 128:CHUNK] = whole[40:44, 68:102]
    proj_ref[...] = whole[N : N + 1, 0:32]
    each(tails, range(5), lambda copy: copy.wait_send())
    each(fields, (3, 4), lambda copy: copy.wait_send())
    for copy in [give, coefs] + chunks:
        copy.wait_send()


def hand_over(grid_ref, proj_ref, grid_out, proj_out, sem):
    copies = [
        pltpu.make_async_copy(src, dst, sem.at[n])
        for n, (src, dst) in enumerate(((grid_ref, grid_out), (proj_ref, proj_out)))
    ]
    for copy in copies:
        copy.start()
    for copy in copies:
        copy.wait()


def on_device(bands, projections, qfunc, species, positions, glist):
    hbm = pl.BlockSpec(memory_space=pltpu.HBM)
    vm = pl.BlockSpec(memory_space=pltpu.VMEM)
    sources = [bands, projections, qfunc, species.reshape(1, ATOMS), positions, glist.reshape(1, NLIST)]
    sources += [jnp.asarray(TABLES[name]) for name in TABLE_NAMES]
    dma = pltpu.SemaphoreType.DMA
    grid, proj = pl.pallas_call(
        kernel,
        out_shape=(jax.ShapeDtypeStruct((N, 1, CHUNK), F32), jax.ShapeDtypeStruct((1, 32), F32)),
        in_specs=[hbm] * len(sources),
        out_specs=(vm, vm),
        scratch_shapes=[
            *[pltpu.VMEM(t.shape, t.dtype) for t in sources],
            pltpu.VMEM((2 + STEPS, XB, LANES), BF16),
            pltpu.VMEM((2 + STEPS, 32, 1296), BF16),
            pltpu.VMEM((2 + STEPS, 16, TAIL), BF16),
            pltpu.VMEM((3 * PK, 2 * NLIST), BF16),
            pltpu.VMEM((NG6 * LOWL, NLIST), BF16),
            pltpu.VMEM((2, ATOMS, NLIST), F32),
            pltpu.VMEM((ATOMS, LG), F32),
            pltpu.VMEM((2 + STEPS, ATOMS, 3 * LG), F32),
            pltpu.VMEM((STEPS, 2 * KL, NG6 * LOWL), F32),
            pltpu.VMEM((STEPS, 2 * KL, NG6 * LOWL), F32),
            pltpu.VMEM((2, XO, LANES), F32),
            pltpu.VMEM((XO, LANES), F32),
            pltpu.VMEM((8, 256), F32),
            pltpu.VMEM((8, 256), F32),
            pltpu.VMEM((8, 56, 128), F32),
            pltpu.VMEM((7, 56, 128), F32),
            dma((len(sources),)),
            *[dma((5,)) for unused in range(4)],
            *[dma((1,)) for unused in range(4)],
            *[dma((7,)) for unused in range(2)],
        ],
        compiler_params=pltpu.CompilerParams(
            collective_id=0, has_side_effects=True, vmem_limit_bytes=60 * 2**20
        ),
    )(*sources)
    grid, proj = pl.pallas_call(
        hand_over,
        out_shape=(jax.ShapeDtypeStruct((N, 1, CHUNK), F32), jax.ShapeDtypeStruct((1, 32), F32)),
        in_specs=[hbm] * 2,
        out_specs=(hbm, hbm),
        scratch_shapes=[dma((2,))],
        compiler_params=pltpu.CompilerParams(vmem_limit_bytes=60 * 2**20),
    )(grid, proj)
    return (jnp.swapaxes(grid, 0, 1), proj)


def solution(mesh):
    return jax.shard_map(
        on_device,
        mesh=mesh,
        in_specs=(P("row", None, None), P("row", None), P(), P(), P(), P()),
        out_specs=(P("row", None, "col"), P("row", "col")),
        check_vma=False,
    )
```

```python
import functools
import math

import jax
import jax.numpy as jnp
import ml_dtypes
import numpy as np
from jax import lax
from jax.experimental import pallas as pl
from jax.experimental.pallas import tpu as pltpu
from jax.sharding import PartitionSpec as P

N = 36
NG6 = 6
LG = 256
LOWL = 128
LANES = NG6 * LG
XB = 48
XO = 40
KL = 24
KR = 40
ATOMS, NH, NSPEC, NLIST = 32, 8, 2, 1024
PK = 80
AUG = N**1.5 / (NH * math.sqrt(ATOMS))
STEPS = 4
TAIL = 384
CHUNK = 162
F32, BF16 = jnp.float32, jnp.bfloat16

ITEMS = [
    [(0, 0, -1, 0), (0, 1, 3, 1), (1, 0, 1, 1), (1, 1, -3, 0)],
    [(0, 0, -1, 1), (0, 1, 3, 0), (1, 0, 1, 0), (1, 1, -3, 1)],
    [(0, 0, 2, 0), (0, 1, -2, 1), (1, 0, -2, 0), (1, 1, 2, 1)],
    [(0, 0, 0, 1), (0, 1, 4, 0), (1, 0, 0, 0), (1, 1, 4, 1)],
]
GIVEN = [[[i for i in items if i[3] == k] for k in range(2)] for items in ITEMS]
TAKEN = [[[i for i in items if i[0] == k] for k in range(2)] for items in ITEMS]


def split_np(a):
    hi = a.astype(np.float32).astype(ml_dtypes.bfloat16)
    lo = (a - hi.astype(np.float64)).astype(np.float32).astype(ml_dtypes.bfloat16)
    return hi, lo


def row_of(pair, kx):
    return 11 * pair + kx if kx <= 10 else KL + 8 * pair + kx - 11


def make_tables():
    k = np.arange(19)[:, None]
    x = np.arange(N)[None, :]
    ang = 2 * np.pi * (k * x % N) / N
    weight = np.where((k == 0) | (k == N // 2), 1.0, 2.0) / N**3
    parts = (np.cos(ang), -np.sin(ang))
    bf = ml_dtypes.bfloat16
    fwd = np.zeros((4 * KR, 4 * XB), bf)
    inv = np.zeros((2 * XO, 6 * KR), bf)
    for pair in range(2):
        for c, part in enumerate(parts):
            fh, fl = split_np(part)
            ih, il = split_np(weight * part)
            for kx in range(19):
                r = c * KR + row_of(pair, kx)
                fwd[r, 96 * pair : 96 * pair + N] = fh[kx]
                fwd[r, 96 * pair + XB : 96 * pair + XB + N] = fh[kx]
                fwd[2 * KR + r, 96 * pair : 96 * pair + N] = fl[kx]
                for b, values in enumerate((ih, ih, il)):
                    inv[XO * pair : XO * pair + N, 2 * KR * b + r] = values[kx]
    r_of = np.repeat(np.arange(6), N)
    z_of = np.tile(np.arange(N), 6)
    near = [(s, kz) for s in (0, 1, 4, 5) for kz in (*range(11), *range(26, 36))]
    order = near + [(s, kz) for s in range(6) for kz in range(N) if (s, kz) not in near]
    s_of = np.array([p[0] for p in order])
    k_of = np.array([p[1] for p in order])
    ang = 2 * np.pi * ((6 * r_of[:, None] * s_of[None, :] + z_of[:, None] * k_of[None, :]) % N) / N
    c = np.zeros((LG, LG))
    s = np.zeros((LG, LG))
    c[:216, :216] = np.cos(ang)
    s[:216, :216] = np.sin(ang)

    def stacked(w):
        hi, lo = split_np(w)
        return np.concatenate([hi, hi, lo], axis=0)

    dft = np.stack([stacked(w) for w in (c, c - s, c + s, c.T, (c + s).T, (c - s).T)])
    tw = np.zeros((16, LG), np.float32)
    for q in range(6):
        a = 2 * np.pi * (r_of * q % N) / N
        tw[q, :216] = np.cos(a)
        tw[8 + q, :216] = -np.sin(a)
    signed = lambda v: np.where(v > N // 2, v - N, v)
    kern = np.zeros((NG6 * KR, LG), np.float32)
    for q in range(6):
        for pair in range(2):
            for kx in range(19):
                n2 = kx**2 + signed(q + 6 * s_of) ** 2 + signed(k_of) ** 2
                kern[q * KR + row_of(pair, kx), :216] = np.where(n2 > 0, N**1.5 / 4 / np.maximum(n2, 1), 0)
    packed = [(s, l, m) for s in range(NSPEC) for l in range(NH) for m in range(l, NH)]
    sel = np.zeros((PK, NSPEC * NH * NH), np.float32)
    rep = np.zeros((NH, 768), np.float32)
    rsum = np.zeros((256, 256), np.float32)
    weight = np.zeros((NSPEC, LG), np.float32)
    kk = np.arange(256) % NH
    k8 = np.arange(NH)
    fold = kk[:, None] == k8[None, :]
    for p, (s, l, m) in enumerate(packed):
        sel[p, s * 64 + l * 8 + m] += 0.5
        sel[p, s * 64 + m * 8 + l] += 0.5
        for b in range(3):
            rep[k8 == l, PK * b + p] = 1
            rep[k8 == m, LG + PK * b + p] = 1
            weight[s, PK * b + p] = 0.5 if l == m else 1.0
        rep[k8 == m, 2 * LG + p] = 1
        rsum[p, kk == l] = 1
        if l != m:
            rep[k8 == l, 2 * LG + PK + p] = 1
            rsum[PK + p, kk == m] = 1
    return dict(
        fwd=fwd, inv=inv, dft=dft, tw=tw, kern=kern, sel=sel.astype(bf), rep=rep.astype(bf), rsum=rsum.astype(bf), fold=fold.astype(bf),
        weight=np.concatenate([weight, np.zeros((6, LG), np.float32)]),
    )


TABLES = make_tables()
TABLE_NAMES = ("fwd", "inv", "dft", "tw", "kern", "sel", "rep", "rsum", "fold", "weight")


def split(a):
    hi = a.astype(BF16)
    return hi, (a - hi.astype(F32)).astype(BF16)


def mm(a, b):
    return jnp.dot(a, b, preferred_element_type=F32)


def mm_nt(a, b):
    return lax.dot_general(a, b, (((1,), (1,)), ((), ())), preferred_element_type=F32)


def dft3(a, b, c, sign):
    h = math.sqrt(3.0) / 2
    sr, si = b[0] + c[0], b[1] + c[1]
    dr, di = (b[0] - c[0]) * h, (b[1] - c[1]) * h
    tr, ti = a[0] - 0.5 * sr, a[1] - 0.5 * si
    zero = (a[0] + sr, a[1] + si)
    minus = (tr + di, ti - dr)
    plus = (tr - di, ti + dr)
    return (zero, minus, plus) if sign < 0 else (zero, plus, minus)


def dft6(v, sign):
    add = lambda p, q: (p[0] + q[0], p[1] + q[1])
    sub = lambda p, q: (p[0] - q[0], p[1] - q[1])
    e = dft3(add(v[0], v[3]), add(v[1], v[4]), add(v[2], v[5]), sign)
    o = dft3(sub(v[0], v[3]), sub(v[4], v[1]), sub(v[2], v[5]), sign)
    return [e[0], o[2], e[1], o[0], e[2], o[1]]


def mm3(x, w):
    hi, lo = split(x)
    return mm(jnp.concatenate([hi, lo, hi], axis=1), w)


def atom_of_lane():
    lane = lax.broadcasted_iota(jnp.int32, (ATOMS, 256), 1)
    return lane // NH == lax.broadcasted_iota(jnp.int32, (ATOMS, 256), 0)


def setup_lists(glist_ref, positions_ref, species_ref, weight_ref, yzt_ref, phase_ref, choose_ref):
    g = glist_ref[...]
    kx = g // (N * N)
    ky = g // N % N
    kz = g % N
    s = ky // 6
    where = (ky % 6) * LOWL + jnp.where(s < 2, s, s - 2) * 21 + jnp.where(kz <= 10, kz, kz - 15)
    step = 256
    for base in range(0, NG6 * LOWL, step):
        rows = lax.broadcasted_iota(jnp.int32, (step, NLIST), 0) + base
        yzt_ref[base : base + step, :] = jnp.where(rows == where, 1.0, 0.0).astype(BF16)
    sg = lambda v: jnp.where(v > N // 2, v - N, v).astype(F32)
    eye = lax.broadcasted_iota(jnp.int32, (ATOMS, ATOMS), 0) == lax.broadcasted_iota(jnp.int32, (ATOMS, ATOMS), 1)
    column = lambda row: jnp.sum(jnp.where(eye, row, 0.0), axis=1, keepdims=True)
    turns = (
        column(positions_ref[0:1, :]) * kx.astype(F32)
        + column(positions_ref[1:2, :]) * sg(ky)
        + column(positions_ref[2:3, :]) * sg(kz)
    )
    theta = (turns - jnp.floor(turns)) * (2.0 * math.pi)
    phase_ref[0] = jnp.cos(theta)
    phase_ref[1] = -jnp.sin(theta)
    spec = column(species_ref[...].astype(F32))
    choose = jnp.zeros((ATOMS, LG), F32)
    for s in range(NSPEC):
        choose = choose + jnp.where(spec == float(s), 1.0, 0.0) * weight_ref[s : s + 1, :]
    choose_ref[...] = choose


def kx_rows(glist_ref):
    kx = glist_ref[...] // (N * N)
    rows = lax.broadcasted_iota(jnp.int32, (KL, NLIST), 0)
    return rows == kx, rows == kx + 11


def augment(n, glist_ref, qz_ref, exp_ref, choose_ref, phase_ref, yzt_ref, faug_ref):
    lane = lax.broadcasted_iota(jnp.int32, (ATOMS, LG), 1)
    middle = jnp.logical_and(lane >= PK, lane < 2 * PK)
    mixed = []
    for t in range(2):
        for i in range(2):
            a, b = exp_ref[i], exp_ref[2 + 2 * n + t]
            full = (a[:, :LG] * b[:, LG : 2 * LG] + b[:, :LG] * a[:, LG : 2 * LG]) * choose_ref[...]
            hi = full.astype(BF16).astype(F32)
            mixed.append(jnp.where(middle, full - hi, hi).astype(BF16)[:, : 3 * PK])
    mixed = jnp.concatenate(mixed, axis=0)
    z_re = mm(mixed, qz_ref[:, :NLIST])
    z_im = mm(mixed, qz_ref[:, NLIST:])
    first, second = kx_rows(glist_ref)
    spread = []
    for t in range(2):
        re, im = [], []
        for i in range(2):
            at = (2 * t + i) * ATOMS
            zr, zi = z_re[at : at + ATOMS], z_im[at : at + ATOMS]
            re.append(jnp.sum(phase_ref[0] * zr - phase_ref[1] * zi, axis=0, keepdims=True) * AUG)
            im.append(jnp.sum(phase_ref[0] * zi + phase_ref[1] * zr, axis=0, keepdims=True) * AUG)
        for rows in (re, im):
            spread.append(jnp.where(first, rows[0], jnp.where(second, rows[1], 0.0)))
    hi, lo = split(jnp.concatenate(spread, axis=0))
    both = jnp.concatenate([hi, lo], axis=0)
    for base in range(0, NG6 * LOWL, LG):
        part = mm_nt(both, yzt_ref[base : base + LG, :])
        part = part[:96] + part[96:]
        for t in range(2):
            faug_ref[2 * n + t, :, base : base + LG] = part[48 * t : 48 * (t + 1)]


def batch(t, band_ref, faug_ref, wst_ref, acc_ref, tabs):
    other = band_ref[2 + t].astype(F32)
    halves = []
    for i in range(2):
        halves += split(band_ref[i].astype(F32) * other)
    out = mm(tabs["fwd"][...], jnp.concatenate(halves, axis=0))
    spec = out[: 2 * KR] + out[2 * KR :]
    v = [(spec[:KR, g * LG : (g + 1) * LG], spec[KR:, g * LG : (g + 1) * LG]) for g in range(NG6)]
    re_rows, im_rows = [], []
    for q, (re, im) in enumerate(dft6(v, -1)):
        if q:
            cr, ci = tabs["tw"][q : q + 1, :], tabs["tw"][8 + q : 9 + q, :]
            re, im = re * cr - im * ci, re * ci + im * cr
        re_rows.append(re)
        im_rows.append(im)
    re, im = jnp.concatenate(re_rows, axis=0), jnp.concatenate(im_rows, axis=0)
    both = mm3(re + im, tabs["dft"][0])
    f = (both - mm3(im, tabs["dft"][1]), both - mm3(re, tabs["dft"][2]))
    w = []
    for c in range(2):
        rows = []
        for q in range(NG6):
            block = f[c][q * KR : (q + 1) * KR]
            kern = tabs["kern"][q * KR : (q + 1) * KR, :]
            low = (block[:KL, :LOWL] + faug_ref[t, c * KL : (c + 1) * KL, q * LOWL : (q + 1) * LOWL]) * kern[:KL, :LOWL]
            wst_ref[t, c * KL : (c + 1) * KL, q * LOWL : (q + 1) * LOWL] = low
            rows.append(jnp.concatenate([low, block[:KL, LOWL:] * kern[:KL, LOWL:]], axis=1))
            rows.append(block[KL:] * kern[KL:])
        w.append(jnp.concatenate(rows, axis=0))
    both = mm3(w[0] + w[1], tabs["dft"][3])
    re, im = both - mm3(w[1], tabs["dft"][4]), both - mm3(w[0], tabs["dft"][5])
    v = []
    for q in range(NG6):
        a, b = re[q * KR : (q + 1) * KR], im[q * KR : (q + 1) * KR]
        if q:
            cr, ci = tabs["tw"][q : q + 1, :], tabs["tw"][8 + q : 9 + q, :]
            a, b = a * cr + b * ci, b * cr - a * ci
        v.append((a, b))
    v = dft6(v, 1)
    w = jnp.concatenate([jnp.concatenate([p[0], p[1]], axis=0) for p in v], axis=1)
    hi, lo = split(w)
    pot = mm(tabs["inv"][...], jnp.concatenate([hi, lo, hi], axis=0))
    acc_ref[0] += pot[:XO] * other[:XO]
    acc_ref[1] += pot[XO:] * other[:XO]


def slopes(n, glist_ref, qz_ref, exp_ref, choose_ref, phase_ref, yzt_ref, wst_ref):
    hi, lo = split(wst_ref[2 * n : 2 * n + 2].reshape(4 * KL, NG6 * LOWL))
    picked = mm(jnp.concatenate([hi, lo], axis=0), yzt_ref[...])
    picked = picked[:96] + picked[96:]
    first, second = kx_rows(glist_ref)
    cross = []
    for t in range(2):
        for mask in (first, second):
            at = t * 2 * KL
            wr = jnp.sum(jnp.where(mask, picked[at : at + KL], 0.0), axis=0, keepdims=True)
            wi = jnp.sum(jnp.where(mask, picked[at + KL : at + 2 * KL], 0.0), axis=0, keepdims=True)
            re = wr * phase_ref[0] + wi * phase_ref[1]
            im = wi * phase_ref[0] - wr * phase_ref[1]
            cross.append(jnp.concatenate([re, im], axis=1))
    hi, lo = split(jnp.concatenate(cross, axis=0))
    full = mm_nt(jnp.concatenate([hi, lo], axis=0), qz_ref[...])
    high, low = full[:128], full[128:]
    rest = high[:, 2 * PK :]
    slope = (high[:, : 2 * PK] + low[:, : 2 * PK] + jnp.concatenate([rest, rest], axis=1)) * (2.0 * AUG / N**3)
    slope = jnp.concatenate([slope, jnp.zeros((128, LG - 2 * PK), F32)], axis=1)
    chosen = jnp.where(choose_ref[...] > 0.0, 1.0, 0.0)
    sums = []
    for i in range(2):
        total = jnp.zeros((ATOMS, LG), F32)
        for t in range(2):
            at = (2 * t + i) * ATOMS
            total = total + slope[at : at + ATOMS] * exp_ref[2 + 2 * n + t][:, 2 * LG :]
        sums.append(total * chosen)
    return sums


def coef_row(packed, rsum):
    hi, lo = split(packed)
    full = mm(hi, rsum) + mm(lo, rsum)
    return jnp.sum(jnp.where(atom_of_lane(), full, 0.0), axis=0, keepdims=True)


def pack_tail(rows, coefs):
    rows = jnp.concatenate([rows[:, 324 * j : 324 * (j + 1)] for j in range(4)], axis=0)
    return jnp.concatenate([rows, coefs[:16], coefs[16:], jnp.zeros((16, TAIL - 340), F32)], axis=1)


def tail_coefs(tail):
    return jnp.concatenate([tail[:, 324:332], tail[:, 332:340]], axis=0)


def spread_band(main, tail):
    rows = jnp.concatenate([tail[4 * j : 4 * (j + 1), :324] for j in range(4)], axis=1)
    full = jnp.concatenate([main, rows, jnp.zeros((12, 1296), F32)], axis=0)
    zero = jnp.zeros((XB, LG - 216), F32)
    return jnp.concatenate([p for g in range(NG6) for p in (full[:, 216 * g : 216 * (g + 1)], zero)], axis=1)


def columns(total, c):
    start = CHUNK * c
    parts = []
    while start < CHUNK * (c + 1):
        g, at = divmod(start, 216)
        end = min(216 * (g + 1), CHUNK * (c + 1))
        parts.append(total[:, g * LG + at : g * LG + at + end - start])
        start = end
    return parts[0] if len(parts) == 1 else jnp.concatenate(parts, axis=1)


def pack_chunk(total, c):
    part = columns(total, c)
    main = part[:, :128]
    rest = part[:, 128:]
    last = jnp.concatenate([rest[32:40], jnp.zeros((8, 34), F32)], axis=0)
    rest = jnp.concatenate([rest[:16], rest[16:32], last, jnp.zeros((16, 26), F32)], axis=1)
    return jnp.concatenate([main, rest], axis=0)


def kernel(*refs):
    nt = len(TABLE_NAMES)
    sources = refs[: 6 + nt]
    out_ref, proj_ref = refs[6 + nt : 8 + nt]
    scratch = refs[8 + nt :]
    bands_ref, coef_ref, q_ref, species_ref, positions_ref, glist_ref = scratch[:6]
    tabs = dict(zip(TABLE_NAMES, scratch[6 : 6 + nt]))
    (band_ref, raw_ref, tail_ref, qz_ref, yzt_ref, phase_ref, choose_ref, exp_ref, faug_ref, wst_ref,
     acc_ref, got_ref, pgive_ref, pgot_ref, chunk_ref, chunks_ref,
     load_sem, tail_send, tail_recv, band_send, band_recv, sum_send, sum_recv, coef_send, coef_recv,
     chunk_send, chunk_recv) = scratch[6 + nt :]
    row, col = lax.axis_index("row"), lax.axis_index("col")
    zed, wide, core = row // 8, row // 2 % 4, row % 2

    far_side = col % 2

    def pick(table, m, e):
        return sum(
            jnp.where(jnp.logical_and(col // 2 == c, core == k), table[c][k][m][e], 0) for c in range(4) for k in range(2)
        )

    def at(dz, dy, k):
        return (((zed + dz + 16) % 8 * 4 + (wide + dy + 8) % 4) * 2 + k, col)

    sibling = at(0, 0, 1 - core)
    partner = (at(0, 2 * far_side - 1, core)[0], col + 1 - 2 * far_side)
    targets, origins = [], []
    for m in range(2):
        k = pick(GIVEN, m, 0)
        targets.append((at(-pick(GIVEN, m, 2), k + far_side - 1, k), pick(GIVEN, m, 1)))
        origins.append(at(pick(TAKEN, m, 2), 1 - core - far_side, pick(TAKEN, m, 3)))
    peers = [(row, (col + step) % 8) for step in range(1, 8)]
    mesh_id = pl.DeviceIdType.MESH

    barrier = pltpu.get_barrier_semaphore()

    def greet(partner):
        pl.semaphore_signal(barrier, inc=1, device_id=partner, device_id_type=mesh_id)

    others = origins + [sibling, partner] + peers
    for other in others:
        greet(other)

    names = ("bands", "projections", "qfunc", "species", "positions", "glist", *TABLE_NAMES)
    loads = [
        pltpu.make_async_copy(src, dst, load_sem.at[n]) for n, (src, dst) in enumerate(zip(sources, scratch[: 6 + nt]))
    ]
    for load in loads:
        load.start()

    def remote(src, dst, to, sems, recvs, n, m=None):
        return pltpu.make_async_remote_copy(
            src_ref=src, dst_ref=dst, send_sem=sems.at[n], recv_sem=recvs.at[n if m is None else m],
            device_id=to, device_id_type=mesh_id,
        )

    loads[0].wait()
    loads[1].wait()
    loads[names.index("fold")].wait()
    own = jnp.where(atom_of_lane(), coef_ref[...].astype(F32), 0.0).astype(BF16)
    tail_ref[0] = pack_tail(bands_ref[0].astype(F32)[32:36], mm(own, tabs["fold"][...])).astype(BF16)
    main = bands_ref.at[0, pl.ds(0, 32)]

    pl.semaphore_wait(barrier, len(others))
    tails = [remote(tail_ref.at[0], tail_ref.at[1], sibling, tail_send, tail_recv, 4)]
    fields = [remote(main, raw_ref.at[1], sibling, band_send, band_recv, 4)]
    for m, (to, t) in enumerate(targets):
        tails.append(remote(tail_ref.at[0], tail_ref.at[2 + t], to, tail_send, tail_recv, m, t))
        fields.append(remote(main, raw_ref.at[2 + t], to, band_send, band_recv, m, t))
    for copy in tails + fields:
        copy.start()

    for n, load in enumerate(loads):
        if n > 1 and names[n] != "fold":
            load.wait()
    setup_lists(glist_ref, positions_ref, species_ref, tabs["weight"], yzt_ref, phase_ref, choose_ref)
    acc_ref[...] = jnp.zeros_like(acc_ref)
    for c in range(2):
        hi, lo = split(q_ref[c].reshape(NSPEC * NH * NH, NLIST))
        packed = mm(tabs["sel"][...], hi) + mm(tabs["sel"][...], lo)
        hi, lo = split(packed)
        qz_ref[:, c * NLIST : (c + 1) * NLIST] = jnp.concatenate([hi, hi, lo], axis=0)

    def arrived(which, ref, recvs, n):
        pltpu.make_async_remote_copy(
            src_ref=which, dst_ref=ref, send_sem=recvs.at[n], recv_sem=recvs.at[n], device_id=sibling,
            device_id_type=mesh_id,
        ).wait_recv()

    def unpack(b):
        band_ref[b] = spread_band(raw_ref[b].astype(F32), tail_ref[b].astype(F32)).astype(BF16)

    def expand(b):
        exp_ref[b] = mm(tail_coefs(tail_ref[b].astype(F32)).astype(BF16), tabs["rep"][...])

    raw_ref[0] = bands_ref[0, 0:32, :]
    unpack(0)
    expand(0)
    arrived(tail_ref.at[0], tail_ref.at[1], tail_recv, 4)
    expand(1)
    arrived(main, raw_ref.at[1], band_recv, 4)
    unpack(1)

    def relay(t, ref, sends, recvs):
        copy = remote(ref.at[2 + t], ref.at[4 + t], partner, sends, recvs, 2 + t)
        copy.start()
        return copy

    def step(t, carry):
        arrived(main, raw_ref.at[2 + t], band_recv, t)
        if isinstance(t, int):
            fields.append(relay(t, raw_ref, band_send, band_recv))
        unpack(2 + t)
        batch(t, band_ref, faug_ref, wst_ref, acc_ref, tabs)
        return carry

    sums = []
    for n in range(2):
        for t in (2 * n, 2 * n + 1):
            arrived(tail_ref.at[0], tail_ref.at[2 + t], tail_recv, t)
            if n == 0:
                tails.append(relay(t, tail_ref, tail_send, tail_recv))
            expand(2 + t)
        augment(n, glist_ref, qz_ref, exp_ref, choose_ref, phase_ref, yzt_ref, faug_ref)
        if n == 0:
            step(0, 0)
            step(1, 0)
            sums.append(slopes(n, glist_ref, qz_ref, exp_ref, choose_ref, phase_ref, yzt_ref, wst_ref))
        else:
            lax.fori_loop(2, 4, step, 0)
    give = remote(acc_ref.at[1], got_ref, sibling, sum_send, sum_recv, 0)
    give.start()
    sums.append(slopes(1, glist_ref, qz_ref, exp_ref, choose_ref, phase_ref, yzt_ref, wst_ref))
    rows = [coef_row(sums[0][i] + sums[1][i], tabs["rsum"][...]) for i in range(2)]
    pgive_ref[...] = jnp.broadcast_to(rows[1], (8, 256))
    coefs = remote(pgive_ref, pgot_ref, sibling, coef_send, coef_recv, 0)
    coefs.start()
    give.wait_recv()
    total = acc_ref[0] + got_ref[...]
    for c in range(8):
        chunk_ref[c] = pack_chunk(total, c)
    coefs.wait_recv()
    proj = rows[0] + pgot_ref[0:1, :]
    for c in range(8):
        chunk_ref[c, N : N + 1, 0:32] = proj[:, 32 * c : 32 * (c + 1)]
    chunks = []
    for n, to in enumerate(peers):
        chunks.append(remote(chunk_ref.at[to[1]], chunks_ref.at[n], to, chunk_send, chunk_recv, n))
        chunks[-1].start()
    whole = chunk_ref[col]
    for n, copy in enumerate(chunks):
        copy.wait_recv()
        whole = whole + chunks_ref[n]
    whole = whole * -0.5
    out_ref[:, 0, 0:128] = whole[:N]
    out_ref[0:16, 0, 128:CHUNK] = whole[40:56, 0:34]
    out_ref[16:32, 0, 128:CHUNK] = whole[40:56, 34:68]
    out_ref[32:36, 0, 128:CHUNK] = whole[40:44, 68:102]
    proj_ref[...] = whole[N : N + 1, 0:32]
    for copy in tails + fields + [give, coefs] + chunks:
        copy.wait_send()


def hand_over(grid_ref, proj_ref, grid_out, proj_out, sem):
    copies = [
        pltpu.make_async_copy(src, dst, sem.at[n])
        for n, (src, dst) in enumerate(((grid_ref, grid_out), (proj_ref, proj_out)))
    ]
    for copy in copies:
        copy.start()
    for copy in copies:
        copy.wait()


def on_device(bands, projections, qfunc, species, positions, glist):
    hbm = pl.BlockSpec(memory_space=pltpu.HBM)
    vm = pl.BlockSpec(memory_space=pltpu.VMEM)
    sources = [bands, projections, qfunc, species.reshape(1, ATOMS), positions, glist.reshape(1, NLIST)]
    sources += [jnp.asarray(TABLES[name]) for name in TABLE_NAMES]
    dma = pltpu.SemaphoreType.DMA
    grid, proj = pl.pallas_call(
        kernel,
        out_shape=(jax.ShapeDtypeStruct((N, 1, CHUNK), F32), jax.ShapeDtypeStruct((1, 32), F32)),
        in_specs=[hbm] * len(sources),
        out_specs=(vm, vm),
        scratch_shapes=[
            *[pltpu.VMEM(t.shape, t.dtype) for t in sources],
            pltpu.VMEM((2 + STEPS, XB, LANES), BF16),
            pltpu.VMEM((2 + STEPS, 32, 1296), BF16),
            pltpu.VMEM((2 + STEPS, 16, TAIL), BF16),
            pltpu.VMEM((3 * PK, 2 * NLIST), BF16),
            pltpu.VMEM((NG6 * LOWL, NLIST), BF16),
            pltpu.VMEM((2, ATOMS, NLIST), F32),
            pltpu.VMEM((ATOMS, LG), F32),
            pltpu.VMEM((2 + STEPS, ATOMS, 3 * LG), F32),
            pltpu.VMEM((STEPS, 2 * KL, NG6 * LOWL), F32),
            pltpu.VMEM((STEPS, 2 * KL, NG6 * LOWL), F32),
            pltpu.VMEM((2, XO, LANES), F32),
            pltpu.VMEM((XO, LANES), F32),
            pltpu.VMEM((8, 256), F32),
            pltpu.VMEM((8, 256), F32),
            pltpu.VMEM((8, 56, 128), F32),
            pltpu.VMEM((7, 56, 128), F32),
            dma((len(sources),)),
            *[dma((5,)) for unused in range(4)],
            *[dma((1,)) for unused in range(4)],
            *[dma((7,)) for unused in range(2)],
        ],
        compiler_params=pltpu.CompilerParams(
            collective_id=0, has_side_effects=True, vmem_limit_bytes=60 * 2**20
        ),
    )(*sources)
    grid, proj = pl.pallas_call(
        hand_over,
        out_shape=(jax.ShapeDtypeStruct((N, 1, CHUNK), F32), jax.ShapeDtypeStruct((1, 32), F32)),
        in_specs=[hbm] * 2,
        out_specs=(hbm, hbm),
        scratch_shapes=[dma((2,))],
        compiler_params=pltpu.CompilerParams(vmem_limit_bytes=60 * 2**20),
    )(grid, proj)
    return (jnp.swapaxes(grid, 0, 1), proj)


def solution(mesh):
    return jax.shard_map(
        on_device,
        mesh=mesh,
        in_specs=(P("row", None, None), P("row", None), P(), P(), P(), P()),
        out_specs=(P("row", None, "col"), P("row", "col")),
        check_vma=False,
    )
```

```python
import functools
import math

import jax
import jax.numpy as jnp
import ml_dtypes
import numpy as np
from jax import lax
from jax.experimental import pallas as pl
from jax.experimental.pallas import tpu as pltpu
from jax.sharding import PartitionSpec as P

N = 36
NG6 = 6
LG = 256
LOWL = 128
LANES = NG6 * LG
XB = 48
XO = 40
KL = 24
KR = 40
ATOMS, NH, NSPEC, NLIST = 32, 8, 2, 1024
PK = 80
AUG = N**1.5 / (NH * math.sqrt(ATOMS))
STEPS = 4
TAIL = 384
CHUNK = 162
F32, BF16 = jnp.float32, jnp.bfloat16

ITEMS = [
    [(0, 0, -1, 0), (0, 1, 3, 1), (1, 0, 1, 1), (1, 1, -3, 0)],
    [(0, 0, -1, 1), (0, 1, 3, 0), (1, 0, 1, 0), (1, 1, -3, 1)],
    [(0, 0, 2, 0), (0, 1, -2, 1), (1, 0, -2, 0), (1, 1, 2, 1)],
    [(0, 0, 0, 1), (0, 1, 4, 0), (1, 0, 0, 0), (1, 1, 4, 1)],
]
GIVEN = [[[i for i in items if i[3] == k] for k in range(2)] for items in ITEMS]
TAKEN = [[[i for i in items if i[0] == k] for k in range(2)] for items in ITEMS]


def split_np(a):
    hi = a.astype(np.float32).astype(ml_dtypes.bfloat16)
    lo = (a - hi.astype(np.float64)).astype(np.float32).astype(ml_dtypes.bfloat16)
    return hi, lo


def row_of(pair, kx):
    return 11 * pair + kx if kx <= 10 else KL + 8 * pair + kx - 11


def make_tables():
    k = np.arange(19)[:, None]
    x = np.arange(N)[None, :]
    ang = 2 * np.pi * (k * x % N) / N
    weight = np.where((k == 0) | (k == N // 2), 1.0, 2.0) / N**3
    parts = (np.cos(ang), -np.sin(ang))
    bf = ml_dtypes.bfloat16
    fwd = np.zeros((4 * KR, 4 * XB), bf)
    inv = np.zeros((2 * XO, 6 * KR), bf)
    for pair in range(2):
        for c, part in enumerate(parts):
            fh, fl = split_np(part)
            ih, il = split_np(weight * part)
            for kx in range(19):
                r = c * KR + row_of(pair, kx)
                fwd[r, 96 * pair : 96 * pair + N] = fh[kx]
                fwd[r, 96 * pair + XB : 96 * pair + XB + N] = fh[kx]
                fwd[2 * KR + r, 96 * pair : 96 * pair + N] = fl[kx]
                for b, values in enumerate((ih, ih, il)):
                    inv[XO * pair : XO * pair + N, 2 * KR * b + r] = values[kx]
    r_of = np.repeat(np.arange(6), N)
    z_of = np.tile(np.arange(N), 6)
    near = [(s, kz) for s in (0, 1, 4, 5) for kz in (*range(11), *range(26, 36))]
    order = near + [(s, kz) for s in range(6) for kz in range(N) if (s, kz) not in near]
    s_of = np.array([p[0] for p in order])
    k_of = np.array([p[1] for p in order])
    ang = 2 * np.pi * ((6 * r_of[:, None] * s_of[None, :] + z_of[:, None] * k_of[None, :]) % N) / N
    c = np.zeros((LG, LG))
    s = np.zeros((LG, LG))
    c[:216, :216] = np.cos(ang)
    s[:216, :216] = np.sin(ang)

    def stacked(w):
        hi, lo = split_np(w)
        return np.concatenate([hi, hi, lo], axis=0)

    dft = np.stack([stacked(w) for w in (c, c - s, c + s, c.T, (c + s).T, (c - s).T)])
    tw = np.zeros((16, LG), np.float32)
    for q in range(6):
        a = 2 * np.pi * (r_of * q % N) / N
        tw[q, :216] = np.cos(a)
        tw[8 + q, :216] = -np.sin(a)
    signed = lambda v: np.where(v > N // 2, v - N, v)
    kern = np.zeros((NG6 * KR, LG), np.float32)
    for q in range(6):
        for pair in range(2):
            for kx in range(19):
                n2 = kx**2 + signed(q + 6 * s_of) ** 2 + signed(k_of) ** 2
                kern[q * KR + row_of(pair, kx), :216] = np.where(n2 > 0, N**1.5 / 4 / np.maximum(n2, 1), 0)
    packed = [(s, l, m) for s in range(NSPEC) for l in range(NH) for m in range(l, NH)]
    sel = np.zeros((PK, NSPEC * NH * NH), np.float32)
    rep = np.zeros((NH, 768), np.float32)
    rsum = np.zeros((256, 256), np.float32)
    weight = np.zeros((NSPEC, LG), np.float32)
    kk = np.arange(256) % NH
    k8 = np.arange(NH)
    fold = kk[:, None] == k8[None, :]
    for p, (s, l, m) in enumerate(packed):
        sel[p, s * 64 + l * 8 + m] += 0.5
        sel[p, s * 64 + m * 8 + l] += 0.5
        for b in range(3):
            rep[k8 == l, PK * b + p] = 1
            rep[k8 == m, LG + PK * b + p] = 1
            weight[s, PK * b + p] = 0.5 if l == m else 1.0
        rep[k8 == m, 2 * LG + p] = 1
        rsum[p, kk == l] = 1
        if l != m:
            rep[k8 == l, 2 * LG + PK + p] = 1
            rsum[PK + p, kk == m] = 1
    return dict(
        fwd=fwd, inv=inv, dft=dft, tw=tw, kern=kern, sel=sel.astype(bf), rep=rep.astype(bf), rsum=rsum.astype(bf), fold=fold.astype(bf),
        weight=np.concatenate([weight, np.zeros((6, LG), np.float32)]),
    )


TABLES = make_tables()
TABLE_NAMES = ("fwd", "inv", "dft", "tw", "kern", "sel", "rep", "rsum", "fold", "weight")


def split(a):
    hi = a.astype(BF16)
    return hi, (a - hi.astype(F32)).astype(BF16)


def mm(a, b):
    return jnp.dot(a, b, preferred_element_type=F32)


def mm_nt(a, b):
    return lax.dot_general(a, b, (((1,), (1,)), ((), ())), preferred_element_type=F32)


def dft3(a, b, c, sign):
    h = math.sqrt(3.0) / 2
    sr, si = b[0] + c[0], b[1] + c[1]
    dr, di = (b[0] - c[0]) * h, (b[1] - c[1]) * h
    tr, ti = a[0] - 0.5 * sr, a[1] - 0.5 * si
    zero = (a[0] + sr, a[1] + si)
    minus = (tr + di, ti - dr)
    plus = (tr - di, ti + dr)
    return (zero, minus, plus) if sign < 0 else (zero, plus, minus)


def dft6(v, sign):
    add = lambda p, q: (p[0] + q[0], p[1] + q[1])
    sub = lambda p, q: (p[0] - q[0], p[1] - q[1])
    e = dft3(add(v[0], v[3]), add(v[1], v[4]), add(v[2], v[5]), sign)
    o = dft3(sub(v[0], v[3]), sub(v[4], v[1]), sub(v[2], v[5]), sign)
    return [e[0], o[2], e[1], o[0], e[2], o[1]]


def mm3(x, w):
    hi, lo = split(x)
    return mm(jnp.concatenate([hi, lo, hi], axis=1), w)


def atom_of_lane():
    lane = lax.broadcasted_iota(jnp.int32, (ATOMS, 256), 1)
    return lane // NH == lax.broadcasted_iota(jnp.int32, (ATOMS, 256), 0)


def setup_lists(glist_ref, positions_ref, species_ref, weight_ref, yzt_ref, phase_ref, choose_ref):
    g = glist_ref[...]
    kx = g // (N * N)
    ky = g // N % N
    kz = g % N
    s = ky // 6
    where = (ky % 6) * LOWL + jnp.where(s < 2, s, s - 2) * 21 + jnp.where(kz <= 10, kz, kz - 15)
    step = 256
    for base in range(0, NG6 * LOWL, step):
        rows = lax.broadcasted_iota(jnp.int32, (step, NLIST), 0) + base
        yzt_ref[base : base + step, :] = jnp.where(rows == where, 1.0, 0.0).astype(BF16)
    sg = lambda v: jnp.where(v > N // 2, v - N, v).astype(F32)
    eye = lax.broadcasted_iota(jnp.int32, (ATOMS, ATOMS), 0) == lax.broadcasted_iota(jnp.int32, (ATOMS, ATOMS), 1)
    column = lambda row: jnp.sum(jnp.where(eye, row, 0.0), axis=1, keepdims=True)
    turns = (
        column(positions_ref[0:1, :]) * kx.astype(F32)
        + column(positions_ref[1:2, :]) * sg(ky)
        + column(positions_ref[2:3, :]) * sg(kz)
    )
    theta = (turns - jnp.floor(turns)) * (2.0 * math.pi)
    phase_ref[0] = jnp.cos(theta)
    phase_ref[1] = -jnp.sin(theta)
    spec = column(species_ref[...].astype(F32))
    choose = jnp.zeros((ATOMS, LG), F32)
    for s in range(NSPEC):
        choose = choose + jnp.where(spec == float(s), 1.0, 0.0) * weight_ref[s : s + 1, :]
    choose_ref[...] = choose


def kx_rows(glist_ref):
    kx = glist_ref[...] // (N * N)
    rows = lax.broadcasted_iota(jnp.int32, (KL, NLIST), 0)
    return rows == kx, rows == kx + 11


def augment(n, glist_ref, qz_ref, exp_ref, choose_ref, phase_ref, yzt_ref, faug_ref):
    lane = lax.broadcasted_iota(jnp.int32, (ATOMS, LG), 1)
    middle = jnp.logical_and(lane >= PK, lane < 2 * PK)
    mixed = []
    for t in range(2):
        for i in range(2):
            a, b = exp_ref[i], exp_ref[2 + 2 * n + t]
            full = (a[:, :LG] * b[:, LG : 2 * LG] + b[:, :LG] * a[:, LG : 2 * LG]) * choose_ref[...]
            hi = full.astype(BF16).astype(F32)
            mixed.append(jnp.where(middle, full - hi, hi).astype(BF16)[:, : 3 * PK])
    mixed = jnp.concatenate(mixed, axis=0)
    z_re = mm(mixed, qz_ref[:, :NLIST])
    z_im = mm(mixed, qz_ref[:, NLIST:])
    first, second = kx_rows(glist_ref)
    spread = []
    for t in range(2):
        re, im = [], []
        for i in range(2):
            at = (2 * t + i) * ATOMS
            zr, zi = z_re[at : at + ATOMS], z_im[at : at + ATOMS]
            re.append(jnp.sum(phase_ref[0] * zr - phase_ref[1] * zi, axis=0, keepdims=True) * AUG)
            im.append(jnp.sum(phase_ref[0] * zi + phase_ref[1] * zr, axis=0, keepdims=True) * AUG)
        for rows in (re, im):
            spread.append(jnp.where(first, rows[0], jnp.where(second, rows[1], 0.0)))
    hi, lo = split(jnp.concatenate(spread, axis=0))
    both = jnp.concatenate([hi, lo], axis=0)
    for base in range(0, NG6 * LOWL, LG):
        part = mm_nt(both, yzt_ref[base : base + LG, :])
        part = part[:96] + part[96:]
        for t in range(2):
            faug_ref[2 * n + t, :, base : base + LG] = part[48 * t : 48 * (t + 1)]


def batch(t, band_ref, faug_ref, wst_ref, acc_ref, tabs):
    other = band_ref[2 + t].astype(F32)
    halves = []
    for i in range(2):
        halves += split(band_ref[i].astype(F32) * other)
    out = mm(tabs["fwd"][...], jnp.concatenate(halves, axis=0))
    spec = out[: 2 * KR] + out[2 * KR :]
    v = [(spec[:KR, g * LG : (g + 1) * LG], spec[KR:, g * LG : (g + 1) * LG]) for g in range(NG6)]
    re_rows, im_rows = [], []
    for q, (re, im) in enumerate(dft6(v, -1)):
        if q:
            cr, ci = tabs["tw"][q : q + 1, :], tabs["tw"][8 + q : 9 + q, :]
            re, im = re * cr - im * ci, re * ci + im * cr
        re_rows.append(re)
        im_rows.append(im)
    re, im = jnp.concatenate(re_rows, axis=0), jnp.concatenate(im_rows, axis=0)
    both = mm3(re + im, tabs["dft"][0])
    f = (both - mm3(im, tabs["dft"][1]), both - mm3(re, tabs["dft"][2]))
    w = []
    for c in range(2):
        rows = []
        for q in range(NG6):
            block = f[c][q * KR : (q + 1) * KR]
            kern = tabs["kern"][q * KR : (q + 1) * KR, :]
            low = (block[:KL, :LOWL] + faug_ref[t, c * KL : (c + 1) * KL, q * LOWL : (q + 1) * LOWL]) * kern[:KL, :LOWL]
            wst_ref[t, c * KL : (c + 1) * KL, q * LOWL : (q + 1) * LOWL] = low
            rows.append(jnp.concatenate([low, block[:KL, LOWL:] * kern[:KL, LOWL:]], axis=1))
            rows.append(block[KL:] * kern[KL:])
        w.append(jnp.concatenate(rows, axis=0))
    both = mm3(w[0] + w[1], tabs["dft"][3])
    re, im = both - mm3(w[1], tabs["dft"][4]), both - mm3(w[0], tabs["dft"][5])
    v = []
    for q in range(NG6):
        a, b = re[q * KR : (q + 1) * KR], im[q * KR : (q + 1) * KR]
        if q:
            cr, ci = tabs["tw"][q : q + 1, :], tabs["tw"][8 + q : 9 + q, :]
            a, b = a * cr + b * ci, b * cr - a * ci
        v.append((a, b))
    v = dft6(v, 1)
    w = jnp.concatenate([jnp.concatenate([p[0], p[1]], axis=0) for p in v], axis=1)
    hi, lo = split(w)
    pot = mm(tabs["inv"][...], jnp.concatenate([hi, lo, hi], axis=0))
    acc_ref[0] += pot[:XO] * other[:XO]
    acc_ref[1] += pot[XO:] * other[:XO]


def slopes(n, glist_ref, qz_ref, exp_ref, choose_ref, phase_ref, yzt_ref, wst_ref):
    hi, lo = split(wst_ref[2 * n : 2 * n + 2].reshape(4 * KL, NG6 * LOWL))
    picked = mm(jnp.concatenate([hi, lo], axis=0), yzt_ref[...])
    picked = picked[:96] + picked[96:]
    first, second = kx_rows(glist_ref)
    cross = []
    for t in range(2):
        for mask in (first, second):
            at = t * 2 * KL
            wr = jnp.sum(jnp.where(mask, picked[at : at + KL], 0.0), axis=0, keepdims=True)
            wi = jnp.sum(jnp.where(mask, picked[at + KL : at + 2 * KL], 0.0), axis=0, keepdims=True)
            re = wr * phase_ref[0] + wi * phase_ref[1]
            im = wi * phase_ref[0] - wr * phase_ref[1]
            cross.append(jnp.concatenate([re, im], axis=1))
    hi, lo = split(jnp.concatenate(cross, axis=0))
    full = mm_nt(jnp.concatenate([hi, lo], axis=0), qz_ref[...])
    high, low = full[:128], full[128:]
    rest = high[:, 2 * PK :]
    slope = (high[:, : 2 * PK] + low[:, : 2 * PK] + jnp.concatenate([rest, rest], axis=1)) * (2.0 * AUG / N**3)
    slope = jnp.concatenate([slope, jnp.zeros((128, LG - 2 * PK), F32)], axis=1)
    chosen = jnp.where(choose_ref[...] > 0.0, 1.0, 0.0)
    sums = []
    for i in range(2):
        total = jnp.zeros((ATOMS, LG), F32)
        for t in range(2):
            at = (2 * t + i) * ATOMS
            total = total + slope[at : at + ATOMS] * exp_ref[2 + 2 * n + t][:, 2 * LG :]
        sums.append(total * chosen)
    return sums


def coef_row(packed, rsum):
    hi, lo = split(packed)
    full = mm(hi, rsum) + mm(lo, rsum)
    return jnp.sum(jnp.where(atom_of_lane(), full, 0.0), axis=0, keepdims=True)


def pack_tail(rows, coefs):
    rows = jnp.concatenate([rows[:, 324 * j : 324 * (j + 1)] for j in range(4)], axis=0)
    return jnp.concatenate([rows, coefs[:16], coefs[16:], jnp.zeros((16, TAIL - 340), F32)], axis=1)


def tail_coefs(tail):
    return jnp.concatenate([tail[:, 324:332], tail[:, 332:340]], axis=0)


def spread_band(main, tail):
    rows = jnp.concatenate([tail[4 * j : 4 * (j + 1), :324] for j in range(4)], axis=1)
    full = jnp.concatenate([main, rows, jnp.zeros((12, 1296), F32)], axis=0)
    zero = jnp.zeros((XB, LG - 216), F32)
    return jnp.concatenate([p for g in range(NG6) for p in (full[:, 216 * g : 216 * (g + 1)], zero)], axis=1)


def columns(total, c):
    start = CHUNK * c
    parts = []
    while start < CHUNK * (c + 1):
        g, at = divmod(start, 216)
        end = min(216 * (g + 1), CHUNK * (c + 1))
        parts.append(total[:, g * LG + at : g * LG + at + end - start])
        start = end
    return parts[0] if len(parts) == 1 else jnp.concatenate(parts, axis=1)


def pack_chunk(total, c):
    part = columns(total, c)
    main = part[:, :128]
    rest = part[:, 128:]
    last = jnp.concatenate([rest[32:40], jnp.zeros((8, 34), F32)], axis=0)
    rest = jnp.concatenate([rest[:16], rest[16:32], last, jnp.zeros((16, 26), F32)], axis=1)
    return jnp.concatenate([main, rest], axis=0)


def kernel(*refs):
    nt = len(TABLE_NAMES)
    sources = refs[: 6 + nt]
    out_ref, proj_ref = refs[6 + nt : 8 + nt]
    scratch = refs[8 + nt :]
    bands_ref, coef_ref, q_ref, species_ref, positions_ref, glist_ref = scratch[:6]
    tabs = dict(zip(TABLE_NAMES, scratch[6 : 6 + nt]))
    (band_ref, raw_ref, tail_ref, qz_ref, yzt_ref, phase_ref, choose_ref, exp_ref, faug_ref, wst_ref,
     acc_ref, got_ref, pgive_ref, pgot_ref, chunk_ref, chunks_ref,
     load_sem, tail_send, tail_recv, band_send, band_recv, sum_send, sum_recv, coef_send, coef_recv,
     chunk_send, chunk_recv) = scratch[6 + nt :]
    row, col = lax.axis_index("row"), lax.axis_index("col")
    zed, wide, core = row // 8, row // 2 % 4, row % 2

    far_side = col % 2

    def pick(table, m, e):
        return sum(
            jnp.where(jnp.logical_and(col // 2 == c, core == k), table[c][k][m][e], 0) for c in range(4) for k in range(2)
        )

    def at(dz, dy, k):
        return (((zed + dz + 16) % 8 * 4 + (wide + dy + 8) % 4) * 2 + k, col)

    sibling = at(0, 0, 1 - core)
    partner = (at(0, 2 * far_side - 1, core)[0], col + 1 - 2 * far_side)
    targets, origins = [], []
    for m in range(2):
        k = pick(GIVEN, m, 0)
        targets.append((at(-pick(GIVEN, m, 2), k + far_side - 1, k), pick(GIVEN, m, 1)))
        origins.append(at(pick(TAKEN, m, 2), 1 - core - far_side, pick(TAKEN, m, 3)))
    peers = [(row, (col + step) % 8) for step in range(1, 8)]
    mesh_id = pl.DeviceIdType.MESH

    barrier = pltpu.get_barrier_semaphore()

    def greet(partner):
        pl.semaphore_signal(barrier, inc=1, device_id=partner, device_id_type=mesh_id)

    others = origins + [sibling, partner] + peers
    for other in others:
        greet(other)

    names = ("bands", "projections", "qfunc", "species", "positions", "glist", *TABLE_NAMES)
    loads = [
        pltpu.make_async_copy(src, dst, load_sem.at[n]) for n, (src, dst) in enumerate(zip(sources, scratch[: 6 + nt]))
    ]
    for load in loads:
        load.start()

    def remote(src, dst, to, sems, recvs, n, m=None):
        return pltpu.make_async_remote_copy(
            src_ref=src, dst_ref=dst, send_sem=sems.at[n], recv_sem=recvs.at[n if m is None else m],
            device_id=to, device_id_type=mesh_id,
        )

    loads[0].wait()
    loads[1].wait()
    loads[names.index("fold")].wait()
    own = jnp.where(atom_of_lane(), coef_ref[...].astype(F32), 0.0).astype(BF16)
    tail_ref[0] = pack_tail(bands_ref[0].astype(F32)[32:36], mm(own, tabs["fold"][...])).astype(BF16)
    main = bands_ref.at[0, pl.ds(0, 32)]

    pl.semaphore_wait(barrier, len(others))
    tails = [remote(tail_ref.at[0], tail_ref.at[1], sibling, tail_send, tail_recv, 4)]
    fields = [remote(main, raw_ref.at[1], sibling, band_send, band_recv, 4)]
    for m, (to, t) in enumerate(targets):
        tails.append(remote(tail_ref.at[0], tail_ref.at[2 + t], to, tail_send, tail_recv, m, t))
        fields.append(remote(main, raw_ref.at[2 + t], to, band_send, band_recv, m, t))
    for copy in tails + fields:
        copy.start()

    for n, load in enumerate(loads):
        if n > 1 and names[n] != "fold":
            load.wait()
    setup_lists(glist_ref, positions_ref, species_ref, tabs["weight"], yzt_ref, phase_ref, choose_ref)
    acc_ref[...] = jnp.zeros_like(acc_ref)
    for c in range(2):
        hi, lo = split(q_ref[c].reshape(NSPEC * NH * NH, NLIST))
        packed = mm(tabs["sel"][...], hi) + mm(tabs["sel"][...], lo)
        hi, lo = split(packed)
        qz_ref[:, c * NLIST : (c + 1) * NLIST] = jnp.concatenate([hi, hi, lo], axis=0)

    def arrived(which, ref, recvs, n):
        pltpu.make_async_remote_copy(
            src_ref=which, dst_ref=ref, send_sem=recvs.at[n], recv_sem=recvs.at[n], device_id=sibling,
            device_id_type=mesh_id,
        ).wait_recv()

    def unpack(b):
        band_ref[b] = spread_band(raw_ref[b].astype(F32), tail_ref[b].astype(F32)).astype(BF16)

    def expand(b):
        exp_ref[b] = mm(tail_coefs(tail_ref[b].astype(F32)).astype(BF16), tabs["rep"][...])

    raw_ref[0] = bands_ref[0, 0:32, :]
    unpack(0)
    expand(0)
    arrived(tail_ref.at[0], tail_ref.at[1], tail_recv, 4)
    expand(1)
    arrived(main, raw_ref.at[1], band_recv, 4)
    unpack(1)

    def relay(t, ref, sends, recvs):
        copy = remote(ref.at[2 + t], ref.at[4 + t], partner, sends, recvs, 2 + t)
        copy.start()
        return copy

    def step(t, carry):
        arrived(main, raw_ref.at[2 + t], band_recv, t)
        if isinstance(t, int):
            fields.append(relay(t, raw_ref, band_send, band_recv))
        unpack(2 + t)
        batch(t, band_ref, faug_ref, wst_ref, acc_ref, tabs)
        return carry

    sums = []
    for n in range(2):
        for t in (2 * n, 2 * n + 1):
            arrived(tail_ref.at[0], tail_ref.at[2 + t], tail_recv, t)
            if n == 0:
                tails.append(relay(t, tail_ref, tail_send, tail_recv))
            expand(2 + t)
        augment(n, glist_ref, qz_ref, exp_ref, choose_ref, phase_ref, yzt_ref, faug_ref)
        if n == 0:
            step(0, 0)
            step(1, 0)
            sums.append(slopes(n, glist_ref, qz_ref, exp_ref, choose_ref, phase_ref, yzt_ref, wst_ref))
        else:
            lax.fori_loop(2, 4, step, 0)
    give = remote(acc_ref.at[1], got_ref, sibling, sum_send, sum_recv, 0)
    give.start()
    sums.append(slopes(1, glist_ref, qz_ref, exp_ref, choose_ref, phase_ref, yzt_ref, wst_ref))
    rows = [coef_row(sums[0][i] + sums[1][i], tabs["rsum"][...]) for i in range(2)]
    pgive_ref[...] = jnp.broadcast_to(rows[1], (8, 256))
    coefs = remote(pgive_ref, pgot_ref, sibling, coef_send, coef_recv, 0)
    coefs.start()
    give.wait_recv()
    total = acc_ref[0] + got_ref[...]
    for c in range(8):
        chunk_ref[c] = pack_chunk(total, c)
    coefs.wait_recv()
    proj = rows[0] + pgot_ref[0:1, :]
    for c in range(8):
        chunk_ref[c, N : N + 1, 0:32] = proj[:, 32 * c : 32 * (c + 1)]
    chunks = []
    for n, to in enumerate(peers):
        chunks.append(remote(chunk_ref.at[to[1]], chunks_ref.at[n], to, chunk_send, chunk_recv, n))
        chunks[-1].start()
    whole = chunk_ref[col]
    for n, copy in enumerate(chunks):
        copy.wait_recv()
        whole = whole + chunks_ref[n]
    whole = whole * -0.5
    out_ref[:, 0, 0:128] = whole[:N]
    out_ref[0:16, 0, 128:CHUNK] = whole[40:56, 0:34]
    out_ref[16:32, 0, 128:CHUNK] = whole[40:56, 34:68]
    out_ref[32:36, 0, 128:CHUNK] = whole[40:44, 68:102]
    proj_ref[...] = whole[N : N + 1, 0:32]
    for copy in tails + fields + [give, coefs] + chunks:
        copy.wait_send()


def hand_over(grid_ref, proj_ref, grid_out, proj_out):
    grid_out[...] = grid_ref[...]
    proj_out[...] = proj_ref[...]


def on_device(bands, projections, qfunc, species, positions, glist):
    hbm = pl.BlockSpec(memory_space=pltpu.HBM)
    vm = pl.BlockSpec(memory_space=pltpu.VMEM)
    sources = [bands, projections, qfunc, species.reshape(1, ATOMS), positions, glist.reshape(1, NLIST)]
    sources += [jnp.asarray(TABLES[name]) for name in TABLE_NAMES]
    dma = pltpu.SemaphoreType.DMA
    grid, proj = pl.pallas_call(
        kernel,
        out_shape=(jax.ShapeDtypeStruct((N, 1, CHUNK), F32), jax.ShapeDtypeStruct((1, 32), F32)),
        in_specs=[hbm] * len(sources),
        out_specs=(vm, vm),
        scratch_shapes=[
            *[pltpu.VMEM(t.shape, t.dtype) for t in sources],
            pltpu.VMEM((2 + STEPS, XB, LANES), BF16),
            pltpu.VMEM((2 + STEPS, 32, 1296), BF16),
            pltpu.VMEM((2 + STEPS, 16, TAIL), BF16),
            pltpu.VMEM((3 * PK, 2 * NLIST), BF16),
            pltpu.VMEM((NG6 * LOWL, NLIST), BF16),
            pltpu.VMEM((2, ATOMS, NLIST), F32),
            pltpu.VMEM((ATOMS, LG), F32),
            pltpu.VMEM((2 + STEPS, ATOMS, 3 * LG), F32),
            pltpu.VMEM((STEPS, 2 * KL, NG6 * LOWL), F32),
            pltpu.VMEM((STEPS, 2 * KL, NG6 * LOWL), F32),
            pltpu.VMEM((2, XO, LANES), F32),
            pltpu.VMEM((XO, LANES), F32),
            pltpu.VMEM((8, 256), F32),
            pltpu.VMEM((8, 256), F32),
            pltpu.VMEM((8, 56, 128), F32),
            pltpu.VMEM((7, 56, 128), F32),
            dma((len(sources),)),
            *[dma((5,)) for unused in range(4)],
            *[dma((1,)) for unused in range(4)],
            *[dma((7,)) for unused in range(2)],
        ],
        compiler_params=pltpu.CompilerParams(
            collective_id=0, has_side_effects=True, vmem_limit_bytes=60 * 2**20
        ),
    )(*sources)
    grid, proj = pl.pallas_call(
        hand_over,
        out_shape=(jax.ShapeDtypeStruct((N, 1, CHUNK), F32), jax.ShapeDtypeStruct((1, 32), F32)),
        in_specs=[vm] * 2,
        out_specs=(vm, vm),
        compiler_params=pltpu.CompilerParams(vmem_limit_bytes=60 * 2**20),
    )(grid, proj)
    return (jnp.swapaxes(grid, 0, 1), proj)


def solution(mesh):
    return jax.shard_map(
        on_device,
        mesh=mesh,
        in_specs=(P("row", None, None), P("row", None), P(), P(), P(), P()),
        out_specs=(P("row", None, "col"), P("row", "col")),
        check_vma=False,
    )
```

```python
import functools
import math

import jax
import jax.numpy as jnp
import ml_dtypes
import numpy as np
from jax import lax
from jax.experimental import pallas as pl
from jax.experimental.pallas import tpu as pltpu
from jax.sharding import PartitionSpec as P

N = 36
NG6 = 6
LG = 256
LOWL = 128
LANES = NG6 * LG
XB = 48
XO = 40
KL = 24
KR = 40
ATOMS, NH, NSPEC, NLIST = 32, 8, 2, 1024
PK = 80
AUG = N**1.5 / (NH * math.sqrt(ATOMS))
STEPS = 4
TAIL = 384
CHUNK = 162
F32, BF16 = jnp.float32, jnp.bfloat16

ITEMS = [
    [(0, 0, -1, 0), (0, 1, 3, 1), (1, 0, 1, 1), (1, 1, -3, 0)],
    [(0, 0, -1, 1), (0, 1, 3, 0), (1, 0, 1, 0), (1, 1, -3, 1)],
    [(0, 0, 2, 0), (0, 1, -2, 1), (1, 0, -2, 0), (1, 1, 2, 1)],
    [(0, 0, 0, 1), (0, 1, 4, 0), (1, 0, 0, 0), (1, 1, 4, 1)],
]
GIVEN = [[[i for i in items if i[3] == k] for k in range(2)] for items in ITEMS]
TAKEN = [[[i for i in items if i[0] == k] for k in range(2)] for items in ITEMS]


def split_np(a):
    hi = a.astype(np.float32).astype(ml_dtypes.bfloat16)
    lo = (a - hi.astype(np.float64)).astype(np.float32).astype(ml_dtypes.bfloat16)
    return hi, lo


def row_of(pair, kx):
    return 11 * pair + kx if kx <= 10 else KL + 8 * pair + kx - 11


def make_tables():
    k = np.arange(19)[:, None]
    x = np.arange(N)[None, :]
    ang = 2 * np.pi * (k * x % N) / N
    weight = np.where((k == 0) | (k == N // 2), 1.0, 2.0) / N**3
    parts = (np.cos(ang), -np.sin(ang))
    bf = ml_dtypes.bfloat16
    fwd = np.zeros((4 * KR, 4 * XB), bf)
    inv = np.zeros((2 * XO, 6 * KR), bf)
    for pair in range(2):
        for c, part in enumerate(parts):
            fh, fl = split_np(part)
            ih, il = split_np(weight * part)
            for kx in range(19):
                r = c * KR + row_of(pair, kx)
                fwd[r, 96 * pair : 96 * pair + N] = fh[kx]
                fwd[r, 96 * pair + XB : 96 * pair + XB + N] = fh[kx]
                fwd[2 * KR + r, 96 * pair : 96 * pair + N] = fl[kx]
                for b, values in enumerate((ih, ih, il)):
                    inv[XO * pair : XO * pair + N, 2 * KR * b + r] = values[kx]
    r_of = np.repeat(np.arange(6), N)
    z_of = np.tile(np.arange(N), 6)
    near = [(s, kz) for s in (0, 1, 4, 5) for kz in (*range(11), *range(26, 36))]
    order = near + [(s, kz) for s in range(6) for kz in range(N) if (s, kz) not in near]
    s_of = np.array([p[0] for p in order])
    k_of = np.array([p[1] for p in order])
    ang = 2 * np.pi * ((6 * r_of[:, None] * s_of[None, :] + z_of[:, None] * k_of[None, :]) % N) / N
    c = np.zeros((LG, LG))
    s = np.zeros((LG, LG))
    c[:216, :216] = np.cos(ang)
    s[:216, :216] = np.sin(ang)

    def stacked(w):
        hi, lo = split_np(w)
        return np.concatenate([hi, hi, lo], axis=0)

    dft = np.stack([stacked(w) for w in (c, c - s, c + s, c.T, (c + s).T, (c - s).T)])
    tw = np.zeros((16, LG), np.float32)
    for q in range(6):
        a = 2 * np.pi * (r_of * q % N) / N
        tw[q, :216] = np.cos(a)
        tw[8 + q, :216] = -np.sin(a)
    signed = lambda v: np.where(v > N // 2, v - N, v)
    kern = np.zeros((NG6 * KR, LG), np.float32)
    for q in range(6):
        for pair in range(2):
            for kx in range(19):
                n2 = kx**2 + signed(q + 6 * s_of) ** 2 + signed(k_of) ** 2
                kern[q * KR + row_of(pair, kx), :216] = np.where(n2 > 0, N**1.5 / 4 / np.maximum(n2, 1), 0)
    packed = [(s, l, m) for s in range(NSPEC) for l in range(NH) for m in range(l, NH)]
    sel = np.zeros((PK, NSPEC * NH * NH), np.float32)
    rep = np.zeros((NH, 768), np.float32)
    rsum = np.zeros((256, 256), np.float32)
    weight = np.zeros((NSPEC, LG), np.float32)
    kk = np.arange(256) % NH
    k8 = np.arange(NH)
    fold = kk[:, None] == k8[None, :]
    for p, (s, l, m) in enumerate(packed):
        sel[p, s * 64 + l * 8 + m] += 0.5
        sel[p, s * 64 + m * 8 + l] += 0.5
        for b in range(3):
            rep[k8 == l, PK * b + p] = 1
            rep[k8 == m, LG + PK * b + p] = 1
            weight[s, PK * b + p] = 0.5 if l == m else 1.0
        rep[k8 == m, 2 * LG + p] = 1
        rsum[p, kk == l] = 1
        if l != m:
            rep[k8 == l, 2 * LG + PK + p] = 1
            rsum[PK + p, kk == m] = 1
    return dict(
        fwd=fwd, inv=inv, dft=dft, tw=tw, kern=kern, sel=sel.astype(bf), rep=rep.astype(bf), rsum=rsum.astype(bf), fold=fold.astype(bf),
        weight=np.concatenate([weight, np.zeros((6, LG), np.float32)]),
    )


TABLES = make_tables()
TABLE_NAMES = ("fwd", "inv", "dft", "tw", "kern", "sel", "rep", "rsum", "fold", "weight")


def split(a):
    hi = a.astype(BF16)
    return hi, (a - hi.astype(F32)).astype(BF16)


def mm(a, b):
    return jnp.dot(a, b, preferred_element_type=F32)


def mm_nt(a, b):
    return lax.dot_general(a, b, (((1,), (1,)), ((), ())), preferred_element_type=F32)


def dft3(a, b, c, sign):
    h = math.sqrt(3.0) / 2
    sr, si = b[0] + c[0], b[1] + c[1]
    dr, di = (b[0] - c[0]) * h, (b[1] - c[1]) * h
    tr, ti = a[0] - 0.5 * sr, a[1] - 0.5 * si
    zero = (a[0] + sr, a[1] + si)
    minus = (tr + di, ti - dr)
    plus = (tr - di, ti + dr)
    return (zero, minus, plus) if sign < 0 else (zero, plus, minus)


def dft6(v, sign):
    add = lambda p, q: (p[0] + q[0], p[1] + q[1])
    sub = lambda p, q: (p[0] - q[0], p[1] - q[1])
    e = dft3(add(v[0], v[3]), add(v[1], v[4]), add(v[2], v[5]), sign)
    o = dft3(sub(v[0], v[3]), sub(v[4], v[1]), sub(v[2], v[5]), sign)
    return [e[0], o[2], e[1], o[0], e[2], o[1]]


def mm3(x, w):
    hi, lo = split(x)
    return mm(jnp.concatenate([hi, lo, hi], axis=1), w)


def atom_of_lane():
    lane = lax.broadcasted_iota(jnp.int32, (ATOMS, 256), 1)
    return lane // NH == lax.broadcasted_iota(jnp.int32, (ATOMS, 256), 0)


def setup_lists(glist_ref, positions_ref, species_ref, weight_ref, yzt_ref, phase_ref, choose_ref):
    g = glist_ref[...]
    kx = g // (N * N)
    ky = g // N % N
    kz = g % N
    s = ky // 6
    where = (ky % 6) * LOWL + jnp.where(s < 2, s, s - 2) * 21 + jnp.where(kz <= 10, kz, kz - 15)
    step = 256
    for base in range(0, NG6 * LOWL, step):
        rows = lax.broadcasted_iota(jnp.int32, (step, NLIST), 0) + base
        yzt_ref[base : base + step, :] = jnp.where(rows == where, 1.0, 0.0).astype(BF16)
    sg = lambda v: jnp.where(v > N // 2, v - N, v).astype(F32)
    eye = lax.broadcasted_iota(jnp.int32, (ATOMS, ATOMS), 0) == lax.broadcasted_iota(jnp.int32, (ATOMS, ATOMS), 1)
    column = lambda row: jnp.sum(jnp.where(eye, row, 0.0), axis=1, keepdims=True)
    turns = (
        column(positions_ref[0:1, :]) * kx.astype(F32)
        + column(positions_ref[1:2, :]) * sg(ky)
        + column(positions_ref[2:3, :]) * sg(kz)
    )
    theta = (turns - jnp.floor(turns)) * (2.0 * math.pi)
    phase_ref[0] = jnp.cos(theta)
    phase_ref[1] = -jnp.sin(theta)
    spec = column(species_ref[...].astype(F32))
    choose = jnp.zeros((ATOMS, LG), F32)
    for s in range(NSPEC):
        choose = choose + jnp.where(spec == float(s), 1.0, 0.0) * weight_ref[s : s + 1, :]
    choose_ref[...] = choose


def kx_rows(glist_ref):
    kx = glist_ref[...] // (N * N)
    rows = lax.broadcasted_iota(jnp.int32, (KL, NLIST), 0)
    return rows == kx, rows == kx + 11


def augment(n, glist_ref, qz_ref, exp_ref, choose_ref, phase_ref, yzt_ref, faug_ref):
    lane = lax.broadcasted_iota(jnp.int32, (ATOMS, LG), 1)
    middle = jnp.logical_and(lane >= PK, lane < 2 * PK)
    mixed = []
    for t in range(2):
        for i in range(2):
            a, b = exp_ref[i], exp_ref[2 + 2 * n + t]
            full = (a[:, :LG] * b[:, LG : 2 * LG] + b[:, :LG] * a[:, LG : 2 * LG]) * choose_ref[...]
            hi = full.astype(BF16).astype(F32)
            mixed.append(jnp.where(middle, full - hi, hi).astype(BF16)[:, : 3 * PK])
    mixed = jnp.concatenate(mixed, axis=0)
    z_re = mm(mixed, qz_ref[:, :NLIST])
    z_im = mm(mixed, qz_ref[:, NLIST:])
    first, second = kx_rows(glist_ref)
    spread = []
    for t in range(2):
        re, im = [], []
        for i in range(2):
            at = (2 * t + i) * ATOMS
            zr, zi = z_re[at : at + ATOMS], z_im[at : at + ATOMS]
            re.append(jnp.sum(phase_ref[0] * zr - phase_ref[1] * zi, axis=0, keepdims=True) * AUG)
            im.append(jnp.sum(phase_ref[0] * zi + phase_ref[1] * zr, axis=0, keepdims=True) * AUG)
        for rows in (re, im):
            spread.append(jnp.where(first, rows[0], jnp.where(second, rows[1], 0.0)))
    hi, lo = split(jnp.concatenate(spread, axis=0))
    both = jnp.concatenate([hi, lo], axis=0)
    for base in range(0, NG6 * LOWL, LG):
        part = mm_nt(both, yzt_ref[base : base + LG, :])
        part = part[:96] + part[96:]
        for t in range(2):
            faug_ref[2 * n + t, :, base : base + LG] = part[48 * t : 48 * (t + 1)]


def batch(t, band_ref, faug_ref, wst_ref, acc_ref, tabs):
    other = band_ref[2 + t].astype(F32)
    halves = []
    for i in range(2):
        halves += split(band_ref[i].astype(F32) * other)
    out = mm(tabs["fwd"][...], jnp.concatenate(halves, axis=0))
    spec = out[: 2 * KR] + out[2 * KR :]
    v = [(spec[:KR, g * LG : (g + 1) * LG], spec[KR:, g * LG : (g + 1) * LG]) for g in range(NG6)]
    re_rows, im_rows = [], []
    for q, (re, im) in enumerate(dft6(v, -1)):
        if q:
            cr, ci = tabs["tw"][q : q + 1, :], tabs["tw"][8 + q : 9 + q, :]
            re, im = re * cr - im * ci, re * ci + im * cr
        re_rows.append(re)
        im_rows.append(im)
    re, im = jnp.concatenate(re_rows, axis=0), jnp.concatenate(im_rows, axis=0)
    both = mm3(re + im, tabs["dft"][0])
    f = (both - mm3(im, tabs["dft"][1]), both - mm3(re, tabs["dft"][2]))
    w = []
    for c in range(2):
        rows = []
        for q in range(NG6):
            block = f[c][q * KR : (q + 1) * KR]
            kern = tabs["kern"][q * KR : (q + 1) * KR, :]
            low = (block[:KL, :LOWL] + faug_ref[t, c * KL : (c + 1) * KL, q * LOWL : (q + 1) * LOWL]) * kern[:KL, :LOWL]
            wst_ref[t, c * KL : (c + 1) * KL, q * LOWL : (q + 1) * LOWL] = low
            rows.append(jnp.concatenate([low, block[:KL, LOWL:] * kern[:KL, LOWL:]], axis=1))
            rows.append(block[KL:] * kern[KL:])
        w.append(jnp.concatenate(rows, axis=0))
    both = mm3(w[0] + w[1], tabs["dft"][3])
    re, im = both - mm3(w[1], tabs["dft"][4]), both - mm3(w[0], tabs["dft"][5])
    v = []
    for q in range(NG6):
        a, b = re[q * KR : (q + 1) * KR], im[q * KR : (q + 1) * KR]
        if q:
            cr, ci = tabs["tw"][q : q + 1, :], tabs["tw"][8 + q : 9 + q, :]
            a, b = a * cr + b * ci, b * cr - a * ci
        v.append((a, b))
    v = dft6(v, 1)
    w = jnp.concatenate([jnp.concatenate([p[0], p[1]], axis=0) for p in v], axis=1)
    hi, lo = split(w)
    pot = mm(tabs["inv"][...], jnp.concatenate([hi, lo, hi], axis=0))
    acc_ref[0] += pot[:XO] * other[:XO]
    acc_ref[1] += pot[XO:] * other[:XO]


def slopes(n, glist_ref, qz_ref, exp_ref, choose_ref, phase_ref, yzt_ref, wst_ref):
    hi, lo = split(wst_ref[2 * n : 2 * n + 2].reshape(4 * KL, NG6 * LOWL))
    picked = mm(jnp.concatenate([hi, lo], axis=0), yzt_ref[...])
    picked = picked[:96] + picked[96:]
    first, second = kx_rows(glist_ref)
    cross = []
    for t in range(2):
        for mask in (first, second):
            at = t * 2 * KL
            wr = jnp.sum(jnp.where(mask, picked[at : at + KL], 0.0), axis=0, keepdims=True)
            wi = jnp.sum(jnp.where(mask, picked[at + KL : at + 2 * KL], 0.0), axis=0, keepdims=True)
            re = wr * phase_ref[0] + wi * phase_ref[1]
            im = wi * phase_ref[0] - wr * phase_ref[1]
            cross.append(jnp.concatenate([re, im], axis=1))
    hi, lo = split(jnp.concatenate(cross, axis=0))
    full = mm_nt(jnp.concatenate([hi, lo], axis=0), qz_ref[...])
    high, low = full[:128], full[128:]
    rest = high[:, 2 * PK :]
    slope = (high[:, : 2 * PK] + low[:, : 2 * PK] + jnp.concatenate([rest, rest], axis=1)) * (2.0 * AUG / N**3)
    slope = jnp.concatenate([slope, jnp.zeros((128, LG - 2 * PK), F32)], axis=1)
    chosen = jnp.where(choose_ref[...] > 0.0, 1.0, 0.0)
    sums = []
    for i in range(2):
        total = jnp.zeros((ATOMS, LG), F32)
        for t in range(2):
            at = (2 * t + i) * ATOMS
            total = total + slope[at : at + ATOMS] * exp_ref[2 + 2 * n + t][:, 2 * LG :]
        sums.append(total * chosen)
    return sums


def coef_row(packed, rsum):
    hi, lo = split(packed)
    full = mm(hi, rsum) + mm(lo, rsum)
    return jnp.sum(jnp.where(atom_of_lane(), full, 0.0), axis=0, keepdims=True)


def pack_tail(rows, coefs):
    rows = jnp.concatenate([rows[:, 324 * j : 324 * (j + 1)] for j in range(4)], axis=0)
    return jnp.concatenate([rows, coefs[:16], coefs[16:], jnp.zeros((16, TAIL - 340), F32)], axis=1)


def tail_coefs(tail):
    return jnp.concatenate([tail[:, 324:332], tail[:, 332:340]], axis=0)


def spread_band(main, tail):
    rows = jnp.concatenate([tail[4 * j : 4 * (j + 1), :324] for j in range(4)], axis=1)
    full = jnp.concatenate([main, rows, jnp.zeros((12, 1296), F32)], axis=0)
    zero = jnp.zeros((XB, LG - 216), F32)
    return jnp.concatenate([p for g in range(NG6) for p in (full[:, 216 * g : 216 * (g + 1)], zero)], axis=1)


def columns(total, c):
    start = CHUNK * c
    parts = []
    while start < CHUNK * (c + 1):
        g, at = divmod(start, 216)
        end = min(216 * (g + 1), CHUNK * (c + 1))
        parts.append(total[:, g * LG + at : g * LG + at + end - start])
        start = end
    return parts[0] if len(parts) == 1 else jnp.concatenate(parts, axis=1)


def pack_chunk(total, c):
    part = columns(total, c)
    main = part[:, :128]
    rest = part[:, 128:]
    last = jnp.concatenate([rest[32:40], jnp.zeros((8, 34), F32)], axis=0)
    rest = jnp.concatenate([rest[:16], rest[16:32], last, jnp.zeros((16, 26), F32)], axis=1)
    return jnp.concatenate([main, rest], axis=0)


def kernel(*refs):
    nt = len(TABLE_NAMES)
    sources = refs[: 6 + nt]
    out_ref, proj_ref = refs[6 + nt : 8 + nt]
    scratch = refs[8 + nt :]
    bands_ref, coef_ref, q_ref, species_ref, positions_ref, glist_ref = scratch[:6]
    tabs = dict(zip(TABLE_NAMES, scratch[6 : 6 + nt]))
    (band_ref, raw_ref, tail_ref, qz_ref, yzt_ref, phase_ref, choose_ref, exp_ref, faug_ref, wst_ref,
     acc_ref, got_ref, pgive_ref, pgot_ref, chunk_ref, chunks_ref,
     load_sem, tail_send, tail_recv, band_send, band_recv, sum_send, sum_recv, coef_send, coef_recv,
     chunk_send, chunk_recv) = scratch[6 + nt :]
    row, col = lax.axis_index("row"), lax.axis_index("col")
    zed, wide, core = row // 8, row // 2 % 4, row % 2

    far_side = col % 2

    def pick(table, m, e):
        return sum(
            jnp.where(jnp.logical_and(col // 2 == c, core == k), table[c][k][m][e], 0) for c in range(4) for k in range(2)
        )

    def at(dz, dy, k):
        return (((zed + dz + 16) % 8 * 4 + (wide + dy + 8) % 4) * 2 + k, col)

    sibling = at(0, 0, 1 - core)
    partner = (at(0, 2 * far_side - 1, core)[0], col + 1 - 2 * far_side)
    targets, origins = [], []
    for m in range(2):
        k = pick(GIVEN, m, 0)
        targets.append((at(-pick(GIVEN, m, 2), k + far_side - 1, k), pick(GIVEN, m, 1)))
        origins.append(at(pick(TAKEN, m, 2), 1 - core - far_side, pick(TAKEN, m, 3)))
    peers = [(row, (col + step) % 8) for step in range(1, 8)]
    mesh_id = pl.DeviceIdType.MESH

    barrier = pltpu.get_barrier_semaphore()

    def greet(partner):
        pl.semaphore_signal(barrier, inc=1, device_id=partner, device_id_type=mesh_id)

    others = origins + [sibling, partner] + peers
    for other in others:
        greet(other)

    names = ("bands", "projections", "qfunc", "species", "positions", "glist", *TABLE_NAMES)
    loads = [
        pltpu.make_async_copy(src, dst, load_sem.at[n]) for n, (src, dst) in enumerate(zip(sources, scratch[: 6 + nt]))
    ]
    for load in loads:
        load.start()

    def remote(src, dst, to, sems, recvs, n, m=None):
        return pltpu.make_async_remote_copy(
            src_ref=src, dst_ref=dst, send_sem=sems.at[n], recv_sem=recvs.at[n if m is None else m],
            device_id=to, device_id_type=mesh_id,
        )

    loads[0].wait()
    loads[1].wait()
    loads[names.index("fold")].wait()
    own = jnp.where(atom_of_lane(), coef_ref[...].astype(F32), 0.0).astype(BF16)
    tail_ref[0] = pack_tail(bands_ref[0].astype(F32)[32:36], mm(own, tabs["fold"][...])).astype(BF16)
    main = bands_ref.at[0, pl.ds(0, 32)]

    pl.semaphore_wait(barrier, len(others))
    tails = [remote(tail_ref.at[0], tail_ref.at[1], sibling, tail_send, tail_recv, 4)]
    fields = [remote(main, raw_ref.at[1], sibling, band_send, band_recv, 4)]
    for m, (to, t) in enumerate(targets):
        tails.append(remote(tail_ref.at[0], tail_ref.at[2 + t], to, tail_send, tail_recv, m, t))
        fields.append(remote(main, raw_ref.at[2 + t], to, band_send, band_recv, m, t))
    for copy in tails + fields:
        copy.start()

    late = ("fwd", "inv", "dft", "tw", "kern", "rsum")
    for n, load in enumerate(loads):
        if n > 1 and names[n] != "fold" and names[n] not in late:
            load.wait()
    setup_lists(glist_ref, positions_ref, species_ref, tabs["weight"], yzt_ref, phase_ref, choose_ref)
    acc_ref[...] = jnp.zeros_like(acc_ref)
    for c in range(2):
        hi, lo = split(q_ref[c].reshape(NSPEC * NH * NH, NLIST))
        packed = mm(tabs["sel"][...], hi) + mm(tabs["sel"][...], lo)
        hi, lo = split(packed)
        qz_ref[:, c * NLIST : (c + 1) * NLIST] = jnp.concatenate([hi, hi, lo], axis=0)

    def arrived(which, ref, recvs, n):
        pltpu.make_async_remote_copy(
            src_ref=which, dst_ref=ref, send_sem=recvs.at[n], recv_sem=recvs.at[n], device_id=sibling,
            device_id_type=mesh_id,
        ).wait_recv()

    def unpack(b):
        band_ref[b] = spread_band(raw_ref[b].astype(F32), tail_ref[b].astype(F32)).astype(BF16)

    def expand(b):
        exp_ref[b] = mm(tail_coefs(tail_ref[b].astype(F32)).astype(BF16), tabs["rep"][...])

    raw_ref[0] = bands_ref[0, 0:32, :]
    unpack(0)
    expand(0)
    arrived(tail_ref.at[0], tail_ref.at[1], tail_recv, 4)
    expand(1)
    arrived(main, raw_ref.at[1], band_recv, 4)
    unpack(1)

    def relay(t, ref, sends, recvs):
        copy = remote(ref.at[2 + t], ref.at[4 + t], partner, sends, recvs, 2 + t)
        copy.start()
        return copy

    def step(t, carry):
        arrived(main, raw_ref.at[2 + t], band_recv, t)
        if isinstance(t, int):
            fields.append(relay(t, raw_ref, band_send, band_recv))
        unpack(2 + t)
        batch(t, band_ref, faug_ref, wst_ref, acc_ref, tabs)
        return carry

    for name in late:
        loads[names.index(name)].wait()
    sums = []
    for n in range(2):
        for t in (2 * n, 2 * n + 1):
            arrived(tail_ref.at[0], tail_ref.at[2 + t], tail_recv, t)
            if n == 0:
                tails.append(relay(t, tail_ref, tail_send, tail_recv))
            expand(2 + t)
        augment(n, glist_ref, qz_ref, exp_ref, choose_ref, phase_ref, yzt_ref, faug_ref)
        if n == 0:
            step(0, 0)
            step(1, 0)
            sums.append(slopes(n, glist_ref, qz_ref, exp_ref, choose_ref, phase_ref, yzt_ref, wst_ref))
        else:
            lax.fori_loop(2, 4, step, 0)
    give = remote(acc_ref.at[1], got_ref, sibling, sum_send, sum_recv, 0)
    give.start()
    sums.append(slopes(1, glist_ref, qz_ref, exp_ref, choose_ref, phase_ref, yzt_ref, wst_ref))
    rows = [coef_row(sums[0][i] + sums[1][i], tabs["rsum"][...]) for i in range(2)]
    pgive_ref[...] = jnp.broadcast_to(rows[1], (8, 256))
    coefs = remote(pgive_ref, pgot_ref, sibling, coef_send, coef_recv, 0)
    coefs.start()
    give.wait_recv()
    total = acc_ref[0] + got_ref[...]
    for c in range(8):
        chunk_ref[c] = pack_chunk(total, c)
    coefs.wait_recv()
    proj = rows[0] + pgot_ref[0:1, :]
    for c in range(8):
        chunk_ref[c, N : N + 1, 0:32] = proj[:, 32 * c : 32 * (c + 1)]
    chunks = []
    for n, to in enumerate(peers):
        chunks.append(remote(chunk_ref.at[to[1]], chunks_ref.at[n], to, chunk_send, chunk_recv, n))
        chunks[-1].start()
    whole = chunk_ref[col]
    for n, copy in enumerate(chunks):
        copy.wait_recv()
        whole = whole + chunks_ref[n]
    whole = whole * -0.5
    out_ref[:, 0, 0:128] = whole[:N]
    out_ref[0:16, 0, 128:CHUNK] = whole[40:56, 0:34]
    out_ref[16:32, 0, 128:CHUNK] = whole[40:56, 34:68]
    out_ref[32:36, 0, 128:CHUNK] = whole[40:44, 68:102]
    proj_ref[...] = whole[N : N + 1, 0:32]
    for copy in tails + fields + [give, coefs] + chunks:
        copy.wait_send()


def hand_over(grid_ref, proj_ref, grid_out, proj_out):
    grid_out[...] = grid_ref[...]
    proj_out[...] = proj_ref[...]


def on_device(bands, projections, qfunc, species, positions, glist):
    hbm = pl.BlockSpec(memory_space=pltpu.HBM)
    vm = pl.BlockSpec(memory_space=pltpu.VMEM)
    sources = [bands, projections, qfunc, species.reshape(1, ATOMS), positions, glist.reshape(1, NLIST)]
    sources += [jnp.asarray(TABLES[name]) for name in TABLE_NAMES]
    dma = pltpu.SemaphoreType.DMA
    grid, proj = pl.pallas_call(
        kernel,
        out_shape=(jax.ShapeDtypeStruct((N, 1, CHUNK), F32), jax.ShapeDtypeStruct((1, 32), F32)),
        in_specs=[hbm] * len(sources),
        out_specs=(vm, vm),
        scratch_shapes=[
            *[pltpu.VMEM(t.shape, t.dtype) for t in sources],
            pltpu.VMEM((2 + STEPS, XB, LANES), BF16),
            pltpu.VMEM((2 + STEPS, 32, 1296), BF16),
            pltpu.VMEM((2 + STEPS, 16, TAIL), BF16),
            pltpu.VMEM((3 * PK, 2 * NLIST), BF16),
            pltpu.VMEM((NG6 * LOWL, NLIST), BF16),
            pltpu.VMEM((2, ATOMS, NLIST), F32),
            pltpu.VMEM((ATOMS, LG), F32),
            pltpu.VMEM((2 + STEPS, ATOMS, 3 * LG), F32),
            pltpu.VMEM((STEPS, 2 * KL, NG6 * LOWL), F32),
            pltpu.VMEM((STEPS, 2 * KL, NG6 * LOWL), F32),
            pltpu.VMEM((2, XO, LANES), F32),
            pltpu.VMEM((XO, LANES), F32),
            pltpu.VMEM((8, 256), F32),
            pltpu.VMEM((8, 256), F32),
            pltpu.VMEM((8, 56, 128), F32),
            pltpu.VMEM((7, 56, 128), F32),
            dma((len(sources),)),
            *[dma((5,)) for unused in range(4)],
            *[dma((1,)) for unused in range(4)],
            *[dma((7,)) for unused in range(2)],
        ],
        compiler_params=pltpu.CompilerParams(
            collective_id=0, has_side_effects=True, vmem_limit_bytes=60 * 2**20
        ),
    )(*sources)
    grid, proj = pl.pallas_call(
        hand_over,
        out_shape=(jax.ShapeDtypeStruct((N, 1, CHUNK), F32), jax.ShapeDtypeStruct((1, 32), F32)),
        in_specs=[vm] * 2,
        out_specs=(vm, vm),
        compiler_params=pltpu.CompilerParams(vmem_limit_bytes=60 * 2**20),
    )(grid, proj)
    return (jnp.swapaxes(grid, 0, 1), proj)


def solution(mesh):
    return jax.shard_map(
        on_device,
        mesh=mesh,
        in_specs=(P("row", None, None), P("row", None), P(), P(), P(), P()),
        out_specs=(P("row", None, "col"), P("row", "col")),
        check_vma=False,
    )
```
